32 devices in a mesh: groups: 2 (over x), seq: 16 (over z, y, core).
Axes of the slice: x: 2, y: 2, z: 4, core: 2. Of those that a mesh axis runs over, the one named last changes fastest.
Arguments:
- cache_keys: bfloat16 [131072, 1024], P(('groups', 'seq')), parts along dimension 0, may hold values from -48 to 48
- cache_values: bfloat16 [131072, 1024], P(('groups', 'seq')), parts along dimension 0, may hold values from -6 to 6
- sketch_matrix: float32 [1024, 160], replicated, may hold values from -6 to 6
- queries: bfloat16 [6, 8192], P('groups'), parts along dimension 0, may hold values from -2000 to 2000
- fresh_keys: bfloat16 [6, 1024], P('groups'), parts along dimension 0, may hold values from -20 to 20
- fresh_values: bfloat16 [6, 1024], P('groups'), parts along dimension 0, may hold values from -6 to 6
- chosen: int32 [6, 8, 256], P('groups'), parts along dimension 0, may hold values from 0 to 8191, as said below
- shard_counts: int32 [6, 8, 16], P('groups'), parts along dimension 0, may hold values from 0 to 48, as said below
- outliers: int32 [64], P('groups'), parts along dimension 0, may hold values from 0 to 8191, as said below
Outputs:
- attended: bfloat16 [6, 8192], P('groups', 'seq'), parts along dimension 0
- key_factor: float32 [131072, 160], P(('groups', 'seq')), parts along dimension 0
The draws below stay inside these ranges and needn't reach their ends.
There are 2 independent parts, one for each index of `groups`. The reference program is written for one: setup_inputs(seed, part) draws one part's arguments, and reference() takes and returns one part's arrays. A program takes and returns all parts, laid end to end along the dimension named above; an argument that names none is the same for every part. Nothing has to cross between parts.
Inputs may be any that keep to these rules, and one draw needn't show every extreme that they name: Each list chosen[t, g] holds distinct span numbers in ascending order, none of them an outlier span; shard s holds spans s * 512 to (s+1) * 512 - 1. shard_counts[t, g, s] is the number of entries of chosen[t, g] on shard s; they sum to 256; the most is 48, reached in every list. `outliers`: distinct span numbers in ascending order; at most 4 on one shard, reached on some shard.
All inputs are finite; a program needn't handle non-finite values.
Results may differ from the reference program's by a relative error of at most 0.0228.
Values may be sent and summed in bfloat16 or wider, within the bound.
No kernel may reach another device: no remote copies, remote signals or barrier semaphores. Data moves between devices by JAX's collectives and lax.ppermute only.
A program may use at most 128 MiB of HBM per device.

```python
import jax
import jax.numpy as jnp
from jax import lax

KVH = 8
HD = 128
QH = 64
RANK = 160
SPAN = 8
STEPS = 3
SEL = 256
OUTL = 32
OMOST = 4
LEN_DEV = 4096
D_KV = 1024
GROUP = 8
LENGTH = 65536
CH_DEV = 512
TOTAL_CH = 8192
MOST = 48
N_SEQ = 16


def capped_deal(deal_key, total_items, cap_items, weights_row):
    hot_key, loop_key = jax.random.split(deal_key)
    hottest = jax.random.randint(hot_key, (), 0, N_SEQ)
    tally = jnp.zeros((N_SEQ,), jnp.int32).at[hottest].set(cap_items)

    def place_one(item_turn, tally_now):
        open_weight = jnp.where(tally_now >= cap_items, 0, weights_row)
        running = jnp.cumsum(open_weight)
        ticket = jax.random.randint(jax.random.fold_in(loop_key, item_turn), (), 0, running[-1])
        target_shard = jnp.sum((running <= ticket).astype(jnp.int32))
        return tally_now.at[target_shard].add(1)
    return lax.fori_loop(0, total_items - cap_items, place_one, tally)


def shard_ranks(rank_key, pushed):
    span_ids = jnp.arange(TOTAL_CH, dtype=jnp.int32)
    shard_of = span_ids // CH_DEV
    shuffled = jax.random.permutation(rank_key, TOTAL_CH).astype(jnp.int32)
    order_pos = jnp.zeros((TOTAL_CH,), jnp.int32).at[shuffled].set(span_ids)
    sort_key = shard_of * (2 * TOTAL_CH) + pushed * TOTAL_CH + order_pos
    ordering = jnp.argsort(sort_key)
    placed = jnp.zeros((TOTAL_CH,), jnp.int32).at[ordering].set(span_ids)
    return placed - shard_of * CH_DEV


def selection_tables(key):
    base_key = jax.random.fold_in(key, 7177)
    out_key, sel_key = jax.random.split(base_key)
    out_deal, out_rank = jax.random.split(out_key)
    outlier_counts = capped_deal(out_deal, OUTL, OMOST, jnp.ones((N_SEQ,), jnp.int32))
    span_ids = jnp.arange(TOTAL_CH, dtype=jnp.int32)
    shard_of = span_ids // CH_DEV
    outlier_rank = shard_ranks(out_rank, jnp.zeros((TOTAL_CH,), jnp.int32))
    is_outlier = outlier_rank < outlier_counts[shard_of]
    outlier_list = jnp.sort(jnp.where(is_outlier, span_ids, TOTAL_CH + span_ids))[:OUTL]

    def one_list(list_key):
        weight_key, deal_key, order_key = jax.random.split(list_key, 3)
        raw_weight = jax.random.randint(weight_key, (N_SEQ,), 1, 9)
        tally = capped_deal(deal_key, SEL, MOST, raw_weight * raw_weight)
        ranks = shard_ranks(order_key, is_outlier.astype(jnp.int32))
        taken = (ranks < tally[shard_of]) & jnp.logical_not(is_outlier)
        return (jnp.sort(jnp.where(taken, span_ids, TOTAL_CH + span_ids))[:SEL], tally)
    lists, tallies = jax.vmap(one_list)(jax.random.split(sel_key, STEPS * KVH))
    return (lists.reshape(STEPS, KVH, SEL), tallies.reshape(STEPS, KVH, N_SEQ), outlier_list)


def query_tables(key):
    base_key = jax.random.fold_in(key, 3131)
    key_query, key_fresh = jax.random.split(base_key, 2)
    query_rows = jnp.clip(jax.random.normal(key_query, (STEPS, QH, HD), jnp.float32), -5.0, 5.0)
    fresh_rows = jnp.clip(jax.random.normal(key_fresh, (STEPS, KVH, HD), jnp.float32), -5.0, 5.0)
    group_sum = jnp.sum(query_rows.reshape(STEPS, KVH, QH // KVH, HD), axis=2) / jnp.sqrt(jnp.float32(QH // KVH))
    strength = 5.0 * jnp.sqrt(jnp.float32(QH // KVH) / jnp.float32(HD))
    fresh_rows = jnp.clip(strength * group_sum + 0.3 * fresh_rows, -20.0, 20.0)
    return (query_rows.reshape(STEPS, QH * HD), fresh_rows.reshape(STEPS, KVH * HD))


def draw_cache_keys(key, part):
    raw_keys = jnp.clip(jax.random.normal(jax.random.fold_in(key, 5151), (LENGTH, D_KV), jnp.float32), -6.0, 6.0)
    levels = jnp.exp(jax.random.uniform(jax.random.fold_in(key, 5252), (D_KV,), jnp.float32, minval=jnp.log(0.5), maxval=jnp.log(2.0)))
    shard_of = jnp.arange(LENGTH, dtype=jnp.int32) // LEN_DEV
    block_of = jnp.arange(D_KV, dtype=jnp.int32) // (D_KV // N_SEQ)
    offset = (block_of[None, :] - shard_of[:, None]) % N_SEQ
    paired = (offset == 0) | (offset == 1) | (offset == N_SEQ // 2) | (offset == N_SEQ // 2 + 1)
    return (raw_keys * jnp.where(paired, 4.0, 1.0) * levels[None, :]).astype(jnp.bfloat16)


def draw_chosen(key, part):
    return selection_tables(key)[0]


def draw_shard_counts(key, part):
    return selection_tables(key)[1]


def draw_outliers(key, part):
    return selection_tables(key)[2]


def draw_queries(key, part):
    return query_tables(key)[0].astype(jnp.bfloat16)


def draw_fresh_keys(key, part):
    return query_tables(key)[1].astype(jnp.bfloat16)


def steps_of(rng, dims, cuts, least, largest):
    factor_of, own = 1.0, jax.random.fold_in(rng, 6)
    for dim, parts in cuts:
        draws = jnp.exp(jax.random.uniform(jax.random.fold_in(own, dim), (parts,), jnp.float32, least / len(cuts), largest / len(cuts)))
        factor_of = factor_of * jnp.repeat(draws, dims[dim] // parts).reshape([-1 if axis == dim else 1 for axis in range(len(dims))])
    return factor_of


def noise(stream_key, dims, scale, bound, shards=(), kind=jnp.bfloat16):
    result = jax.random.normal(stream_key, dims, jnp.float32) * scale
    if len(shards) > 0:
        result = steps_of(stream_key, dims, shards, -0.22, 0.18) * result
    return jnp.clip(result, min=-bound, max=bound).astype(kind)


def setup_inputs(seed: int = 0, part: int = 0) -> dict:
    streams_of = jax.random.split(jax.random.key(seed), 10)
    own_keys = jax.random.split(jax.random.fold_in(streams_of[9], part), 10)
    cache_keys = draw_cache_keys(jax.random.fold_in(jax.random.fold_in(streams_of[9], part), 71), part)
    cache_values = noise(own_keys[1], (LENGTH, D_KV), 1.0, 6.0, ((0, 16),))
    sketch_matrix = noise(streams_of[2], (D_KV, RANK), 1.0, 6.0, (), jnp.float32)
    queries = draw_queries(jax.random.fold_in(jax.random.fold_in(streams_of[9], part), 71), part)
    fresh_keys = draw_fresh_keys(jax.random.fold_in(jax.random.fold_in(streams_of[9], part), 71), part)
    fresh_values = noise(own_keys[5], (STEPS, D_KV), 1.0, 6.0)
    chosen = draw_chosen(jax.random.fold_in(jax.random.fold_in(streams_of[9], part), 71), part)
    shard_counts = draw_shard_counts(jax.random.fold_in(jax.random.fold_in(streams_of[9], part), 71), part)
    outliers = draw_outliers(jax.random.fold_in(jax.random.fold_in(streams_of[9], part), 71), part)
    return {"cache_keys": cache_keys, "cache_values": cache_values, "sketch_matrix": sketch_matrix, "queries": queries, "fresh_keys": fresh_keys, "fresh_values": fresh_values, "chosen": chosen, "shard_counts": shard_counts, "outliers": outliers}


def rotate(vectors, positions):
    half_width = vectors.shape[-1] // 2
    exponents = jnp.arange(half_width, dtype=jnp.float32) * (2.0 / vectors.shape[-1])
    inverse_freq = jnp.exp(-jnp.log(jnp.float32(500000.0)) * exponents)
    angles = positions.astype(jnp.float32)[..., None] * inverse_freq
    cosine = jnp.cos(angles)
    sine = jnp.sin(angles)
    first_half = vectors[..., :half_width]
    second_half = vectors[..., half_width:]
    return jnp.concatenate([first_half * cosine - second_half * sine, second_half * cosine + first_half * sine], axis=-1)

def make_basis(sketch):
    small_gram = jnp.dot(sketch.T, sketch, precision=lax.Precision.HIGHEST)
    lower = jnp.linalg.cholesky(small_gram)
    solved = lax.linalg.triangular_solve(lower, sketch.T, left_side=True, lower=True)
    return solved.T.astype(jnp.bfloat16)

def reference(cache_keys, cache_values, sketch_matrix, queries, fresh_keys, fresh_values, chosen, shard_counts, outliers):
    contract = (((0,), (0,)), ((), ()))
    gram_total = lax.dot_general(cache_keys.astype(jnp.float32), cache_keys.astype(jnp.float32), contract, preferred_element_type=jnp.float32) / LENGTH
    sketch = jnp.dot(gram_total, sketch_matrix, precision=lax.Precision.HIGHEST)
    key_basis = make_basis(sketch)
    key_factor = jnp.dot(cache_keys.astype(jnp.float32), key_basis.astype(jnp.float32), preferred_element_type=jnp.float32)
    preceding = jnp.cumsum(shard_counts, axis=2) - shard_counts
    padded_list = jnp.concatenate([chosen, jnp.zeros((STEPS, KVH, MOST), jnp.int32)], axis=2)
    slot_ids = jnp.arange(MOST, dtype=jnp.int32)
    place = (preceding[..., None] + slot_ids).reshape(STEPS, KVH, N_SEQ * MOST)
    picked = jnp.take_along_axis(padded_list, place, axis=2).reshape(STEPS, KVH, N_SEQ, MOST)
    is_live = slot_ids < shard_counts[..., None]
    shard_base = (jnp.arange(N_SEQ, dtype=jnp.int32) * CH_DEV)[:, None]
    span_ids = jnp.clip(picked - shard_base, 0, CH_DEV - 1) + shard_base
    span_ids = span_ids.reshape(STEPS, KVH, N_SEQ * MOST)
    is_live = is_live.reshape(STEPS, KVH, N_SEQ * MOST)
    factor_spans = key_factor.reshape(TOTAL_CH, SPAN, RANK)[span_ids]
    basis_heads = key_basis.reshape(KVH, HD, RANK)
    rebuilt = jnp.einsum('tgmcr,gdr->tgmcd', factor_spans.astype(jnp.float32), basis_heads.astype(jnp.float32), precision=lax.Precision.HIGHEST)
    token_pos = span_ids[..., None] * SPAN + jnp.arange(SPAN, dtype=jnp.int32)
    sel_keys = rotate(rebuilt, token_pos).astype(jnp.bfloat16)
    value_blocks = cache_values.reshape(TOTAL_CH, SPAN, KVH, HD)
    head_ids = jnp.arange(KVH, dtype=jnp.int32)
    sel_values = value_blocks[span_ids, :, head_ids[None, :, None], :]
    key_blocks = cache_keys.reshape(TOTAL_CH, SPAN, KVH, HD)
    out_keys = key_blocks[outliers[None, :], :, head_ids[:, None], :]
    out_pos = outliers[:, None] * SPAN + jnp.arange(SPAN, dtype=jnp.int32)
    out_keys = rotate(out_keys.astype(jnp.float32), out_pos).astype(jnp.bfloat16)
    out_values = value_blocks[outliers[None, :], :, head_ids[:, None], :]
    all_keys = jnp.concatenate([sel_keys.reshape(STEPS, KVH, -1, HD), jnp.broadcast_to(out_keys.reshape(1, KVH, -1, HD), (STEPS, KVH, OUTL * SPAN, HD))], axis=2)
    all_values = jnp.concatenate([sel_values.reshape(STEPS, KVH, -1, HD), jnp.broadcast_to(out_values.reshape(1, KVH, -1, HD), (STEPS, KVH, OUTL * SPAN, HD))], axis=2)
    live_tokens = jnp.concatenate([jnp.repeat(is_live, SPAN, axis=2), jnp.ones((STEPS, KVH, OUTL * SPAN), bool)], axis=2)
    step_pos = LENGTH + jnp.arange(STEPS, dtype=jnp.int32)
    query_rows = rotate(queries.reshape(STEPS, QH, HD).astype(jnp.float32), step_pos[:, None]).reshape(STEPS, KVH, GROUP, HD)
    new_keys = rotate(fresh_keys.reshape(STEPS, KVH, HD).astype(jnp.float32), step_pos[:, None]).astype(jnp.bfloat16)
    new_values = fresh_values.reshape(STEPS, KVH, HD)
    score_scale = 1.0 / jnp.sqrt(jnp.float32(HD))
    cache_scores = jnp.einsum('tgqd,tgld->tgql', query_rows, all_keys.astype(jnp.float32), precision=lax.Precision.HIGHEST) * score_scale
    cache_scores = jnp.where(live_tokens[:, :, None, :], cache_scores, -1e+30)
    new_scores = jnp.einsum('tgqd,sgd->tgqs', query_rows, new_keys.astype(jnp.float32), precision=lax.Precision.HIGHEST) * score_scale
    causal = jnp.arange(STEPS)[None, :] <= jnp.arange(STEPS)[:, None]
    new_scores = jnp.where(causal[:, None, None, :], new_scores, -1e+30)
    row_max = jnp.maximum(lax.optimization_barrier(jnp.max(cache_scores, axis=-1)), lax.optimization_barrier(jnp.max(new_scores, axis=-1)))
    cache_weights = jnp.exp(cache_scores - row_max[..., None]) * live_tokens[:, :, None, :]
    new_weights = jnp.exp(new_scores - row_max[..., None]) * causal[:, None, None, :]
    totals = lax.optimization_barrier(jnp.sum(cache_weights, axis=-1)) + lax.optimization_barrier(jnp.sum(new_weights, axis=-1))
    summed = jnp.einsum('tgql,tgld->tgqd', cache_weights, all_values.astype(jnp.float32), precision=lax.Precision.HIGHEST)
    summed = summed + jnp.einsum('tgqs,sgd->tgqd', new_weights, new_values.astype(jnp.float32), precision=lax.Precision.HIGHEST)
    attended = (summed / totals[..., None]).reshape(STEPS, QH * HD).astype(jnp.bfloat16)
    return (attended, key_factor)
```

```python
import functools

import jax
import jax.numpy as jnp
from jax import lax
from jax.experimental import pallas as pl
from jax.experimental.pallas import tpu as pltpu
from jax.sharding import PartitionSpec as P

KVH = 8
HD = 128
QH = 64
SPAN = 8
OMOST = 4
BF = jnp.bfloat16
F32 = jnp.float32
DEAD = -1e30
LANES = 128
NT = (((1,), (1,)), ((), ()))
TN = (((0,), (0,)), ((), ()))


def vmem():
    return pl.BlockSpec(memory_space=pltpu.VMEM)


def smem():
    return pl.BlockSpec(memory_space=pltpu.SMEM)


def hbm():
    return pl.BlockSpec(memory_space=pl.ANY)


def round_up(x, m):
    return (x + m - 1) // m * m


def split2(x):
    high = x.astype(BF)
    return high, (x - high.astype(F32)).astype(BF)


def split3(x):
    high = x.astype(BF).astype(F32)
    rest = x - high
    middle = rest.astype(BF).astype(F32)
    return high, middle, rest - middle


def sketch_kernel(me_ref, st_ref, keys_hbm, keep_ref, send_ref, keys_ref, acc_ref, sem, *, scale, chunk):
    seq_len = keys_ref.shape[0]
    rank = st_ref.shape[0]
    half = rank // 2
    n = seq_len // chunk
    copies = [
        pltpu.make_async_copy(
            keys_hbm.at[pl.ds(i * chunk, chunk)], keys_ref.at[pl.ds(i * chunk, chunk)], sem.at[i]
        )
        for i in range(n)
    ]
    for c in copies:
        c.start()
    st = st_ref[...].astype(BF)

    def rows(i):
        return keys_ref[i * chunk:(i + 1) * chunk, :]

    def first(i):
        return lax.dot_general(st, rows(i), NT, preferred_element_type=F32).astype(BF)

    def second(i, y):
        return jnp.dot(y, rows(i), preferred_element_type=F32)

    copies[0].wait()
    y = first(0)
    for i in range(1, n):
        copies[i].wait()
        y_next = first(i)
        z = second(i - 1, y)
        if i == 1:
            acc_ref[...] = z
        else:
            acc_ref[...] += z
        y = y_next
    acc_ref[...] = (acc_ref[...] + second(n - 1, y)) * scale
    core = me_ref[0] % 2
    keep_ref[...] = acc_ref[pl.ds(pl.multiple_of(core * half, 8), half), :]
    send_ref[...] = acc_ref[pl.ds(pl.multiple_of((1 - core) * half, 8), half), :]


def sketch_share(me, sketch_t, cache_keys, length):
    seq_len, width = cache_keys.shape
    rank = sketch_t.shape[0]
    chunk = min(512, seq_len)
    half = jax.ShapeDtypeStruct((rank // 2, width), F32)
    return pl.pallas_call(
        functools.partial(sketch_kernel, scale=1.0 / length, chunk=chunk),
        in_specs=[smem(), vmem(), hbm()],
        out_specs=[vmem(), vmem()],
        out_shape=[half, half],
        scratch_shapes=[
            pltpu.VMEM((seq_len, width), BF),
            pltpu.VMEM((rank, width), F32),
            pltpu.SemaphoreType.DMA((seq_len // chunk,)),
        ],
        compiler_params=pltpu.CompilerParams(vmem_limit_bytes=40 << 20),
        name="sketch_share",
    )(me, sketch_t, cache_keys)


def prepare_kernel(
    me_ref, chosen_ref, counts_ref, outl_ref, q_ref, fk_ref, fv_ref, ca_ref, sa_ref, cb_ref, sb_ref, cq_ref, sq_ref,
    keys_hbm, values_hbm,
    slots_ref, live_ref, cc_ref, ss_ref, vg_ref, kx_ref, qs_ref,
    values_ref, okeys_ref, vtmp_ref, xtmp_ref, qtmp_ref, sem, osem, *, most, per_device, tok_sel, tok_main
):
    steps = q_ref.shape[0]
    seq_len = values_ref.shape[0]
    spans = seq_len // SPAN
    me = me_ref[0]
    base = me * spans
    n_chunks = sem.shape[0]
    chunk = seq_len // n_chunks
    copies = [
        pltpu.make_async_copy(
            values_hbm.at[pl.ds(i * chunk, chunk)], values_ref.at[pl.ds(i * chunk, chunk)], sem.at[i]
        )
        for i in range(n_chunks)
    ]
    for c in copies:
        c.start()

    n_out = outl_ref.shape[0]

    def below(i, carry):
        first, here = carry
        s = outl_ref[i]
        return (first + (s < base).astype(jnp.int32), here + ((s >= base) & (s < base + spans)).astype(jnp.int32))

    o_first, o_here = lax.fori_loop(0, n_out, below, (jnp.int32(0), jnp.int32(0)), unroll=8)
    o_span = [
        jnp.clip(outl_ref[jnp.minimum(o_first + j, n_out - 1)] - base, 0, spans - 1) for j in range(OMOST)
    ]
    o_copies = [
        pltpu.make_async_copy(
            keys_hbm.at[pl.ds(pl.multiple_of(o_span[j] // 2 * 16, 16), 16)], okeys_ref.at[j], osem.at[j]
        )
        for j in range(OMOST)
    ]
    for c in o_copies:
        c.start()

    blk = cb_ref.shape[0]
    for a in range(seq_len // blk):
        ca = ca_ref[a:a + 1, :]
        sa = sa_ref[a:a + 1, :]
        cb = cb_ref[...]
        sb = sb_ref[...]
        cc_ref[a * blk:(a + 1) * blk, :] = ca * cb - sa * sb
        ss_ref[a * blk:(a + 1) * blk, :] = sa * cb + ca * sb

    lane = lax.broadcasted_iota(jnp.int32, (8, LANES), 1)
    sign = jnp.where(lane < HD // 2, -1.0, 1.0)

    def turn(x, c, s):
        return x * c + pltpu.roll(x, HD // 2, 1) * (s * sign[:x.shape[0]])

    group = QH // KVH
    n_dest = qs_ref.shape[0]
    rp = qs_ref.shape[1] // 2
    scale = 1.0 / (HD ** 0.5)
    qtmp_ref[...] = jnp.zeros_like(qtmp_ref)
    for t in range(steps):
        c = cq_ref[t:t + 1, :]
        s = sq_ref[t:t + 1, :]
        for h in range(QH):
            x = q_ref[t:t + 1, h * HD:(h + 1) * HD].astype(F32)
            d, i = h // per_device, h % per_device
            r = t * per_device + i
            qtmp_ref[d, r:r + 1, :] = x
        for d in range(n_dest):
            r = t * per_device
            x = qtmp_ref[d, r:r + per_device, :]
            qtmp_ref[d, r:r + per_device, :] = (
                x * c + pltpu.roll(x, HD // 2, 1) * (s * sign[:1])
            ) * scale
    lane_r = lax.broadcasted_iota(jnp.int32, (rp, LANES), 1)
    for d in range(n_dest):
        x = qtmp_ref[d]
        z = jnp.where(lane_r < HD // 2, 1.0, -1.0) * pltpu.roll(x, HD // 2, 1)
        hi, lo = split2(jnp.concatenate([x, z], 1))
        qs_ref[d] = jnp.concatenate([hi, lo], 0)

    for c in o_copies:
        c.wait()
    x_rows = kx_ref.shape[1]
    for g in range(KVH):
        sl = slice(g * HD, (g + 1) * HD)
        xtmp_ref[...] = jnp.zeros_like(xtmp_ref)
        for j in range(OMOST):
            wide = okeys_ref[j, :, sl].astype(F32)
            x = jnp.where(o_span[j] % 2 == 0, wide[:8], wide[8:])
            rows = pl.ds(pl.multiple_of(o_span[j] * SPAN, SPAN), SPAN)
            xtmp_ref[j * SPAN:(j + 1) * SPAN, :] = turn(x, cc_ref[rows, :], ss_ref[rows, :])
        x = fk_ref[:, sl].astype(F32)
        o = OMOST * SPAN
        xtmp_ref[o:o + steps, :] = x * cq_ref[:steps, :] + pltpu.roll(x, HD // 2, 1) * (sq_ref[:steps, :] * sign[:1])
        kx_ref[g, :, :HD] = xtmp_ref[...].astype(BF)
        kx_ref[g, :, HD:] = jnp.zeros((x_rows, HD), BF)

    for c in copies:
        c.wait()
    vtmp_ref[...] = jnp.zeros_like(vtmp_ref)
    live_ref[steps * KVH] = o_here
    live_ref[steps * KVH + 1] = me
    sel = chosen_ref.shape[1]
    part = 16 if most % 16 == 0 else 8

    def value_rows(span, lanes):
        wide = values_ref[pl.ds(pl.multiple_of(span // 2 * 16, 16), 16), lanes].astype(F32)
        return jnp.where(span % 2 == 0, wide[:8], wide[8:])

    for g in range(KVH):
        lanes = slice(g * HD, (g + 1) * HD)
        for j in range(OMOST):
            o = tok_main + j * SPAN
            vtmp_ref[o:o + SPAN, :] = value_rows(o_span[j], lanes)
        o = tok_main + OMOST * SPAN
        vtmp_ref[o:o + steps, :] = fv_ref[:, lanes].astype(F32)

        def one_list(t, _, g=g, lanes=lanes):
            i = t * KVH + g
            start = lax.fori_loop(0, me, lambda r, s: s + counts_ref[i, r], jnp.int32(0))
            count = counts_ref[i, me]
            live_ref[i] = count
            for k in range(most // part):
                @pl.when(k * part < count)
                def _():
                    for j in range(k * part, (k + 1) * part):
                        picked = chosen_ref[i, jnp.minimum(start + j, sel - 1)]
                        span = jnp.clip(picked - base, 0, spans - 1)
                        slots_ref[i, j] = span
                        o = j * SPAN if j * SPAN < tok_main else j * SPAN + LANES
                        vtmp_ref[o:o + SPAN, :] = value_rows(span, lanes)
            vg_ref[i] = vtmp_ref[...].astype(BF)
            return 0

        lax.fori_loop(0, steps, one_list, 0)


def attend_kernel(
    core_ref, slots_ref, live_ref, zmine_ref, zother_ref, kx_ref, qs_ref,
    keys_hbm, cc_hbm, ss_hbm, vg_hbm,
    kft_hbm, out_ref,
    keys_ref, cc_ref, ss_ref, vg_ref, z_ref, a_ref, qt_ref, kf_ref, kft_ref, kg_ref, cg_ref, sg_ref, sc_ref,
    sem, out_sem, *, most, per_device, steps, tok_main
):
    rank, width = z_ref.shape
    half = rank // 2
    seq_len = keys_ref.shape[0]
    loads = [
        pltpu.make_async_copy(keys_hbm, keys_ref, sem.at[0]),
        pltpu.make_async_copy(cc_hbm, cc_ref, sem.at[1]),
        pltpu.make_async_copy(ss_hbm, ss_ref, sem.at[2]),
        pltpu.make_async_copy(vg_hbm, vg_ref, sem.at[3]),
    ]
    for c in loads:
        c.start()

    core = core_ref[0] % 2
    z_ref[pl.ds(pl.multiple_of(core * half, 16), half), :] = zmine_ref[...]
    z_ref[pl.ds(pl.multiple_of((1 - core) * half, 16), half), :] = zother_ref[...]
    basis(z_ref, a_ref, qt_ref)
    qt = qt_ref[...]

    loads[0].wait()
    chunk = 512 if seq_len % 512 == 0 else seq_len
    stores = []
    for i in range(seq_len // chunk):
        rows = keys_ref[i * chunk:(i + 1) * chunk, :]
        kf_ref[i * chunk:(i + 1) * chunk, :] = lax.dot_general(rows, qt, NT, preferred_element_type=F32)
        kft_ref[:, i * chunk:(i + 1) * chunk] = lax.dot_general(qt, rows, NT, preferred_element_type=F32)
    store = pltpu.make_async_copy(kft_ref, kft_hbm, out_sem)
    store.start()

    loads[1].wait()
    loads[2].wait()
    n_lists = steps * KVH
    part = 8

    def gather_list(i, _):
        count = live_ref[i]

        def gather_part(k, _):
            for j in range(part):
                slot = k * part + j
                src = pl.ds(pl.multiple_of(slots_ref[i, slot] * SPAN, SPAN), SPAN)
                dst = pl.ds(pl.multiple_of(slot * SPAN, SPAN), SPAN)
                kg_ref[i, dst, :] = kf_ref[src, :]
                cg_ref[i, dst, :] = cc_ref[src, :]
                sg_ref[i, dst, :] = ss_ref[src, :]
            return 0

        lax.fori_loop(0, (count + part - 1) // part, gather_part, 0)
        return 0

    lax.fori_loop(0, n_lists, gather_list, 0)

    group = QH // KVH
    dests = group // per_device
    rp = sc_ref.shape[1]
    toks = sc_ref.shape[2]
    main = min(tok_main, most * SPAN)
    sc_ref[...] = jnp.full(sc_ref.shape, DEAD, F32)
    o_live = live_ref[n_lists] * SPAN
    first_shard = live_ref[n_lists + 1] == 0

    def q_rows(g):
        hi = jnp.concatenate([qs_ref[g * dests + a, :rp] for a in range(dests)], 0)
        lo = jnp.concatenate([qs_ref[g * dests + a, rp:] for a in range(dests)], 0)
        return jnp.concatenate([hi, lo], 0)

    def slot_scores(g, t, q, lo_row, n_rows):
        i = t * KVH + g
        x = jnp.dot(
            kg_ref[i, lo_row:lo_row + n_rows, :].astype(BF), qt[:, g * HD:(g + 1) * HD], preferred_element_type=F32
        )
        y = jnp.concatenate(
            [x * cg_ref[i, lo_row:lo_row + n_rows, :], x * sg_ref[i, lo_row:lo_row + n_rows, :]], 1
        ).astype(BF)
        s = lax.dot_general(q, y, NT, preferred_element_type=F32)
        s = s[:dests * rp] + s[dests * rp:]
        lane = lax.broadcasted_iota(jnp.int32, (dests * rp, n_rows), 1) + lo_row
        return jnp.where(lane < live_ref[i] * SPAN, s, DEAD)

    def put(g, t, s, at):
        for a in range(dests):
            r = t * per_device
            sc_ref[g * dests + a, r:r + per_device, at:at + s.shape[1]] = s[a * rp + r:a * rp + r + per_device]

    for g in range(KVH):
        q = q_rows(g)
        for t in range(steps):
            put(g, t, slot_scores(g, t, q, 0, main), 0)
        s = lax.dot_general(q, kx_ref[g], NT, preferred_element_type=F32)
        s = s[:dests * rp] + s[dests * rp:]
        lane = lax.broadcasted_iota(jnp.int32, s.shape, 1)
        row = lax.broadcasted_iota(jnp.int32, s.shape, 0) % rp
        new = lane - OMOST * SPAN
        is_live = (lane < o_live) | (first_shard & (new >= 0) & (new * per_device <= row))
        is_live = is_live & (new < steps) & (row < steps * per_device)
        s = jnp.where(is_live, s, DEAD)
        for a in range(dests):
            sc_ref[g * dests + a, :, tok_main:tok_main + LANES] = s[a * rp:(a + 1) * rp]
        if most * SPAN > main:
            for t in range(steps):
                @pl.when(live_ref[t * KVH + g] * SPAN > main)
                def _():
                    put(g, t, slot_scores(g, t, q, main, most * SPAN - main), tok_main + LANES)

    loads[3].wait()
    base_toks = tok_main + LANES
    rowi = lax.broadcasted_iota(jnp.int32, (rp, LANES), 0)
    eye = rowi == lax.broadcasted_iota(jnp.int32, (rp, LANES), 1)
    used = steps * per_device
    for g in range(KVH):
        ps = []
        ms = []
        ls = []
        for a in range(dests):
            s = sc_ref[g * dests + a]
            m = jnp.max(s, axis=1, keepdims=True)
            p = jnp.where(s > 0.5 * DEAD, jnp.exp(s - m), 0.0)
            l = jnp.sum(p, axis=1, keepdims=True)
            sc_ref[g * dests + a] = p
            ps.append(p)
            ms.append(m)
            ls.append(l)
        p = jnp.concatenate(ps, 0)
        hi, lo = split2(p)
        pp = jnp.concatenate([hi, lo], 0)
        acc = jnp.zeros((dests * rp, HD), F32)
        row = lax.broadcasted_iota(jnp.int32, (dests * rp, HD), 0) % rp // per_device
        for t in range(steps):
            i = t * KVH + g
            r = jnp.dot(pp[:, :base_toks], vg_ref[i, :base_toks, :], preferred_element_type=F32)
            r = r[:dests * rp] + r[dests * rp:]
            acc = jnp.where(row == t, r, acc)
        for a in range(dests):
            d = g * dests + a
            m_row = jnp.sum(jnp.where(eye, ms[a], 0.0), axis=0, keepdims=True)
            l_row = jnp.sum(jnp.where(eye, ls[a], 0.0), axis=0, keepdims=True)
            r = acc[a * rp:(a + 1) * rp]
            out_ref[d] = jnp.where(rowi == used, m_row, jnp.where(rowi == used + 1, l_row, r))
        if toks > base_toks:
            for t in range(steps):
                @pl.when(live_ref[t * KVH + g] * SPAN > main)
                def _():
                    i = t * KVH + g
                    rs = slice(t * per_device, (t + 1) * per_device)
                    p = jnp.concatenate([sc_ref[g * dests + a, :, base_toks:] for a in range(dests)], 0)
                    hi, lo = split2(p)
                    pp = jnp.concatenate([hi, lo], 0)
                    r = jnp.dot(pp, vg_ref[i, base_toks:, :], preferred_element_type=F32)
                    r = r[:dests * rp] + r[dests * rp:]
                    for a in range(dests):
                        out_ref[g * dests + a, rs, :] += r[a * rp + rs.start:a * rp + rs.stop]
    store.wait()


def basis(z_ref, a_ref, qt_ref):
    rank = z_ref.shape[0]
    wide = round_up(rank, LANES)
    z = z_ref[...]
    c = lax.dot_general(z, z, NT, preferred_element_type=F32)
    rows = lax.broadcasted_iota(jnp.int32, (rank, wide), 0)
    cols = lax.broadcasted_iota(jnp.int32, (rank, wide), 1)
    a_ref[:, :wide] = jnp.where(rows == cols, 1.0, 0.0)
    a_ref[:, wide:wide + rank] = c
    a_ref[:, wide + rank:] = jnp.zeros((rank, wide - rank), F32)
    nb = 32
    half_tiles = wide // LANES
    for j0 in range(0, rank, nb):
        tiles = [t for t in range(half_tiles) if t * LANES < j0 + nb]
        tiles += [half_tiles + t for t in range(half_tiles) if (t + 1) * LANES > j0]
        part = {t: a_ref[j0:j0 + nb, t * LANES:(t + 1) * LANES] for t in tiles}
        row = lax.broadcasted_iota(jnp.int32, (nb, LANES), 0)
        column = []
        for j in range(nb):
            t, o = divmod(j0 + j, LANES)
            column.append(jnp.broadcast_to(part[half_tiles + t][:, o:o + 1], (nb, LANES)))
        for j in range(nb):
            inverse = lax.rsqrt(jnp.broadcast_to(column[j][j:j + 1, :], (nb, LANES)))
            low = jnp.where(row > j, column[j] * inverse, 0.0)
            for k in range(j + 1, nb):
                column[k] = column[k] - low * jnp.broadcast_to(low[k:k + 1, :], (nb, LANES))
            for t in tiles:
                upper = jnp.broadcast_to(part[t][j:j + 1, :], (nb, LANES)) * inverse
                part[t] = jnp.where(row == j, upper, part[t] - low * upper)
        for t in tiles:
            a_ref[j0:j0 + nb, t * LANES:(t + 1) * LANES] = part[t]
        if j0 + nb < rank:
            upper = jnp.concatenate(
                [part[t] if t in part else jnp.zeros((nb, LANES), F32) for t in range(2 * half_tiles)], 1
            )
            h, m, l = split3(upper)
            left = jnp.concatenate([h, h, m, m, h, l], 0)[:, wide:].astype(BF)
            right = jnp.concatenate([h, m, h, m, l, h], 0).astype(BF)
            for s in range(2):
                d = lax.dot_general(left, right[:, s * wide:(s + 1) * wide], TN, preferred_element_type=F32)
                a_ref[j0 + nb:, s * wide:(s + 1) * wide] -= d[j0 + nb:rank]
    h, m, _ = split3(a_ref[:, :rank])
    q = jnp.dot(jnp.concatenate([h, m], 0).astype(BF), z, preferred_element_type=F32)
    qt_ref[...] = (q[:rank] + q[rank:]).astype(BF)


def merge_kernel(parts_ref, out_ref, *, steps, per_device):
    n, rp, _ = parts_ref.shape
    used = steps * per_device
    eye = lax.broadcasted_iota(jnp.int32, (rp, LANES), 0) == lax.broadcasted_iota(jnp.int32, (rp, LANES), 1)

    def column(s, r):
        return jnp.sum(jnp.where(eye, parts_ref[s, r:r + 1, :], 0.0), axis=1, keepdims=True)

    ms = [column(s, used) for s in range(n)]
    top = functools.reduce(jnp.maximum, ms)
    total = jnp.zeros((rp, 1), F32)
    acc = jnp.zeros((rp, HD), F32)
    for s in range(n):
        w = jnp.exp(ms[s] - top)
        total = total + w * column(s, used + 1)
        acc = acc + w * parts_ref[s]
    o = acc / total
    for t in range(steps):
        for i in range(per_device):
            r = t * per_device + i
            out_ref[t:t + 1, i * HD:(i + 1) * HD] = o[r:r + 1, :].astype(BF)


def swap(x, moves):
    return lax.ppermute(x, "seq", moves)


def on_device(
    cache_keys,
    cache_values,
    sketch_matrix,
    queries,
    fresh_keys,
    fresh_values,
    chosen,
    shard_counts,
    outliers,
):
    seq_len, width = cache_keys.shape
    devices = lax.axis_size("seq")
    myself = lax.axis_index("seq")
    length = seq_len * devices
    steps = queries.shape[0]
    rank = sketch_matrix.shape[1]
    per_device = QH // devices
    n_lists = steps * KVH
    most = 3 * chosen.shape[2] // devices
    tok_sel = most * SPAN
    tok_main = min(256, round_up(tok_sel, LANES))
    toks = tok_main + LANES + max(0, round_up(tok_sel - tok_main, LANES))
    used = steps * per_device
    rp = round_up(used + 2, 8)
    me = jnp.full((1,), myself, jnp.int32)

    keep, send = sketch_share(me, sketch_matrix.T, cache_keys, length)

    half_width = HD // 2
    exponents = jnp.arange(half_width, dtype=F32) * (2.0 / HD)
    inverse_freq = jnp.exp(-jnp.log(F32(500000.0)) * exponents)
    inverse_freq = jnp.concatenate([inverse_freq, inverse_freq])
    blk = 64
    coarse = (myself * seq_len + blk * jnp.arange(seq_len // blk, dtype=jnp.int32)).astype(F32)[:, None] * inverse_freq
    fine = jnp.arange(blk, dtype=jnp.int32).astype(F32)[:, None] * inverse_freq
    late = (length + jnp.arange(steps, dtype=jnp.int32)).astype(F32)[:, None] * inverse_freq

    x_rows = LANES
    table = jax.ShapeDtypeStruct((seq_len, HD), F32)
    n_chunks = 8 if seq_len % 128 == 0 else 1
    n_dest = devices
    slots, live, cc, ss, vg, kx, qs = pl.pallas_call(
        functools.partial(
            prepare_kernel, most=most, per_device=per_device, tok_sel=tok_sel, tok_main=tok_main
        ),
        in_specs=[smem()] * 4 + [vmem()] * 9 + [hbm()] * 2,
        out_specs=[smem()] * 2 + [vmem()] * 5,
        out_shape=[
            jax.ShapeDtypeStruct((n_lists, most), jnp.int32),
            jax.ShapeDtypeStruct((n_lists + 2,), jnp.int32),
            table,
            table,
            jax.ShapeDtypeStruct((n_lists, toks, HD), BF),
            jax.ShapeDtypeStruct((KVH, x_rows, 2 * HD), BF),
            jax.ShapeDtypeStruct((n_dest, 2 * rp, 2 * HD), BF),
        ],
        scratch_shapes=[
            pltpu.VMEM((seq_len, width), BF),
            pltpu.VMEM((OMOST, 16, width), BF),
            pltpu.VMEM((toks, HD), F32),
            pltpu.VMEM((x_rows, HD), F32),
            pltpu.VMEM((n_dest, rp, HD), F32),
            pltpu.SemaphoreType.DMA((n_chunks,)),
            pltpu.SemaphoreType.DMA((OMOST,)),
        ],
        compiler_params=pltpu.CompilerParams(vmem_limit_bytes=48 << 20),
        name="prepare",
    )(
        me, chosen.reshape(n_lists, -1), shard_counts.reshape(n_lists, -1), outliers,
        queries, fresh_keys, fresh_values,
        jnp.cos(coarse), jnp.sin(coarse), jnp.cos(fine), jnp.sin(fine), jnp.cos(late), jnp.sin(late),
        cache_keys, cache_values,
    )

    z = keep + swap(send, [(i, i ^ 1) for i in range(devices)])
    hops = [1 << k for k in range(1, devices.bit_length() - 1)]
    for k in range(len(hops)):
        other = k ^ 1 if k < 2 and len(hops) >= 2 else k
        moves = [(i, i ^ hops[k if i % 2 == 0 else other]) for i in range(devices)]
        z = z + swap(z.astype(BF), moves).astype(F32)
    z = z.astype(BF)
    z_other = swap(z, [(i, i ^ 1) for i in range(devices)])

    kft, parts = pl.pallas_call(
        functools.partial(
            attend_kernel, most=most, per_device=per_device, steps=steps, tok_main=tok_main
        ),
        in_specs=[smem()] * 3 + [vmem()] * 4 + [hbm()] * 4,
        out_specs=[hbm(), vmem()],
        out_shape=[
            jax.ShapeDtypeStruct((rank, seq_len), F32),
            jax.ShapeDtypeStruct((n_dest, rp, HD), F32),
        ],
        scratch_shapes=[
            pltpu.VMEM((seq_len, width), BF),
            pltpu.VMEM((seq_len, HD), F32),
            pltpu.VMEM((seq_len, HD), F32),
            pltpu.VMEM((n_lists, toks, HD), BF),
            pltpu.VMEM((rank, width), BF),
            pltpu.VMEM((rank, 2 * round_up(rank, LANES)), F32),
            pltpu.VMEM((rank, width), BF),
            pltpu.VMEM((seq_len, rank), F32),
            pltpu.VMEM((rank, seq_len), F32),
            pltpu.VMEM((n_lists, tok_sel, rank), F32),
            pltpu.VMEM((n_lists, tok_sel, HD), F32),
            pltpu.VMEM((n_lists, tok_sel, HD), F32),
            pltpu.VMEM((n_dest, rp, toks), F32),
            pltpu.SemaphoreType.DMA((4,)),
            pltpu.SemaphoreType.DMA,
        ],
        compiler_params=pltpu.CompilerParams(vmem_limit_bytes=60 << 20),
        name="attend",
    )(me, slots, live, z, z_other, kx, qs, cache_keys, cc, ss, vg)

    parts = lax.all_to_all(parts, "seq", 0, 0, tiled=True)
    attended = pl.pallas_call(
        functools.partial(merge_kernel, steps=steps, per_device=per_device),
        in_specs=[vmem()],
        out_specs=vmem(),
        out_shape=jax.ShapeDtypeStruct((steps, per_device * HD), BF),
        name="merge",
    )(parts)
    return (attended, kft.T)


def solution(mesh):
    in_specs = (
        P(("groups", "seq"), None),
        P(("groups", "seq"), None),
        P(),
        P("groups", None),
        P("groups", None),
        P("groups", None),
        P("groups", None, None),
        P("groups", None, None),
        P("groups"),
    )
    out_specs = (P("groups", "seq"), P(("groups", "seq"), None))
    return jax.shard_map(
        on_device, mesh=mesh, in_specs=in_specs, out_specs=out_specs, check_vma=False
    )
```

```python
import functools

import jax
import jax.numpy as jnp
from jax import lax
from jax.experimental import pallas as pl
from jax.experimental.pallas import tpu as pltpu
from jax.sharding import PartitionSpec as P

KVH = 8
HD = 128
QH = 64
SPAN = 8
OMOST = 4
BF = jnp.bfloat16
F32 = jnp.float32
DEAD = -1e30
LANES = 128
MAIN = 640
NT = (((1,), (1,)), ((), ()))
TN = (((0,), (0,)), ((), ()))


def vmem():
    return pl.BlockSpec(memory_space=pltpu.VMEM)


def smem():
    return pl.BlockSpec(memory_space=pltpu.SMEM)


def hbm():
    return pl.BlockSpec(memory_space=pltpu.HBM)


def anywhere():
    return pl.BlockSpec(memory_space=pl.ANY)


def round_up(x, m):
    return (x + m - 1) // m * m


def split2(x):
    high = x.astype(BF)
    return high, (x - high.astype(F32)).astype(BF)


def split3(x):
    high = x.astype(BF).astype(F32)
    rest = x - high
    middle = rest.astype(BF).astype(F32)
    return high, middle, rest - middle


def sketch_kernel(
    me_ref, st_hbm, keys_hbm, keep_ref, send_ref, st_ref, keys_ref, acc_ref, st_sem, sem, *, scale, chunk
):
    seq_len = keys_ref.shape[0]
    rank = st_ref.shape[0]
    half = rank // 2
    n = seq_len // chunk
    st_copy = pltpu.make_async_copy(st_hbm, st_ref, st_sem)
    st_copy.start()
    copies = [
        pltpu.make_async_copy(
            keys_hbm.at[pl.ds(i * chunk, chunk)], keys_ref.at[pl.ds(i * chunk, chunk)], sem.at[i]
        )
        for i in range(n)
    ]
    for c in copies:
        c.start()
    st_copy.wait()
    st = st_ref[...].astype(BF)

    def rows(i):
        return keys_ref[i * chunk:(i + 1) * chunk, :]

    def first(i):
        return lax.dot_general(st, rows(i), NT, preferred_element_type=F32).astype(BF)

    def second(i, y):
        return jnp.dot(y, rows(i), preferred_element_type=F32)

    copies[0].wait()
    y = first(0)
    for i in range(1, n):
        copies[i].wait()
        y_next = first(i)
        z = second(i - 1, y)
        if i == 1:
            acc_ref[...] = z
        else:
            acc_ref[...] += z
        y = y_next
    acc_ref[...] = (acc_ref[...] + second(n - 1, y)) * scale
    core = me_ref[0] % 2
    keep_ref[...] = acc_ref[pl.ds(pl.multiple_of(core * half, 8), half), :]
    send_ref[...] = acc_ref[pl.ds(pl.multiple_of((1 - core) * half, 8), half), :]


def sketch_share(me, sketch_t, cache_keys, length):
    seq_len, width = cache_keys.shape
    rank = sketch_t.shape[0]
    chunk = min(512, seq_len)
    half = jax.ShapeDtypeStruct((rank // 2, width), F32)
    return pl.pallas_call(
        functools.partial(sketch_kernel, scale=1.0 / length, chunk=chunk),
        in_specs=[smem(), hbm(), hbm()],
        out_specs=[vmem(), vmem()],
        out_shape=[half, half],
        scratch_shapes=[
            pltpu.VMEM((rank, width), F32),
            pltpu.VMEM((seq_len, width), BF),
            pltpu.VMEM((rank, width), F32),
            pltpu.SemaphoreType.DMA,
            pltpu.SemaphoreType.DMA((seq_len // chunk,)),
        ],
        compiler_params=pltpu.CompilerParams(vmem_limit_bytes=24 << 20),
        name="sketch_share",
    )(me, sketch_t, cache_keys)


def prepare_kernel(
    me_ref, chosen_ref, counts_ref, outl_ref, q_ref, fk_ref, ca_ref, sa_ref, cb_ref, sb_ref, cq_ref, sq_ref,
    keys_hbm, after_ref,
    slots_ref, live_ref, kx_ref, qs_ref,
    okeys_ref, xtmp_ref, qtmp_ref, osem, *, most, per_device, spans
):
    steps = q_ref.shape[0]
    me = me_ref[0]
    base = me * spans

    n_out = outl_ref.shape[0]
    o_first = jnp.int32(0)
    o_here = jnp.int32(0)
    for i in range(n_out):
        s = outl_ref[i]
        o_first = o_first + (s < base).astype(jnp.int32)
        o_here = o_here + ((s >= base) & (s < base + spans)).astype(jnp.int32)
    o_span = [
        jnp.clip(outl_ref[jnp.minimum(o_first + j, n_out - 1)] - base, 0, spans - 1) for j in range(OMOST)
    ]
    o_copies = [
        pltpu.make_async_copy(
            keys_hbm.at[pl.ds(pl.multiple_of(o_span[j] // 2 * 16, 16), 16)], okeys_ref.at[j], osem.at[j]
        )
        for j in range(OMOST)
    ]
    for c in o_copies:
        c.start()

    sel = chosen_ref.shape[1]
    shards = counts_ref.shape[1]
    for g in range(KVH):
        at = jnp.int32(0)
        for t in range(steps):
            i = t * KVH + g
            start = jnp.int32(0)
            for r in range(shards):
                start = start + jnp.where(r < me, counts_ref[i, r], 0)
            count = jnp.minimum(counts_ref[i, me], most)
            live_ref[g * (steps + 1) + t] = at

            def put(j, _, i=i, start=start, at=at, g=g):
                picked = chosen_ref[i, jnp.minimum(start + j, sel - 1)]
                slots_ref[g, at + j] = jnp.clip(picked - base, 0, spans - 1)
                return 0

            lax.fori_loop(0, count, put, 0)
            at = at + count
        live_ref[g * (steps + 1) + steps] = at

        def fill(j, _, g=g):
            slots_ref[g, j] = 0
            return 0

        lax.fori_loop(at, (at + 7) // 8 * 8, fill, 0)
    n_at = KVH * (steps + 1)
    live_ref[n_at] = o_here
    live_ref[n_at + 1] = me
    for j in range(OMOST):
        live_ref[n_at + 2 + j] = o_span[j]

    lane = lax.broadcasted_iota(jnp.int32, (8, LANES), 1)
    sign = jnp.where(lane < HD // 2, -1.0, 1.0)

    n_dest = qs_ref.shape[0]
    rp = qs_ref.shape[1] // 2
    scale = 1.0 / (HD ** 0.5)
    qtmp_ref[...] = jnp.zeros_like(qtmp_ref)
    for t in range(steps):
        x = q_ref[t:t + 1, :].astype(F32)
        for h in range(QH):
            d, i = h // per_device, h % per_device
            r = t * per_device + i
            qtmp_ref[d, r:r + 1, :] = x[:, h * HD:(h + 1) * HD]
    row = lax.broadcasted_iota(jnp.int32, (rp, LANES), 0)
    lane_r = lax.broadcasted_iota(jnp.int32, (rp, LANES), 1)
    cq = jnp.zeros((rp, LANES), F32)
    sq = jnp.zeros((rp, LANES), F32)
    for t in range(steps):
        here = (row >= t * per_device) & (row < (t + 1) * per_device)
        cq = jnp.where(here, cq_ref[t:t + 1, :], cq)
        sq = jnp.where(here, sq_ref[t:t + 1, :], sq)
    sq = jnp.where(lane_r < HD // 2, -sq, sq)
    for d in range(n_dest):
        x = qtmp_ref[d]
        x = (x * cq + pltpu.roll(x, HD // 2, 1) * sq) * scale
        z = jnp.where(lane_r < HD // 2, 1.0, -1.0) * pltpu.roll(x, HD // 2, 1)
        hi, lo = split2(jnp.concatenate([x, z], 1))
        qs_ref[d] = jnp.concatenate([hi, lo], 0)

    blk = cb_ref.shape[0] // SPAN
    turns = []
    for j in range(OMOST):
        a = o_span[j] // blk
        b = pl.ds(pl.multiple_of(o_span[j] % blk * SPAN, SPAN), SPAN)
        ca, sa = ca_ref[pl.ds(a, 1), :], sa_ref[pl.ds(a, 1), :]
        cb, sb = cb_ref[b, :], sb_ref[b, :]
        turns.append((ca * cb - sa * sb, (sa * cb + ca * sb) * sign))
    for c in o_copies:
        c.wait()
    x_rows = kx_ref.shape[1]
    xtmp_ref[...] = jnp.zeros_like(xtmp_ref)
    fs = sq_ref[:steps, :] * sign[:1]
    for g in range(KVH):
        sl = slice(g * HD, (g + 1) * HD)
        for j in range(OMOST):
            wide = okeys_ref[j, :, sl].astype(F32)
            x = jnp.where(o_span[j] % 2 == 0, wide[:8], wide[8:])
            xtmp_ref[j * SPAN:(j + 1) * SPAN, :] = x * turns[j][0] + pltpu.roll(x, HD // 2, 1) * turns[j][1]
        x = fk_ref[:, sl].astype(F32)
        o = OMOST * SPAN
        xtmp_ref[o:o + steps, :] = x * cq_ref[:steps, :] + pltpu.roll(x, HD // 2, 1) * fs
        kx_ref[g, :, :HD] = xtmp_ref[...].astype(BF)
        kx_ref[g, :, HD:] = jnp.zeros((x_rows, HD), BF)


def values_kernel(
    slots_ref, live_ref, fv_ref, values_hbm, after_ref, vg_ref, tie_ref, values_ref, vtmp_ref, sem, *, main
):
    steps = fv_ref.shape[0]
    rows_all = vtmp_ref.shape[0]
    copies = [
        pltpu.make_async_copy(values_hbm.at[:, pl.ds(g * HD, HD)], values_ref.at[g], sem.at[g]) for g in range(KVH)
    ]
    for c in copies:
        c.start()
    tie_ref[...] = jnp.zeros_like(tie_ref)
    vtmp_ref[...] = jnp.zeros_like(vtmp_ref)
    n_at = KVH * (steps + 1)

    for g in range(KVH):
        def rows_of(span, g=g):
            wide = values_ref[g, pl.ds(pl.multiple_of(span // 2 * 16, 16), 16), :].astype(F32)
            return jnp.where(span % 2 == 0, wide[:8], wide[8:])

        copies[g].wait()
        for j in range(OMOST):
            vtmp_ref[j * SPAN:(j + 1) * SPAN, :] = rows_of(live_ref[n_at + 2 + j])
        vtmp_ref[OMOST * SPAN:OMOST * SPAN + steps, :] = fv_ref[:, g * HD:(g + 1) * HD].astype(F32)
        count = live_ref[g * (steps + 1) + steps]

        def put(k, _, g=g, rows_of=rows_of):
            for j in range(8):
                o = pl.multiple_of(LANES + (k * 8 + j) * SPAN, SPAN)
                vtmp_ref[pl.ds(o, SPAN), :] = rows_of(slots_ref[g, k * 8 + j])
            return 0

        lax.fori_loop(0, (count + 7) // 8, put, 0)
        vg_ref[g, :LANES + main, :] = vtmp_ref[:LANES + main, :].astype(BF)
        if LANES + main < rows_all:
            def more(k, _, g=g):
                at = pl.ds(pl.multiple_of(LANES + main + k * LANES, LANES), LANES)
                vg_ref[g, at, :] = vtmp_ref[at, :].astype(BF)
                return 0

            lax.fori_loop(0, (jnp.maximum(count * SPAN - main, 0) + LANES - 1) // LANES, more, 0)


def attend_kernel(
    core_ref, slots_ref, live_ref, zmine_ref, zother_ref, kx_ref, qs_ref, vg_ref, ca_ref, sa_ref, cb_ref, sb_ref,
    keys_hbm,
    kft_hbm, out_ref,
    keys_ref, z_ref, a_ref, qt_ref, kf_ref, kft_ref, kg_ref, cg_ref, sg_ref, sc_ref,
    sem, out_sem, *, per_device, steps, main, stop=9
):
    rank, width = z_ref.shape
    half = rank // 2
    seq_len = keys_ref.shape[0]
    load = pltpu.make_async_copy(keys_hbm, keys_ref, sem)
    load.start()

    core = core_ref[0] % 2
    z_ref[pl.ds(pl.multiple_of(core * half, 16), half), :] = zmine_ref[...]
    z_ref[pl.ds(pl.multiple_of((1 - core) * half, 16), half), :] = zother_ref[...]
    basis(z_ref, a_ref, qt_ref)
    qt = qt_ref[...]

    load.wait()
    if stop == 1:
        return
    chunk = seq_len // KVH
    for i in range(KVH):
        rows = keys_ref[i * chunk:(i + 1) * chunk, :]
        kf_ref[i * chunk:(i + 1) * chunk, :] = lax.dot_general(rows, qt, NT, preferred_element_type=F32)
    if stop == 2:
        return

    part = 8
    blk = cb_ref.shape[0] // SPAN
    totals = [live_ref[g * (steps + 1) + steps] for g in range(KVH)]
    for g in range(KVH):
        def gather(k, _, g=g):
            for j in range(part):
                slot = k * part + j
                span = slots_ref[g, slot]
                src = pl.ds(pl.multiple_of(span * SPAN, SPAN), SPAN)
                dst = pl.ds(pl.multiple_of(slot * SPAN, SPAN), SPAN)
                kg_ref[g, dst, :] = kf_ref[src, :]
                a = span // blk
                b = pl.ds(pl.multiple_of(span % blk * SPAN, SPAN), SPAN)
                ca, sa = ca_ref[pl.ds(a, 1), :], sa_ref[pl.ds(a, 1), :]
                cb, sb = cb_ref[b, :], sb_ref[b, :]
                cg_ref[g, dst, :] = ca * cb - sa * sb
                sg_ref[g, dst, :] = sa * cb + ca * sb
            return 0

        lax.fori_loop(0, (totals[g] + part - 1) // part, gather, 0)
    if stop == 3:
        return

    group = QH // KVH
    dests = group // per_device
    rp = sc_ref.shape[1]
    qr = dests * rp
    n_at = KVH * (steps + 1)
    o_live = live_ref[n_at] * SPAN
    first_shard = live_ref[n_at + 1] == 0

    def q_rows(g):
        hi = jnp.concatenate([qs_ref[g * dests + a, :rp] for a in range(dests)], 0)
        lo = jnp.concatenate([qs_ref[g * dests + a, rp:] for a in range(dests)], 0)
        return jnp.concatenate([hi, lo], 0)

    def bounds(g, shape):
        step = lax.broadcasted_iota(jnp.int32, shape, 0) % rp // per_device
        first = jnp.zeros(shape, jnp.int32)
        last = jnp.zeros(shape, jnp.int32)
        for t in range(steps):
            first = jnp.where(step == t, live_ref[g * (steps + 1) + t] * SPAN, first)
            last = jnp.where(step == t, live_ref[g * (steps + 1) + t + 1] * SPAN, last)
        return first, last

    def slot_scores(g, q, rows, n_rows, at):
        x = jnp.dot(kg_ref[g, rows, :].astype(BF), qt_ref[:, g * HD:(g + 1) * HD], preferred_element_type=F32)
        y = jnp.concatenate([x * cg_ref[g, rows, :], x * sg_ref[g, rows, :]], 1).astype(BF)
        s = lax.dot_general(q, y, NT, preferred_element_type=F32)
        s = s[:qr] + s[qr:]
        lane = lax.broadcasted_iota(jnp.int32, (qr, n_rows), 1) + at
        first, last = bounds(g, (qr, n_rows))
        return jnp.where((lane >= first) & (lane < last), s, DEAD)

    def put(g, s, lanes):
        for a in range(dests):
            sc_ref[g * dests + a, :, lanes] = s[a * rp:(a + 1) * rp]

    def kft_part(i):
        rows = keys_ref[i * chunk:(i + 1) * chunk, :]
        kft_ref[:, i * chunk:(i + 1) * chunk] = lax.dot_general(qt, rows, NT, preferred_element_type=F32)

    for g in range(KVH):
        q = q_rows(g)
        put(g, slot_scores(g, q, slice(0, main), main, 0), slice(LANES, LANES + main))
        s = lax.dot_general(q, kx_ref[g], NT, preferred_element_type=F32)
        s = s[:qr] + s[qr:]
        lane = lax.broadcasted_iota(jnp.int32, s.shape, 1)
        row = lax.broadcasted_iota(jnp.int32, s.shape, 0) % rp
        new = lane - OMOST * SPAN
        is_live = (lane < o_live) | (first_shard & (new >= 0) & (new * per_device <= row))
        is_live = is_live & (new < steps) & (row < steps * per_device)
        put(g, jnp.where(is_live, s, DEAD), slice(0, LANES))
        kft_part(g)
    store = pltpu.make_async_copy(kft_ref, kft_hbm, out_sem)
    store.start()
    extra = kg_ref.shape[1] - main
    blocks = [(jnp.maximum(totals[g] * SPAN - main, 0) + LANES - 1) // LANES for g in range(KVH)]
    if extra > 0:
        for g in range(KVH):
            def more(k, _, g=g):
                at = pl.multiple_of(main + k * LANES, LANES)
                s = slot_scores(g, q_rows(g), pl.ds(at, LANES), LANES, at)
                put(g, s, pl.ds(pl.multiple_of(LANES + at, LANES), LANES))
                return 0

            lax.fori_loop(0, blocks[g], more, 0)
    if stop == 4:
        store.wait()
        return

    rowi = lax.broadcasted_iota(jnp.int32, (rp, LANES), 0)
    eye = rowi == lax.broadcasted_iota(jnp.int32, (rp, LANES), 1)
    used = steps * per_device

    def weighted(p, values):
        hi, lo = split2(p)
        r = jnp.dot(jnp.concatenate([hi, lo], 0), values, preferred_element_type=F32)
        return r[:qr] + r[qr:]

    def weights(s, m):
        return jnp.where(s > 0.5 * DEAD, jnp.exp(s - m), 0.0)

    def heads(g):
        return slice(g * dests, (g + 1) * dests)

    for g in range(KVH):
        s = sc_ref[heads(g), :, :LANES + main].reshape(qr, LANES + main)
        m = jnp.max(s, axis=1, keepdims=True)
        if extra > 0:
            def top(k, m, g=g):
                at = pl.ds(pl.multiple_of(LANES + main + k * LANES, LANES), LANES)
                return jnp.maximum(m, jnp.max(sc_ref[heads(g), :, at].reshape(qr, LANES), axis=1, keepdims=True))

            m = lax.fori_loop(0, blocks[g], top, m)
        p = weights(s, m)
        l = jnp.sum(p, axis=1, keepdims=True)
        acc = weighted(p, vg_ref[g, :LANES + main, :])
        if extra > 0:
            def add(k, carry, g=g, m=m):
                l, acc = carry
                at = pl.ds(pl.multiple_of(LANES + main + k * LANES, LANES), LANES)
                p = weights(sc_ref[heads(g), :, at].reshape(qr, LANES), m)
                return l + jnp.sum(p, axis=1, keepdims=True), acc + weighted(p, vg_ref[g, at, :])

            l, acc = lax.fori_loop(0, blocks[g], add, (l, acc))
        for a in range(dests):
            rs = slice(a * rp, (a + 1) * rp)
            m_row = jnp.sum(jnp.where(eye, m[rs], 0.0), axis=0, keepdims=True)
            l_row = jnp.sum(jnp.where(eye, l[rs], 0.0), axis=0, keepdims=True)
            out_ref[g * dests + a] = jnp.where(
                rowi == used, m_row, jnp.where(rowi == used + 1, l_row, acc[rs])
            )
    store.wait()


def basis(z_ref, a_ref, qt_ref):
    rank = z_ref.shape[0]
    wide = round_up(rank, LANES)
    z = z_ref[...]
    c = lax.dot_general(z, z, NT, preferred_element_type=F32)
    rows = lax.broadcasted_iota(jnp.int32, (rank, wide), 0)
    cols = lax.broadcasted_iota(jnp.int32, (rank, wide), 1)
    a_ref[:, :wide] = jnp.where(rows == cols, 1.0, 0.0)
    a_ref[:, wide:wide + rank] = c
    a_ref[:, wide + rank:] = jnp.zeros((rank, wide - rank), F32)
    nb = 32
    half_tiles = wide // LANES
    for j0 in range(0, rank, nb):
        tiles = [t for t in range(half_tiles) if t * LANES < j0 + nb]
        tiles += [half_tiles + t for t in range(half_tiles) if (t + 1) * LANES > j0]
        part = {t: a_ref[j0:j0 + nb, t * LANES:(t + 1) * LANES] for t in tiles}
        row = lax.broadcasted_iota(jnp.int32, (nb, LANES), 0)
        column = []
        for j in range(nb):
            t, o = divmod(j0 + j, LANES)
            column.append(jnp.broadcast_to(part[half_tiles + t][:, o:o + 1], (nb, LANES)))
        for j in range(nb):
            inverse = lax.rsqrt(jnp.broadcast_to(column[j][j:j + 1, :], (nb, LANES)))
            low = jnp.where(row > j, column[j] * inverse, 0.0)
            for k in range(j + 1, nb):
                column[k] = column[k] - low * jnp.broadcast_to(low[k:k + 1, :], (nb, LANES))
            for t in tiles:
                upper = jnp.broadcast_to(part[t][j:j + 1, :], (nb, LANES)) * inverse
                part[t] = jnp.where(row == j, upper, part[t] - low * upper)
        for t in tiles:
            a_ref[j0:j0 + nb, t * LANES:(t + 1) * LANES] = part[t]
        if j0 + nb < rank:
            upper = jnp.concatenate(
                [part[t] if t in part else jnp.zeros((nb, LANES), F32) for t in range(2 * half_tiles)], 1
            )
            h, m, l = split3(upper)
            left = jnp.concatenate([h, h, m, m, h, l], 0)[:, wide:].astype(BF)
            right = jnp.concatenate([h, m, h, m, l, h], 0).astype(BF)
            for s in range(2):
                d = lax.dot_general(left, right[:, s * wide:(s + 1) * wide], TN, preferred_element_type=F32)
                a_ref[j0 + nb:, s * wide:(s + 1) * wide] -= d[j0 + nb:rank]
    h, m, _ = split3(a_ref[:, :rank])
    q = jnp.dot(jnp.concatenate([h, m], 0).astype(BF), z, preferred_element_type=F32)
    qt_ref[...] = (q[:rank] + q[rank:]).astype(BF)


def merge_kernel(parts_ref, out_ref, *, steps, per_device):
    n, rp, _ = parts_ref.shape
    used = steps * per_device
    eye = lax.broadcasted_iota(jnp.int32, (rp, LANES), 0) == lax.broadcasted_iota(jnp.int32, (rp, LANES), 1)

    def column(s, r):
        return jnp.sum(jnp.where(eye, parts_ref[s, r:r + 1, :], 0.0), axis=1, keepdims=True)

    ms = [column(s, used) for s in range(n)]
    top = functools.reduce(jnp.maximum, ms)
    total = jnp.zeros((rp, 1), F32)
    acc = jnp.zeros((rp, HD), F32)
    for s in range(n):
        w = jnp.exp(ms[s] - top)
        total = total + w * column(s, used + 1)
        acc = acc + w * parts_ref[s]
    o = acc / total
    for t in range(steps):
        for i in range(per_device):
            r = t * per_device + i
            out_ref[t:t + 1, i * HD:(i + 1) * HD] = o[r:r + 1, :].astype(BF)


def swap(x, moves):
    return lax.ppermute(x, "seq", moves)


def on_device(
    cache_keys,
    cache_values,
    sketch_matrix,
    queries,
    fresh_keys,
    fresh_values,
    chosen,
    shard_counts,
    outliers,
):
    seq_len, width = cache_keys.shape
    devices = lax.axis_size("seq")
    myself = lax.axis_index("seq")
    length = seq_len * devices
    steps = queries.shape[0]
    rank = sketch_matrix.shape[1]
    per_device = QH // devices
    n_lists = steps * KVH
    most = 3 * chosen.shape[2] // devices
    slots_all = round_up(steps * most, LANES // SPAN)
    tok_all = slots_all * SPAN
    main = min(MAIN, tok_all)
    used = steps * per_device
    rp = round_up(used + 2, 8)
    n_dest = devices
    me = jnp.full((1,), myself, jnp.int32)

    keep, send = sketch_share(me, sketch_matrix.T, cache_keys, length)

    half_width = HD // 2
    exponents = jnp.arange(half_width, dtype=F32) * (2.0 / HD)
    inverse_freq = jnp.exp(-jnp.log(F32(500000.0)) * exponents)
    inverse_freq = jnp.concatenate([inverse_freq, inverse_freq])
    blk = 64
    coarse = (myself * seq_len + blk * jnp.arange(seq_len // blk, dtype=jnp.int32)).astype(F32)[:, None] * inverse_freq
    fine = jnp.arange(blk, dtype=jnp.int32).astype(F32)[:, None] * inverse_freq
    late = (length + jnp.arange(steps, dtype=jnp.int32)).astype(F32)[:, None] * inverse_freq
    turns = (jnp.cos(coarse), jnp.sin(coarse), jnp.cos(fine), jnp.sin(fine))

    def prepare(after):
        return pl.pallas_call(
            functools.partial(prepare_kernel, most=most, per_device=per_device, spans=seq_len // SPAN),
            in_specs=[smem()] * 4 + [vmem()] * 8 + [hbm(), anywhere()],
            out_specs=[smem()] * 2 + [vmem()] * 2,
            out_shape=[
                jax.ShapeDtypeStruct((KVH, slots_all), jnp.int32),
                jax.ShapeDtypeStruct((KVH * (steps + 1) + 2 + OMOST,), jnp.int32),
                jax.ShapeDtypeStruct((KVH, LANES, 2 * HD), BF),
                jax.ShapeDtypeStruct((n_dest, 2 * rp, 2 * HD), BF),
            ],
            scratch_shapes=[
                pltpu.VMEM((OMOST, 16, width), BF),
                pltpu.VMEM((LANES, HD), F32),
                pltpu.VMEM((n_dest, rp, HD), F32),
                pltpu.SemaphoreType.DMA((OMOST,)),
            ],
            compiler_params=pltpu.CompilerParams(vmem_limit_bytes=8 << 20),
            name="prepare",
        )(
            me, chosen.reshape(n_lists, -1), shard_counts.reshape(n_lists, -1), outliers,
            queries, fresh_keys, *turns, jnp.cos(late), jnp.sin(late), cache_keys, after,
        )

    def slot_values(slots, live, after):
        return pl.pallas_call(
            functools.partial(values_kernel, main=main),
            in_specs=[smem()] * 2 + [vmem(), hbm(), anywhere()],
            out_specs=[vmem()] * 2,
            out_shape=[
                jax.ShapeDtypeStruct((KVH, LANES + tok_all, HD), BF),
                jax.ShapeDtypeStruct((1, LANES), F32),
            ],
            scratch_shapes=[
                pltpu.VMEM((KVH, seq_len, HD), BF),
                pltpu.VMEM((LANES + tok_all, HD), F32),
                pltpu.SemaphoreType.DMA((KVH,)),
            ],
            compiler_params=pltpu.CompilerParams(vmem_limit_bytes=16 << 20),
            name="slot_values",
        )(slots, live, fresh_values, cache_values, after)

    z = keep + swap(send, [(i, i ^ 1) for i in range(devices)])
    hops = [1 << k for k in range(1, devices.bit_length() - 1)]
    for k in range(len(hops)):
        other = k ^ 1 if k < 2 and len(hops) >= 2 else k
        moves = [(i, i ^ hops[k if i % 2 == 0 else other]) for i in range(devices)]
        going = z.astype(BF)
        if k == len(hops) - 2:
            slots, live, kx, qs = prepare(going)
        came = swap(going, moves).astype(F32)
        if k == len(hops) - 1:
            vg, tie = slot_values(slots, live, going)
            came = came + tie[0, 0]
        z = z + came
    z = z.astype(BF)
    z_other = swap(z, [(i, i ^ 1) for i in range(devices)])

    kft, parts = pl.pallas_call(
        functools.partial(attend_kernel, per_device=per_device, steps=steps, main=main),
        in_specs=[smem()] * 3 + [vmem()] * 9 + [hbm()],
        out_specs=[hbm(), vmem()],
        out_shape=[
            jax.ShapeDtypeStruct((rank, seq_len), F32),
            jax.ShapeDtypeStruct((n_dest, rp, HD), F32),
        ],
        scratch_shapes=[
            pltpu.VMEM((seq_len, width), BF),
            pltpu.VMEM((rank, width), BF),
            pltpu.VMEM((rank, 2 * round_up(rank, LANES)), F32),
            pltpu.VMEM((rank, width), BF),
            pltpu.VMEM((seq_len, rank), F32),
            pltpu.VMEM((rank, seq_len), F32),
            pltpu.VMEM((KVH, tok_all, rank), F32),
            pltpu.VMEM((KVH, tok_all, HD), F32),
            pltpu.VMEM((KVH, tok_all, HD), F32),
            pltpu.VMEM((n_dest, rp, LANES + tok_all), F32),
            pltpu.SemaphoreType.DMA,
            pltpu.SemaphoreType.DMA,
        ],
        compiler_params=pltpu.CompilerParams(vmem_limit_bytes=42 << 20),
        name="attend",
    )(me, slots, live, z, z_other, kx, qs, vg, *turns, cache_keys)

    parts = lax.all_to_all(parts, "seq", 0, 0, tiled=True)
    attended = pl.pallas_call(
        functools.partial(merge_kernel, steps=steps, per_device=per_device),
        in_specs=[vmem()],
        out_specs=vmem(),
        out_shape=jax.ShapeDtypeStruct((steps, per_device * HD), BF),
        name="merge",
    )(parts)
    return (attended, kft.T)


def solution(mesh):
    in_specs = (
        P(("groups", "seq"), None),
        P(("groups", "seq"), None),
        P(),
        P("groups", None),
        P("groups", None),
        P("groups", None),
        P("groups", None, None),
        P("groups", None, None),
        P("groups"),
    )
    out_specs = (P("groups", "seq"), P(("groups", "seq"), None))
    return jax.shard_map(
        on_device, mesh=mesh, in_specs=in_specs, out_specs=out_specs, check_vma=False
    )
```

```python
import functools

import jax
import jax.numpy as jnp
from jax import lax
from jax.experimental import pallas as pl
from jax.experimental.pallas import tpu as pltpu
from jax.sharding import PartitionSpec as P

KVH = 8
HD = 128
QH = 64
SPAN = 8
OMOST = 4
BF = jnp.bfloat16
F32 = jnp.float32
DEAD = -1e30
LANES = 128
MAIN = 640
PART = 8
AHEAD = 3
NT = (((1,), (1,)), ((), ()))
TN = (((0,), (0,)), ((), ()))


def vmem():
    return pl.BlockSpec(memory_space=pltpu.VMEM)


def smem():
    return pl.BlockSpec(memory_space=pltpu.SMEM)


def hbm():
    return pl.BlockSpec(memory_space=pltpu.HBM)


def in_hbm(x):
    return pltpu.with_memory_space_constraint(x, pltpu.HBM)


def anywhere():
    return pl.BlockSpec(memory_space=pl.ANY)


def round_up(x, m):
    return (x + m - 1) // m * m


def split2(x):
    high = x.astype(BF)
    return high, (x - high.astype(F32)).astype(BF)


def split3(x):
    high = x.astype(BF).astype(F32)
    rest = x - high
    middle = rest.astype(BF).astype(F32)
    return high, middle, rest - middle


def sketch_kernel(
    me_ref, st_hbm, keys_hbm, keep_ref, send_ref, st_ref, keys_ref, acc_ref, st_sem, sem, *, scale, chunk
):
    seq_len = keys_ref.shape[0]
    rank = st_ref.shape[0]
    half = rank // 2
    n = seq_len // chunk
    st_copy = pltpu.make_async_copy(st_hbm, st_ref, st_sem)
    st_copy.start()
    copies = [
        pltpu.make_async_copy(
            keys_hbm.at[pl.ds(i * chunk, chunk)], keys_ref.at[pl.ds(i * chunk, chunk)], sem.at[i]
        )
        for i in range(n)
    ]
    for c in copies[:AHEAD]:
        c.start()
    st_copy.wait()
    st = st_ref[...].astype(BF)

    def rows(i):
        return keys_ref[i * chunk:(i + 1) * chunk, :]

    def first(i):
        return lax.dot_general(st, rows(i), NT, preferred_element_type=F32).astype(BF)

    def second(i, y):
        return jnp.dot(y, rows(i), preferred_element_type=F32)

    def arrive(i):
        copies[i].wait()
        if i + AHEAD < n:
            copies[i + AHEAD].start()

    arrive(0)
    y = first(0)
    for i in range(1, n):
        arrive(i)
        y_next = first(i)
        z = second(i - 1, y)
        if i == 1:
            acc_ref[...] = z
        else:
            acc_ref[...] += z
        y = y_next
    acc_ref[...] = (acc_ref[...] + second(n - 1, y)) * scale
    core = me_ref[0] % 2
    keep_ref[...] = acc_ref[pl.ds(pl.multiple_of(core * half, 8), half), :]
    send_ref[...] = acc_ref[pl.ds(pl.multiple_of((1 - core) * half, 8), half), :]


def sketch_share(me, sketch_t, cache_keys, length):
    seq_len, width = cache_keys.shape
    rank = sketch_t.shape[0]
    chunk = min(512, seq_len)
    half = jax.ShapeDtypeStruct((rank // 2, width), F32)
    return pl.pallas_call(
        functools.partial(sketch_kernel, scale=1.0 / length, chunk=chunk),
        in_specs=[smem(), hbm(), hbm()],
        out_specs=[vmem(), vmem()],
        out_shape=[half, half],
        scratch_shapes=[
            pltpu.VMEM((rank, width), F32),
            pltpu.VMEM((seq_len, width), BF),
            pltpu.VMEM((rank, width), F32),
            pltpu.SemaphoreType.DMA,
            pltpu.SemaphoreType.DMA((seq_len // chunk,)),
        ],
        compiler_params=pltpu.CompilerParams(vmem_limit_bytes=24 << 20),
        name="sketch_share",
    )(me, in_hbm(sketch_t), in_hbm(cache_keys))


def slots_kernel(me_ref, chosen_ref, counts_ref, outl_ref, after_ref, slots_ref, live_ref, tie_ref, *, most, spans, steps):
    me = me_ref[0]
    base = me * spans
    tie_ref[...] = jnp.zeros_like(tie_ref)

    n_out = outl_ref.shape[0]
    o_first = jnp.int32(0)
    o_here = jnp.int32(0)
    for i in range(n_out):
        s = outl_ref[i]
        o_first = o_first + (s < base).astype(jnp.int32)
        o_here = o_here + ((s >= base) & (s < base + spans)).astype(jnp.int32)
    n_at = KVH * (steps + 1)
    live_ref[n_at] = jnp.minimum(o_here, OMOST)
    live_ref[n_at + 1] = me
    for j in range(OMOST):
        live_ref[n_at + 2 + j] = jnp.clip(outl_ref[jnp.minimum(o_first + j, n_out - 1)] - base, 0, spans - 1)

    sel = chosen_ref.shape[1]
    shards = counts_ref.shape[1]
    for g in range(KVH):
        at = jnp.int32(0)
        for t in range(steps):
            i = t * KVH + g
            start = jnp.int32(0)
            for r in range(shards):
                start = start + jnp.where(r < me, counts_ref[i, r], 0)
            count = jnp.minimum(counts_ref[i, me], most)
            live_ref[g * (steps + 1) + t] = at

            def put(k, _, i=i, start=start, at=at, g=g):
                for j in range(PART):
                    slot = k * PART + j
                    picked = chosen_ref[i, jnp.minimum(start + slot, sel - 1)]
                    slots_ref[g, at + slot] = jnp.clip(picked - base, 0, spans - 1)
                return 0

            lax.fori_loop(0, (count + PART - 1) // PART, put, 0)
            at = at + count
        live_ref[g * (steps + 1) + steps] = at
        for j in range(PART):
            slots_ref[g, at + j] = 0


def known_kernel(
    live_ref, q_ref, fk_ref, ca_ref, sa_ref, cb_ref, sb_ref, cq_ref, sq_ref, keys_hbm, after_ref,
    kx_ref, w_ref, tie_ref,
    okeys_ref, xtmp_ref, qtmp_ref, osem, *, per_device, rp
):
    steps = q_ref.shape[0]
    tie_ref[...] = jnp.zeros_like(tie_ref)
    n_at = KVH * (steps + 1)
    o_span = [live_ref[n_at + 2 + j] for j in range(OMOST)]
    o_copies = [
        pltpu.make_async_copy(
            keys_hbm.at[pl.ds(pl.multiple_of(o_span[j] // 2 * 16, 16), 16)], okeys_ref.at[j], osem.at[j]
        )
        for j in range(OMOST)
    ]
    for c in o_copies:
        c.start()

    lane = lax.broadcasted_iota(jnp.int32, (8, LANES), 1)
    sign = jnp.where(lane < HD // 2, -1.0, 1.0)

    qtmp_ref[...] = jnp.zeros_like(qtmp_ref)
    for t in range(steps):
        x = q_ref[t:t + 1, :].astype(F32)
        for h in range(QH):
            r = h // per_device * rp + t * per_device + h % per_device
            qtmp_ref[r:r + 1, :] = x[:, h * HD:(h + 1) * HD]
    scale = 1.0 / (HD ** 0.5)
    row = lax.broadcasted_iota(jnp.int32, (LANES, LANES), 0) % rp
    lane_r = lax.broadcasted_iota(jnp.int32, (LANES, LANES), 1)
    cq = jnp.zeros((LANES, LANES), F32)
    sq = jnp.zeros((LANES, LANES), F32)
    for t in range(steps):
        here = (row >= t * per_device) & (row < (t + 1) * per_device)
        cq = jnp.where(here, cq_ref[t:t + 1, :] * scale, cq)
        sq = jnp.where(here, sq_ref[t:t + 1, :] * scale, sq)
    sq = jnp.where(lane_r < HD // 2, -sq, sq)
    for pk in range(w_ref.shape[0]):
        x = qtmp_ref[pk * LANES:(pk + 1) * LANES, :]
        x = x * cq + pltpu.roll(x, HD // 2, 1) * sq
        z = jnp.where(lane_r < HD // 2, 1.0, -1.0) * pltpu.roll(x, HD // 2, 1)
        hi, lo = split2(jnp.concatenate([x.T, z.T], 0))
        w_ref[pk] = jnp.concatenate([hi, lo], 0)

    blk = cb_ref.shape[0] // SPAN
    turns = []
    for j in range(OMOST):
        a = o_span[j] // blk
        b = pl.ds(pl.multiple_of(o_span[j] % blk * SPAN, SPAN), SPAN)
        ca, sa = ca_ref[pl.ds(a, 1), :], sa_ref[pl.ds(a, 1), :]
        cb, sb = cb_ref[b, :], sb_ref[b, :]
        turns.append((ca * cb - sa * sb, (sa * cb + ca * sb) * sign))
    for c in o_copies:
        c.wait()
    x_rows = kx_ref.shape[1]
    xtmp_ref[...] = jnp.zeros_like(xtmp_ref)
    fs = sq_ref[:steps, :] * sign[:1]
    for g in range(KVH):
        sl = slice(g * HD, (g + 1) * HD)
        for j in range(OMOST):
            wide = okeys_ref[j, :, sl].astype(F32)
            x = jnp.where(o_span[j] % 2 == 0, wide[:8], wide[8:])
            xtmp_ref[j * SPAN:(j + 1) * SPAN, :] = x * turns[j][0] + pltpu.roll(x, HD // 2, 1) * turns[j][1]
        x = fk_ref[:, sl].astype(F32)
        o = OMOST * SPAN
        xtmp_ref[o:o + steps, :] = x * cq_ref[:steps, :] + pltpu.roll(x, HD // 2, 1) * fs
        kx_ref[g, :, :HD] = xtmp_ref[...].astype(BF)
        kx_ref[g, :, HD:] = jnp.zeros((x_rows, HD), BF)


def values_kernel(
    slots_ref, live_ref, fv_ref, values_hbm, after_ref, vg_ref, tie_ref, values_ref, vtmp_ref, sem, *, main
):
    steps = fv_ref.shape[0]
    rows_all = vtmp_ref.shape[0]
    copies = [
        pltpu.make_async_copy(values_hbm.at[:, pl.ds(g * HD, HD)], values_ref.at[g], sem.at[g]) for g in range(KVH)
    ]
    for c in copies[:AHEAD]:
        c.start()
    tie_ref[...] = jnp.zeros_like(tie_ref)
    vtmp_ref[...] = jnp.zeros_like(vtmp_ref)
    n_at = KVH * (steps + 1)

    for g in range(KVH):
        def rows_of(span, g=g):
            wide = values_ref[g, pl.ds(pl.multiple_of(span // 2 * 16, 16), 16), :].astype(F32)
            return jnp.where(span % 2 == 0, wide[:8], wide[8:])

        copies[g].wait()
        if g + AHEAD < KVH:
            copies[g + AHEAD].start()
        for j in range(OMOST):
            vtmp_ref[j * SPAN:(j + 1) * SPAN, :] = rows_of(live_ref[n_at + 2 + j])
        vtmp_ref[OMOST * SPAN:OMOST * SPAN + steps, :] = fv_ref[:, g * HD:(g + 1) * HD].astype(F32)
        count = live_ref[g * (steps + 1) + steps]

        def put(k, _, g=g, rows_of=rows_of):
            for j in range(PART):
                o = pl.multiple_of(LANES + (k * PART + j) * SPAN, SPAN)
                vtmp_ref[pl.ds(o, SPAN), :] = rows_of(slots_ref[g, k * PART + j])
            return 0

        lax.fori_loop(0, (count + PART - 1) // PART, put, 0)
        vg_ref[g, :LANES + main, :] = vtmp_ref[:LANES + main, :].astype(BF)
        if LANES + main < rows_all:
            def more(k, _, g=g):
                at = pl.ds(pl.multiple_of(LANES + main + k * LANES, LANES), LANES)
                vg_ref[g, at, :] = vtmp_ref[at, :].astype(BF)
                return 0

            lax.fori_loop(0, (jnp.maximum(count * SPAN - main, 0) + LANES - 1) // LANES, more, 0)


def attend_kernel(
    core_ref, slots_ref, live_ref, zmine_ref, zother_ref, kx_ref, w_ref, vg_ref, ca_ref, sa_ref, cb_ref, sb_ref,
    keys_hbm,
    kft_hbm, out_ref,
    keys_ref, z_ref, a_ref, qt_ref, kf_ref, kft_ref, kg_ref, cg_ref, sg_ref, sc_ref,
    sem, out_sem, *, per_device, steps, main, stop=9
):
    rank, width = z_ref.shape
    half = rank // 2
    seq_len = keys_ref.shape[0]
    load = pltpu.make_async_copy(keys_hbm, keys_ref, sem)
    load.start()

    core = core_ref[0] % 2
    z_ref[pl.ds(pl.multiple_of(core * half, 16), half), :] = zmine_ref[...]
    z_ref[pl.ds(pl.multiple_of((1 - core) * half, 16), half), :] = zother_ref[...]
    basis(z_ref, a_ref, qt_ref)
    qt = qt_ref[...]

    load.wait()
    if stop == 1:
        return
    chunk = seq_len // KVH
    for i in range(KVH):
        rows = slice(i * chunk, (i + 1) * chunk)
        kf = lax.dot_general(keys_ref[rows, :], qt, NT, preferred_element_type=F32)
        kf_ref[rows, :] = kf
        kft_ref[:, rows] = kf.T
    store = pltpu.make_async_copy(kft_ref, kft_hbm, out_sem)
    store.start()
    if stop == 2:
        store.wait()
        return

    blk = cb_ref.shape[0] // SPAN
    totals = [live_ref[g * (steps + 1) + steps] for g in range(KVH)]
    for g in range(KVH):
        def gather(k, _, g=g):
            for j in range(PART):
                slot = k * PART + j
                span = slots_ref[g, slot]
                src = pl.ds(pl.multiple_of(span * SPAN, SPAN), SPAN)
                dst = pl.ds(pl.multiple_of(slot * SPAN, SPAN), SPAN)
                kg_ref[g, dst, :] = kf_ref[src, :]
                a = span // blk
                b = pl.ds(pl.multiple_of(span % blk * SPAN, SPAN), SPAN)
                ca, sa = ca_ref[pl.ds(a, 1), :], sa_ref[pl.ds(a, 1), :]
                cb, sb = cb_ref[b, :], sb_ref[b, :]
                cg_ref[g, dst, :] = ca * cb - sa * sb
                sg_ref[g, dst, :] = sa * cb + ca * sb
            return 0

        lax.fori_loop(0, (totals[g] + PART - 1) // PART, gather, 0)
    if stop == 3:
        store.wait()
        return

    n_dest, rp, _ = out_ref.shape
    dests = n_dest // KVH
    qr = dests * rp
    heads = LANES // qr
    packs = w_ref.shape[0]
    n_at = KVH * (steps + 1)
    o_live = live_ref[n_at] * SPAN
    first_shard = live_ref[n_at + 1] == 0
    column = lax.broadcasted_iota(jnp.int32, (8, LANES), 1)[:1]
    col_head = column // qr
    col_row = column % rp
    col_step = col_row // per_device

    def bounds(pk, h):
        first = jnp.full((1, LANES), 1 << 30, jnp.int32)
        last = jnp.zeros((1, LANES), jnp.int32)
        for t in range(steps):
            at = (pk * heads + h) * (steps + 1) + t
            here = (col_head == h) & (col_step == t)
            first = jnp.where(here, live_ref[at] * SPAN, first)
            last = jnp.where(here, live_ref[at + 1] * SPAN, last)
        return first, last

    def product(pk, y):
        return jnp.dot(jnp.concatenate([y, y], 1), w_ref[pk], preferred_element_type=F32)

    token = lax.broadcasted_iota(jnp.int32, (LANES, LANES), 0)

    def slot_scores(pk, at, limits):
        s = jnp.full((LANES, LANES), DEAD, F32)
        rows = pl.ds(at, LANES)
        for h in range(heads):
            g = pk * heads + h
            x = jnp.dot(kg_ref[g, rows, :].astype(BF), qt_ref[:, g * HD:(g + 1) * HD], preferred_element_type=F32)
            y = jnp.concatenate([(x * cg_ref[g, rows, :]).astype(BF), (x * sg_ref[g, rows, :]).astype(BF)], 1)
            first, last = limits[h]
            here = token + at
            s = jnp.where((here >= first) & (here < last), product(pk, y), s)
        return s

    def known_scores(pk):
        s = jnp.full((LANES, LANES), DEAD, F32)
        new = token - OMOST * SPAN
        is_live = (token < o_live) | (first_shard & (new >= 0) & (new <= col_step))
        is_live = is_live & (new < steps) & (col_row < steps * per_device)
        for h in range(heads):
            s = jnp.where(is_live & (col_head == h), product(pk, kx_ref[pk * heads + h]), s)
        return s

    limits = [[bounds(pk, h) for h in range(heads)] for pk in range(packs)]
    extra = kg_ref.shape[1] - main
    blocks = []
    for pk in range(packs):
        most = functools.reduce(jnp.maximum, totals[pk * heads:(pk + 1) * heads])
        blocks.append((jnp.maximum(most * SPAN - main, 0) + LANES - 1) // LANES)

    tops = []
    for pk in range(packs):
        s = known_scores(pk)
        sc_ref[pk, :LANES, :] = s
        top = s
        for at in range(0, main, LANES):
            s = slot_scores(pk, at, limits[pk])
            sc_ref[pk, LANES + at:2 * LANES + at, :] = s
            top = jnp.maximum(top, s)
        tops.append(jnp.max(top, axis=0, keepdims=True))
    if extra > 0:
        for pk in range(packs):
            def more(k, top, pk=pk):
                at = pl.multiple_of(main + k * LANES, LANES)
                s = slot_scores(pk, at, limits[pk])
                sc_ref[pk, pl.ds(pl.multiple_of(LANES + at, LANES), LANES), :] = s
                return jnp.maximum(top, jnp.max(s, axis=0, keepdims=True))

            tops[pk] = lax.fori_loop(0, blocks[pk], more, tops[pk])
    if stop == 4:
        store.wait()
        return

    used = steps * per_device

    def weights(s, top):
        return jnp.where(s > 0.5 * DEAD, jnp.exp(s - top), 0.0)

    def weighted(pt, h, values):
        hi, lo = split2(pt[h * qr:(h + 1) * qr, :])
        r = jnp.dot(jnp.concatenate([hi, lo], 0), values, preferred_element_type=F32)
        return r[:qr] + r[qr:]

    sums = []
    for pk in range(packs):
        pts = []
        total = jnp.zeros((LANES, LANES), F32)
        for at in range(0, LANES + main, LANES):
            p = weights(sc_ref[pk, at:at + LANES, :], tops[pk])
            total = total + p
            pts.append(p.T)
        sums.append(jnp.sum(total, axis=0, keepdims=True))
        pt = jnp.concatenate(pts, 1)
        for h in range(heads):
            g = pk * heads + h
            acc = weighted(pt, h, vg_ref[g, :LANES + main, :])
            for a in range(dests):
                out_ref[g * dests + a] = acc[a * rp:(a + 1) * rp]
    if extra > 0:
        for pk in range(packs):
            def add(k, total, pk=pk):
                at = pl.multiple_of(LANES + main + k * LANES, LANES)
                p = weights(sc_ref[pk, pl.ds(at, LANES), :], tops[pk])
                pt = p.T
                for h in range(heads):
                    g = pk * heads + h

                    @pl.when(totals[g] * SPAN > main + k * LANES)
                    def _():
                        acc = weighted(pt, h, vg_ref[g, pl.ds(at, LANES), :])
                        for a in range(dests):
                            out_ref[g * dests + a] += acc[a * rp:(a + 1) * rp]

                return total + jnp.sum(p, axis=0, keepdims=True)

            sums[pk] = lax.fori_loop(0, blocks[pk], add, sums[pk])
    for d in range(n_dest):
        pk = d // (heads * dests)
        out_ref[d, used:used + 1, :] = tops[pk]
        out_ref[d, used + 1:used + 2, :] = sums[pk]
    store.wait()


def basis(z_ref, a_ref, qt_ref):
    rank = z_ref.shape[0]
    wide = round_up(rank, LANES)
    z = z_ref[...]
    c = lax.dot_general(z, z, NT, preferred_element_type=F32)
    rows = lax.broadcasted_iota(jnp.int32, (rank, wide), 0)
    cols = lax.broadcasted_iota(jnp.int32, (rank, wide), 1)
    a_ref[:, :wide] = jnp.where(rows == cols, 1.0, 0.0)
    a_ref[:, wide:wide + rank] = c
    a_ref[:, wide + rank:] = jnp.zeros((rank, wide - rank), F32)
    nb = 32
    half_tiles = wide // LANES
    for j0 in range(0, rank, nb):
        tiles = [t for t in range(half_tiles) if t * LANES < j0 + nb]
        tiles += [half_tiles + t for t in range(half_tiles) if (t + 1) * LANES > j0]
        part = {t: a_ref[j0:j0 + nb, t * LANES:(t + 1) * LANES] for t in tiles}
        row = lax.broadcasted_iota(jnp.int32, (nb, LANES), 0)
        column = []
        for j in range(nb):
            t, o = divmod(j0 + j, LANES)
            column.append(jnp.broadcast_to(part[half_tiles + t][:, o:o + 1], (nb, LANES)))
        for j in range(nb):
            inverse = lax.rsqrt(jnp.broadcast_to(column[j][j:j + 1, :], (nb, LANES)))
            low = jnp.where(row > j, column[j] * inverse, 0.0)
            for k in range(j + 1, nb):
                column[k] = column[k] - low * jnp.broadcast_to(low[k:k + 1, :], (nb, LANES))
            for t in tiles:
                upper = jnp.broadcast_to(part[t][j:j + 1, :], (nb, LANES)) * inverse
                part[t] = jnp.where(row == j, upper, part[t] - low * upper)
        for t in tiles:
            a_ref[j0:j0 + nb, t * LANES:(t + 1) * LANES] = part[t]
        if j0 + nb < rank:
            upper = jnp.concatenate(
                [part[t] if t in part else jnp.zeros((nb, LANES), F32) for t in range(2 * half_tiles)], 1
            )
            h, m, l = split3(upper)
            left = jnp.concatenate([h, h, m, m, h, l], 0)[:, wide:].astype(BF)
            right = jnp.concatenate([h, m, h, m, l, h], 0).astype(BF)
            for s in range(2):
                d = lax.dot_general(left, right[:, s * wide:(s + 1) * wide], TN, preferred_element_type=F32)
                a_ref[j0 + nb:, s * wide:(s + 1) * wide] -= d[j0 + nb:rank]
    h, m, _ = split3(a_ref[:, :rank])
    q = jnp.dot(jnp.concatenate([h, m], 0).astype(BF), z, preferred_element_type=F32)
    qt_ref[...] = (q[:rank] + q[rank:]).astype(BF)


def attend_call(
    me, slots, live, z, z_other, kx, w, vg, ca, sa, cb, sb, cache_keys,
    *, steps, per_device, main, rp, n_dest, stop=9
):
    seq_len, width = cache_keys.shape
    rank = 2 * z.shape[0]
    tok_all = vg.shape[1] - LANES
    return pl.pallas_call(
        functools.partial(attend_kernel, per_device=per_device, steps=steps, main=main, stop=stop),
        in_specs=[smem()] * 3 + [vmem()] * 9 + [hbm()],
        out_specs=[hbm(), vmem()],
        out_shape=[
            jax.ShapeDtypeStruct((rank, seq_len), F32),
            jax.ShapeDtypeStruct((n_dest, rp, HD), F32),
        ],
        scratch_shapes=[
            pltpu.VMEM((seq_len, width), BF),
            pltpu.VMEM((rank, width), BF),
            pltpu.VMEM((rank, 2 * round_up(rank, LANES)), F32),
            pltpu.VMEM((rank, width), BF),
            pltpu.VMEM((seq_len, rank), F32),
            pltpu.VMEM((rank, seq_len), F32),
            pltpu.VMEM((KVH, tok_all, rank), F32),
            pltpu.VMEM((KVH, tok_all, HD), F32),
            pltpu.VMEM((KVH, tok_all, HD), F32),
            pltpu.VMEM((w.shape[0], LANES + tok_all, LANES), F32),
            pltpu.SemaphoreType.DMA,
            pltpu.SemaphoreType.DMA,
        ],
        compiler_params=pltpu.CompilerParams(vmem_limit_bytes=42 << 20),
        name="attend",
    )(me, slots, live, z, z_other, kx, w, vg, ca, sa, cb, sb, in_hbm(cache_keys))


def merge_kernel(me_ref, parts_ref, out_ref, *, steps, per_device):
    n, rp, _ = parts_ref.shape
    used = steps * per_device
    shift = me_ref[0] % (LANES // rp) * rp
    eye = lax.broadcasted_iota(jnp.int32, (rp, LANES), 0) + shift == lax.broadcasted_iota(jnp.int32, (rp, LANES), 1)

    def column(s, r):
        return jnp.sum(jnp.where(eye, parts_ref[s, r:r + 1, :], 0.0), axis=1, keepdims=True)

    ms = [column(s, used) for s in range(n)]
    top = functools.reduce(jnp.maximum, ms)
    total = jnp.zeros((rp, 1), F32)
    acc = jnp.zeros((rp, HD), F32)
    for s in range(n):
        w = jnp.exp(ms[s] - top)
        total = total + w * column(s, used + 1)
        acc = acc + w * parts_ref[s]
    o = acc / total
    for t in range(steps):
        for i in range(per_device):
            r = t * per_device + i
            out_ref[t:t + 1, i * HD:(i + 1) * HD] = o[r:r + 1, :].astype(BF)


def swap(x, moves):
    return lax.ppermute(x, "seq", moves)


def on_device(
    cache_keys,
    cache_values,
    sketch_matrix,
    queries,
    fresh_keys,
    fresh_values,
    chosen,
    shard_counts,
    outliers,
):
    seq_len, width = cache_keys.shape
    devices = lax.axis_size("seq")
    myself = lax.axis_index("seq")
    length = seq_len * devices
    steps = queries.shape[0]
    rank = sketch_matrix.shape[1]
    per_device = QH // devices
    n_lists = steps * KVH
    most = 3 * chosen.shape[2] // devices
    slots_all = round_up(steps * most, LANES // SPAN)
    tok_all = slots_all * SPAN
    main = min(MAIN, tok_all)
    used = steps * per_device
    rp = round_up(used + 2, 8)
    n_dest = devices
    me = jnp.full((1,), myself, jnp.int32)

    keep, send = sketch_share(me, sketch_matrix.T, cache_keys, length)

    half_width = HD // 2
    exponents = jnp.arange(half_width, dtype=F32) * (2.0 / HD)
    inverse_freq = jnp.exp(-jnp.log(F32(500000.0)) * exponents)
    inverse_freq = jnp.concatenate([inverse_freq, inverse_freq])
    blk = 64
    coarse = (myself * seq_len + blk * jnp.arange(seq_len // blk, dtype=jnp.int32)).astype(F32)[:, None] * inverse_freq
    fine = jnp.arange(blk, dtype=jnp.int32).astype(F32)[:, None] * inverse_freq
    late = (length + jnp.arange(steps, dtype=jnp.int32)).astype(F32)[:, None] * inverse_freq
    turns = (jnp.cos(coarse), jnp.sin(coarse), jnp.cos(fine), jnp.sin(fine))

    tie_shape = jax.ShapeDtypeStruct((1, LANES), F32)

    def find_slots(after):
        return pl.pallas_call(
            functools.partial(slots_kernel, most=most, spans=seq_len // SPAN, steps=steps),
            in_specs=[smem()] * 4 + [anywhere()],
            out_specs=[smem()] * 2 + [vmem()],
            out_shape=[
                jax.ShapeDtypeStruct((KVH, slots_all + 2 * PART), jnp.int32),
                jax.ShapeDtypeStruct((KVH * (steps + 1) + 2 + OMOST,), jnp.int32),
                tie_shape,
            ],
            name="find_slots",
        )(me, chosen.reshape(n_lists, -1), shard_counts.reshape(n_lists, -1), outliers, after)

    def known(live, after):
        return pl.pallas_call(
            functools.partial(known_kernel, per_device=per_device, rp=rp),
            in_specs=[smem()] + [vmem()] * 8 + [hbm(), anywhere()],
            out_specs=[vmem()] * 3,
            out_shape=[
                jax.ShapeDtypeStruct((KVH, LANES, 2 * HD), BF),
                jax.ShapeDtypeStruct((n_dest * rp // LANES, 4 * HD, LANES), BF),
                tie_shape,
            ],
            scratch_shapes=[
                pltpu.VMEM((OMOST, 16, width), BF),
                pltpu.VMEM((LANES, HD), F32),
                pltpu.VMEM((n_dest * rp, HD), F32),
                pltpu.SemaphoreType.DMA((OMOST,)),
            ],
            compiler_params=pltpu.CompilerParams(vmem_limit_bytes=8 << 20),
            name="known_keys",
        )(live, queries, fresh_keys, *turns, jnp.cos(late), jnp.sin(late), in_hbm(cache_keys), after)

    def slot_values(slots, live, after):
        return pl.pallas_call(
            functools.partial(values_kernel, main=main),
            in_specs=[smem()] * 2 + [vmem(), hbm(), anywhere()],
            out_specs=[vmem()] * 2,
            out_shape=[jax.ShapeDtypeStruct((KVH, LANES + tok_all, HD), BF), tie_shape],
            scratch_shapes=[
                pltpu.VMEM((KVH, seq_len, HD), BF),
                pltpu.VMEM((LANES + tok_all, HD), F32),
                pltpu.SemaphoreType.DMA((KVH,)),
            ],
            compiler_params=pltpu.CompilerParams(vmem_limit_bytes=16 << 20),
            name="slot_values",
        )(slots, live, fresh_values, in_hbm(cache_values), after)

    z = keep + swap(send, [(i, i ^ 1) for i in range(devices)])
    hops = [1 << k for k in range(1, devices.bit_length() - 1)]
    for k in range(len(hops)):
        other = k ^ 1 if k < 2 and len(hops) >= 2 else k
        moves = [(i, i ^ hops[k if i % 2 == 0 else other]) for i in range(devices)]
        going = z.astype(BF)
        came = swap(going, moves).astype(F32)
        if k == 0:
            slots, live, tie = find_slots(going)
            came = came + tie[0, 0]
        if k == min(1, len(hops) - 1):
            kx, w, tie = known(live, going)
            came = came + tie[0, 0]
        if k == len(hops) - 1:
            vg, tie = slot_values(slots, live, going)
            came = came + tie[0, 0]
        z = z + came
    z = z.astype(BF)
    z_other = swap(z, [(i, i ^ 1) for i in range(devices)])

    kft, parts = attend_call(
        me, slots, live, z, z_other, kx, w, vg, *turns, cache_keys,
        steps=steps, per_device=per_device, main=main, rp=rp, n_dest=n_dest,
    )
    parts = lax.all_to_all(parts, "seq", 0, 0, tiled=True)
    attended = pl.pallas_call(
        functools.partial(merge_kernel, steps=steps, per_device=per_device),
        in_specs=[smem(), vmem()],
        out_specs=vmem(),
        out_shape=jax.ShapeDtypeStruct((steps, per_device * HD), BF),
        name="merge",
    )(me, parts)
    return (attended, kft.T)


def solution(mesh):
    in_specs = (
        P(("groups", "seq"), None),
        P(("groups", "seq"), None),
        P(),
        P("groups", None),
        P("groups", None),
        P("groups", None),
        P("groups", None, None),
        P("groups", None, None),
        P("groups"),
    )
    out_specs = (P("groups", "seq"), P(("groups", "seq"), None))
    return jax.shard_map(
        on_device, mesh=mesh, in_specs=in_specs, out_specs=out_specs, check_vma=False
    )
```

```python
import functools

import jax
import jax.numpy as jnp
from jax import lax
from jax.experimental import pallas as pl
from jax.experimental.pallas import tpu as pltpu
from jax.sharding import PartitionSpec as P

KVH = 8
HD = 128
QH = 64
SPAN = 8
OMOST = 4
BF = jnp.bfloat16
F32 = jnp.float32
DEAD = -1e30
LANES = 128
MAIN = 640
PART = 8
STRAIGHT = 6
AHEAD = 3
NT = (((1,), (1,)), ((), ()))
TN = (((0,), (0,)), ((), ()))


def vmem():
    return pl.BlockSpec(memory_space=pltpu.VMEM)


def smem():
    return pl.BlockSpec(memory_space=pltpu.SMEM)


def hbm():
    return pl.BlockSpec(memory_space=pltpu.HBM)


def in_hbm(x):
    return pltpu.with_memory_space_constraint(x, pltpu.HBM)


def anywhere():
    return pl.BlockSpec(memory_space=pl.ANY)


def round_up(x, m):
    return (x + m - 1) // m * m


def split2(x):
    high = x.astype(BF)
    return high, (x - high.astype(F32)).astype(BF)


def split3(x):
    high = x.astype(BF).astype(F32)
    rest = x - high
    middle = rest.astype(BF).astype(F32)
    return high, middle, rest - middle


def sketch_kernel(
    me_ref, st_hbm, keys_hbm, keep_ref, send_ref, st_ref, keys_ref, acc_ref, st_sem, sem, *, scale, chunk
):
    seq_len = keys_ref.shape[0]
    rank = st_ref.shape[0]
    half = rank // 2
    n = seq_len // chunk
    st_copy = pltpu.make_async_copy(st_hbm, st_ref, st_sem)
    st_copy.start()
    copies = [
        pltpu.make_async_copy(
            keys_hbm.at[pl.ds(i * chunk, chunk)], keys_ref.at[pl.ds(i * chunk, chunk)], sem.at[i]
        )
        for i in range(n)
    ]
    for c in copies[:AHEAD]:
        c.start()
    st_copy.wait()
    st = st_ref[...].astype(BF)

    def rows(i):
        return keys_ref[i * chunk:(i + 1) * chunk, :]

    def first(i):
        return lax.dot_general(st, rows(i), NT, preferred_element_type=F32).astype(BF)

    def second(i, y):
        return jnp.dot(y, rows(i), preferred_element_type=F32)

    def arrive(i):
        copies[i].wait()
        if i + AHEAD < n:
            copies[i + AHEAD].start()

    arrive(0)
    y = first(0)
    for i in range(1, n):
        arrive(i)
        y_next = first(i)
        z = second(i - 1, y)
        if i == 1:
            acc_ref[...] = z
        else:
            acc_ref[...] += z
        y = y_next
    acc_ref[...] = (acc_ref[...] + second(n - 1, y)) * scale
    core = me_ref[0] % 2
    keep_ref[...] = acc_ref[pl.ds(pl.multiple_of(core * half, 8), half), :]
    send_ref[...] = acc_ref[pl.ds(pl.multiple_of((1 - core) * half, 8), half), :]


def sketch_share(me, sketch_t, cache_keys, length):
    seq_len, width = cache_keys.shape
    rank = sketch_t.shape[0]
    chunk = min(512, seq_len)
    half = jax.ShapeDtypeStruct((rank // 2, width), F32)
    return pl.pallas_call(
        functools.partial(sketch_kernel, scale=1.0 / length, chunk=chunk),
        in_specs=[smem(), hbm(), hbm()],
        out_specs=[vmem(), vmem()],
        out_shape=[half, half],
        scratch_shapes=[
            pltpu.VMEM((rank, width), F32),
            pltpu.VMEM((seq_len, width), BF),
            pltpu.VMEM((rank, width), F32),
            pltpu.SemaphoreType.DMA,
            pltpu.SemaphoreType.DMA((seq_len // chunk,)),
        ],
        compiler_params=pltpu.CompilerParams(vmem_limit_bytes=24 << 20),
        name="sketch_share",
    )(me, in_hbm(sketch_t), in_hbm(cache_keys))


def slots_kernel(me_ref, chosen_ref, place_ref, outl_ref, after_ref, slots_ref, live_ref, tie_ref, *, most, spans, steps):
    me = me_ref[0]
    base = me * spans
    tie_ref[...] = jnp.zeros_like(tie_ref)

    n_out = outl_ref.shape[0]
    o_first = jnp.int32(0)
    o_here = jnp.int32(0)
    for i in range(n_out):
        s = outl_ref[i]
        o_first = o_first + (s < base).astype(jnp.int32)
        o_here = o_here + ((s >= base) & (s < base + spans)).astype(jnp.int32)
    n_at = KVH * (steps + 1)
    live_ref[n_at] = jnp.minimum(o_here, OMOST)
    live_ref[n_at + 1] = me
    for j in range(OMOST):
        live_ref[n_at + 2 + j] = jnp.clip(outl_ref[jnp.minimum(o_first + j, n_out - 1)] - base, 0, spans - 1)

    sel = chosen_ref.shape[1]
    n_lists = chosen_ref.shape[0]
    for g in range(KVH):
        at = jnp.int32(0)
        for t in range(steps):
            i = t * KVH + g
            start = place_ref[i]
            count = jnp.minimum(place_ref[n_lists + i], most)
            live_ref[g * (steps + 1) + t] = at

            def put(k, _, i=i, start=start, at=at, g=g):
                found = []
                for j in range(PART):
                    picked = chosen_ref[i, jnp.minimum(start + (k * PART + j), sel - 1)]
                    found.append(jnp.clip(picked - base, 0, spans - 1))
                for j in range(PART):
                    slots_ref[g, at + (k * PART + j)] = found[j]
                return 0

            put(0, 0)
            put(1, 0)
            lax.fori_loop(2, (count + PART - 1) // PART, put, 0)
            at = at + count
        live_ref[g * (steps + 1) + steps] = at
        for j in range(PART):
            slots_ref[g, at + j] = 0


def known_kernel(
    live_ref, q_ref, fk_ref, ca_ref, sa_ref, cb_ref, sb_ref, cq_ref, sq_ref, keys_hbm, after_ref,
    kx_ref, w_ref, tie_ref,
    okeys_ref, xtmp_ref, qtmp_ref, osem, *, per_device, rp
):
    steps = q_ref.shape[0]
    tie_ref[...] = jnp.zeros_like(tie_ref)
    n_at = KVH * (steps + 1)
    o_span = [live_ref[n_at + 2 + j] for j in range(OMOST)]
    o_copies = [
        pltpu.make_async_copy(
            keys_hbm.at[pl.ds(pl.multiple_of(o_span[j] // 2 * 16, 16), 16)], okeys_ref.at[j], osem.at[j]
        )
        for j in range(OMOST)
    ]
    for c in o_copies:
        c.start()

    lane = lax.broadcasted_iota(jnp.int32, (8, LANES), 1)
    sign = jnp.where(lane < HD // 2, -1.0, 1.0)

    qtmp_ref[...] = jnp.zeros_like(qtmp_ref)
    for t in range(steps):
        x = q_ref[t:t + 1, :].astype(F32)
        for h in range(QH):
            r = h // per_device * rp + t * per_device + h % per_device
            qtmp_ref[r:r + 1, :] = x[:, h * HD:(h + 1) * HD]
    scale = 1.0 / (HD ** 0.5)
    row = lax.broadcasted_iota(jnp.int32, (LANES, LANES), 0) % rp
    lane_r = lax.broadcasted_iota(jnp.int32, (LANES, LANES), 1)
    cq = jnp.zeros((LANES, LANES), F32)
    sq = jnp.zeros((LANES, LANES), F32)
    for t in range(steps):
        here = (row >= t * per_device) & (row < (t + 1) * per_device)
        cq = jnp.where(here, cq_ref[t:t + 1, :] * scale, cq)
        sq = jnp.where(here, sq_ref[t:t + 1, :] * scale, sq)
    sq = jnp.where(lane_r < HD // 2, -sq, sq)
    for pk in range(w_ref.shape[0]):
        x = qtmp_ref[pk * LANES:(pk + 1) * LANES, :]
        x = x * cq + pltpu.roll(x, HD // 2, 1) * sq
        z = jnp.where(lane_r < HD // 2, 1.0, -1.0) * pltpu.roll(x, HD // 2, 1)
        hi, lo = split2(jnp.concatenate([x.T, z.T], 0))
        w_ref[pk] = jnp.concatenate([hi, lo], 0)

    blk = cb_ref.shape[0] // SPAN
    turns = []
    for j in range(OMOST):
        a = o_span[j] // blk
        b = pl.ds(pl.multiple_of(o_span[j] % blk * SPAN, SPAN), SPAN)
        ca, sa = ca_ref[pl.ds(a, 1), :], sa_ref[pl.ds(a, 1), :]
        cb, sb = cb_ref[b, :], sb_ref[b, :]
        turns.append((ca * cb - sa * sb, (sa * cb + ca * sb) * sign))
    for c in o_copies:
        c.wait()
    x_rows = kx_ref.shape[1]
    xtmp_ref[...] = jnp.zeros_like(xtmp_ref)
    fs = sq_ref[:steps, :] * sign[:1]
    for g in range(KVH):
        sl = slice(g * HD, (g + 1) * HD)
        for j in range(OMOST):
            wide = okeys_ref[j, :, sl].astype(F32)
            x = jnp.where(o_span[j] % 2 == 0, wide[:8], wide[8:])
            xtmp_ref[j * SPAN:(j + 1) * SPAN, :] = x * turns[j][0] + pltpu.roll(x, HD // 2, 1) * turns[j][1]
        x = fk_ref[:, sl].astype(F32)
        o = OMOST * SPAN
        xtmp_ref[o:o + steps, :] = x * cq_ref[:steps, :] + pltpu.roll(x, HD // 2, 1) * fs
        kx_ref[g, :, :HD] = xtmp_ref[...].astype(BF)
        kx_ref[g, :, HD:] = jnp.zeros((x_rows, HD), BF)


def values_kernel(
    slots_ref, live_ref, fv_ref, values_hbm, after_ref, vg_ref, tie_ref, values_ref, vtmp_ref, sem, *, main
):
    steps = fv_ref.shape[0]
    rows_all = vtmp_ref.shape[0]
    spans = values_ref.shape[1] // SPAN
    copies = [
        pltpu.make_async_copy(values_hbm.at[:, pl.ds(g * HD, HD)], values_ref.at[g], sem.at[g]) for g in range(KVH)
    ]
    for c in copies[:AHEAD]:
        c.start()
    tie_ref[...] = jnp.zeros_like(tie_ref)
    vtmp_ref[...] = jnp.zeros_like(vtmp_ref)
    n_at = KVH * (steps + 1)

    for g in range(KVH):
        def rows_of(span, g=g):
            wide = values_ref[g, pl.ds(pl.multiple_of(span // 2 * 16, 16), 16), :].astype(F32)
            return jnp.where(span % 2 == 0, wide[:8], wide[8:])

        copies[g].wait()
        if g + AHEAD < KVH:
            copies[g + AHEAD].start()
        for j in range(OMOST):
            vtmp_ref[j * SPAN:(j + 1) * SPAN, :] = rows_of(live_ref[n_at + 2 + j])
        vtmp_ref[OMOST * SPAN:OMOST * SPAN + steps, :] = fv_ref[:, g * HD:(g + 1) * HD].astype(F32)
        count = live_ref[g * (steps + 1) + steps]

        def put(k, _, g=g, rows_of=rows_of):
            rows = [rows_of(jnp.clip(slots_ref[g, k * PART + j], 0, spans - 1)) for j in range(PART)]
            dst = pl.ds(pl.multiple_of(LANES + k * (PART * SPAN), PART * SPAN), PART * SPAN)
            vtmp_ref[dst, :] = jnp.concatenate(rows, 0)
            return 0

        straight = min(STRAIGHT, (rows_all - LANES) // (PART * SPAN))
        for k in range(straight):
            put(k, 0)
        lax.fori_loop(straight, (count + PART - 1) // PART, put, 0)
        vg_ref[g, :LANES + main, :] = vtmp_ref[:LANES + main, :].astype(BF)
        if LANES + main < rows_all:
            def more(k, _, g=g):
                at = pl.ds(pl.multiple_of(LANES + main + k * LANES, LANES), LANES)
                vg_ref[g, at, :] = vtmp_ref[at, :].astype(BF)
                return 0

            lax.fori_loop(0, (jnp.maximum(count * SPAN - main, 0) + LANES - 1) // LANES, more, 0)


def attend_kernel(
    core_ref, slots_ref, live_ref, zmine_ref, zother_ref, kx_ref, w_ref, vg_ref, ca_ref, sa_ref, cb_ref, sb_ref,
    keys_hbm,
    kft_hbm, out_ref,
    keys_ref, z_ref, a_ref, qt_ref, kf_ref, kft_ref, kg_ref, cg_ref, sg_ref, sc_ref, cc_ref, ss_ref,
    sem, out_sem, *, per_device, steps, main, stop=9
):
    rank, width = z_ref.shape
    half = rank // 2
    seq_len = keys_ref.shape[0]
    load = pltpu.make_async_copy(keys_hbm, keys_ref, sem)
    load.start()

    core = core_ref[0] % 2
    z_ref[pl.ds(pl.multiple_of(core * half, 16), half), :] = zmine_ref[...]
    z_ref[pl.ds(pl.multiple_of((1 - core) * half, 16), half), :] = zother_ref[...]
    turn_tables(ca_ref, sa_ref, cb_ref, sb_ref, cc_ref, ss_ref)
    basis(z_ref, a_ref, qt_ref)
    qt = qt_ref[...]

    load.wait()
    if stop == 1:
        return
    chunk = seq_len // KVH
    for i in range(KVH):
        rows = slice(i * chunk, (i + 1) * chunk)
        kf = lax.dot_general(keys_ref[rows, :], qt, NT, preferred_element_type=F32)
        kf_ref[rows, :] = kf
        kft_ref[:, rows] = kf.T
    store = pltpu.make_async_copy(kft_ref, kft_hbm, out_sem)
    store.start()
    if stop == 2:
        store.wait()
        return

    totals = [live_ref[g * (steps + 1) + steps] for g in range(KVH)]
    spans = seq_len // SPAN
    parts_all = kg_ref.shape[1] // (PART * SPAN)
    straight = min(STRAIGHT, parts_all)
    for g in range(KVH):
        def gather(k, _, g=g):
            got = []
            for j in range(PART):
                span = jnp.clip(slots_ref[g, k * PART + j], 0, spans - 1)
                src = pl.ds(pl.multiple_of(span * SPAN, SPAN), SPAN)
                got.append((kf_ref[src, :], cc_ref[src, :], ss_ref[src, :]))
            for ref, rows in zip((kg_ref, cg_ref, sg_ref), zip(*got)):
                dst = pl.ds(pl.multiple_of(k * (PART * SPAN), PART * SPAN), PART * SPAN)
                ref[g, dst, :] = jnp.concatenate(rows, 0).astype(ref.dtype)
            return 0

        for k in range(straight):
            gather(k, 0)
        lax.fori_loop(straight, (totals[g] + PART - 1) // PART, gather, 0)
    if stop == 3:
        store.wait()
        return

    n_dest, rp, _ = out_ref.shape
    dests = n_dest // KVH
    qr = dests * rp
    heads = LANES // qr
    packs = w_ref.shape[0]
    n_at = KVH * (steps + 1)
    o_live = live_ref[n_at] * SPAN
    first_shard = live_ref[n_at + 1] == 0
    column = lax.broadcasted_iota(jnp.int32, (8, LANES), 1)[:1]
    col_head = column // qr
    col_row = column % rp
    col_step = col_row // per_device

    def bounds(pk, h):
        first = jnp.full((1, LANES), 1 << 30, jnp.int32)
        last = jnp.zeros((1, LANES), jnp.int32)
        for t in range(steps):
            at = (pk * heads + h) * (steps + 1) + t
            here = (col_head == h) & (col_step == t)
            first = jnp.where(here, live_ref[at] * SPAN, first)
            last = jnp.where(here, live_ref[at + 1] * SPAN, last)
        return first, last

    def product(pk, y):
        r = jnp.dot(y, w_ref[pk, :2 * HD, :], preferred_element_type=F32)
        return r + jnp.dot(y, w_ref[pk, 2 * HD:, :], preferred_element_type=F32)

    token = lax.broadcasted_iota(jnp.int32, (LANES, LANES), 0)

    def slot_scores(pk, at, n, limits):
        rows = pl.ds(at, n)
        ys = []
        for h in range(heads):
            g = pk * heads + h
            x = jnp.dot(kg_ref[g, rows, :].astype(BF), qt_ref[:, g * HD:(g + 1) * HD], preferred_element_type=F32)
            ys.append(jnp.concatenate([(x * cg_ref[g, rows, :]).astype(BF), (x * sg_ref[g, rows, :]).astype(BF)], 1))
        r = product(pk, jnp.concatenate(ys, 0))
        s = jnp.full((n, LANES), DEAD, F32)
        here = lax.broadcasted_iota(jnp.int32, (n, LANES), 0) + at
        for h in range(heads):
            first, last = limits[h]
            s = jnp.where((here >= first) & (here < last), r[h * n:(h + 1) * n], s)
        return s

    def known_scores(pk):
        s = jnp.full((LANES, LANES), DEAD, F32)
        new = token - OMOST * SPAN
        is_live = (token < o_live) | (first_shard & (new >= 0) & (new <= col_step))
        is_live = is_live & (new < steps) & (col_row < steps * per_device)
        r = product(pk, kx_ref[pk * heads:(pk + 1) * heads].reshape(heads * LANES, 2 * HD))
        for h in range(heads):
            s = jnp.where(is_live & (col_head == h), r[h * LANES:(h + 1) * LANES], s)
        return s

    limits = [[bounds(pk, h) for h in range(heads)] for pk in range(packs)]
    extra = kg_ref.shape[1] - main
    blocks = []
    for pk in range(packs):
        most = functools.reduce(jnp.maximum, totals[pk * heads:(pk + 1) * heads])
        blocks.append((jnp.maximum(most * SPAN - main, 0) + LANES - 1) // LANES)

    tops = []
    for pk in range(packs):
        s = known_scores(pk)
        sc_ref[pk, :LANES, :] = s
        top = jnp.max(s, axis=0, keepdims=True)
        s = slot_scores(pk, 0, main, limits[pk])
        sc_ref[pk, LANES:LANES + main, :] = s
        tops.append(jnp.maximum(top, jnp.max(s, axis=0, keepdims=True)))
    if extra > 0:
        for pk in range(packs):
            def more(k, top, pk=pk):
                at = pl.multiple_of(main + k * LANES, LANES)
                s = slot_scores(pk, at, LANES, limits[pk])
                sc_ref[pk, pl.ds(pl.multiple_of(LANES + at, LANES), LANES), :] = s
                return jnp.maximum(top, jnp.max(s, axis=0, keepdims=True))

            tops[pk] = lax.fori_loop(0, blocks[pk], more, tops[pk])
    if stop == 4:
        store.wait()
        return

    used = steps * per_device

    def weights(s, top):
        return jnp.where(s > 0.5 * DEAD, jnp.exp(s - top), 0.0)

    def weighted(pt, h, values):
        hi, lo = split2(pt[h * qr:(h + 1) * qr, :])
        r = jnp.dot(jnp.concatenate([hi, lo], 0), values, preferred_element_type=F32)
        return r[:qr] + r[qr:]

    sums = []
    for pk in range(packs):
        pts = []
        total = jnp.zeros((LANES, LANES), F32)
        for at in range(0, LANES + main, LANES):
            p = weights(sc_ref[pk, at:at + LANES, :], tops[pk])
            total = total + p
            pts.append(p.T)
        sums.append(jnp.sum(total, axis=0, keepdims=True))
        pt = jnp.concatenate(pts, 1)
        for h in range(heads):
            g = pk * heads + h
            acc = weighted(pt, h, vg_ref[g, :LANES + main, :])
            for a in range(dests):
                out_ref[g * dests + a] = acc[a * rp:(a + 1) * rp]
    if extra > 0:
        for pk in range(packs):
            def add(k, total, pk=pk):
                at = pl.multiple_of(LANES + main + k * LANES, LANES)
                p = weights(sc_ref[pk, pl.ds(at, LANES), :], tops[pk])
                pt = p.T
                for h in range(heads):
                    g = pk * heads + h

                    @pl.when(totals[g] * SPAN > main + k * LANES)
                    def _():
                        acc = weighted(pt, h, vg_ref[g, pl.ds(at, LANES), :])
                        for a in range(dests):
                            out_ref[g * dests + a] += acc[a * rp:(a + 1) * rp]

                return total + jnp.sum(p, axis=0, keepdims=True)

            sums[pk] = lax.fori_loop(0, blocks[pk], add, sums[pk])
    for d in range(n_dest):
        pk = d // (heads * dests)
        out_ref[d, used:used + 1, :] = tops[pk]
        out_ref[d, used + 1:used + 2, :] = sums[pk]
    store.wait()


def turn_tables(ca_ref, sa_ref, cb_ref, sb_ref, cc_ref, ss_ref):
    blk = cb_ref.shape[0]
    cb = cb_ref[...]
    sb = sb_ref[...]
    for a in range(cc_ref.shape[0] // blk):
        ca = ca_ref[a:a + 1, :]
        sa = sa_ref[a:a + 1, :]
        cc_ref[a * blk:(a + 1) * blk, :] = ca * cb - sa * sb
        ss_ref[a * blk:(a + 1) * blk, :] = sa * cb + ca * sb


def basis(z_ref, a_ref, qt_ref):
    rank = z_ref.shape[0]
    wide = round_up(rank, LANES)
    z = z_ref[...]
    c = lax.dot_general(z, z, NT, preferred_element_type=F32)
    rows = lax.broadcasted_iota(jnp.int32, (rank, wide), 0)
    cols = lax.broadcasted_iota(jnp.int32, (rank, wide), 1)
    a_ref[:, :wide] = jnp.where(rows == cols, 1.0, 0.0)
    a_ref[:, wide:wide + rank] = c
    a_ref[:, wide + rank:] = jnp.zeros((rank, wide - rank), F32)
    nb = 32
    half_tiles = wide // LANES
    for j0 in range(0, rank, nb):
        tiles = [t for t in range(half_tiles) if t * LANES < j0 + nb]
        tiles += [half_tiles + t for t in range(half_tiles) if (t + 1) * LANES > j0]
        part = {t: a_ref[j0:j0 + nb, t * LANES:(t + 1) * LANES] for t in tiles}
        row = lax.broadcasted_iota(jnp.int32, (nb, LANES), 0)
        column = []
        for j in range(nb):
            t, o = divmod(j0 + j, LANES)
            column.append(jnp.broadcast_to(part[half_tiles + t][:, o:o + 1], (nb, LANES)))
        for j in range(nb):
            inverse = lax.rsqrt(jnp.broadcast_to(column[j][j:j + 1, :], (nb, LANES)))
            low = jnp.where(row > j, column[j] * inverse, 0.0)
            for k in range(j + 1, nb):
                column[k] = column[k] - low * jnp.broadcast_to(low[k:k + 1, :], (nb, LANES))
            for t in tiles:
                upper = jnp.broadcast_to(part[t][j:j + 1, :], (nb, LANES)) * inverse
                part[t] = jnp.where(row == j, upper, part[t] - low * upper)
        for t in tiles:
            a_ref[j0:j0 + nb, t * LANES:(t + 1) * LANES] = part[t]
        if j0 + nb < rank:
            upper = jnp.concatenate(
                [part[t] if t in part else jnp.zeros((nb, LANES), F32) for t in range(2 * half_tiles)], 1
            )
            h, m, l = split3(upper)
            left = jnp.concatenate([h, h, m, m, h, l], 0)[:, wide:].astype(BF)
            right = jnp.concatenate([h, m, h, m, l, h], 0).astype(BF)
            for s in range(2):
                d = lax.dot_general(left, right[:, s * wide:(s + 1) * wide], TN, preferred_element_type=F32)
                a_ref[j0 + nb:, s * wide:(s + 1) * wide] -= d[j0 + nb:rank]
    h, m, _ = split3(a_ref[:, :rank])
    q = jnp.dot(jnp.concatenate([h, m], 0).astype(BF), z, preferred_element_type=F32)
    qt_ref[...] = (q[:rank] + q[rank:]).astype(BF)


def attend_call(
    me, slots, live, z, z_other, kx, w, vg, ca, sa, cb, sb, cache_keys,
    *, steps, per_device, main, rp, n_dest, stop=9
):
    seq_len, width = cache_keys.shape
    rank = 2 * z.shape[0]
    tok_all = vg.shape[1] - LANES
    return pl.pallas_call(
        functools.partial(attend_kernel, per_device=per_device, steps=steps, main=main, stop=stop),
        in_specs=[smem()] * 3 + [vmem()] * 9 + [hbm()],
        out_specs=[hbm(), vmem()],
        out_shape=[
            jax.ShapeDtypeStruct((rank, seq_len), F32),
            jax.ShapeDtypeStruct((n_dest, rp, HD), F32),
        ],
        scratch_shapes=[
            pltpu.VMEM((seq_len, width), BF),
            pltpu.VMEM((rank, width), BF),
            pltpu.VMEM((rank, 2 * round_up(rank, LANES)), F32),
            pltpu.VMEM((rank, width), BF),
            pltpu.VMEM((seq_len, rank), F32),
            pltpu.VMEM((rank, seq_len), F32),
            pltpu.VMEM((KVH, tok_all, rank), F32),
            pltpu.VMEM((KVH, tok_all, HD), F32),
            pltpu.VMEM((KVH, tok_all, HD), F32),
            pltpu.VMEM((w.shape[0], LANES + tok_all, LANES), F32),
            pltpu.VMEM((seq_len, HD), F32),
            pltpu.VMEM((seq_len, HD), F32),
            pltpu.SemaphoreType.DMA,
            pltpu.SemaphoreType.DMA,
        ],
        compiler_params=pltpu.CompilerParams(vmem_limit_bytes=42 << 20),
        name="attend",
    )(me, slots, live, z, z_other, kx, w, vg, ca, sa, cb, sb, in_hbm(cache_keys))


def merge_kernel(me_ref, parts_ref, out_ref, *, steps, per_device):
    n, rp, _ = parts_ref.shape
    used = steps * per_device
    shift = me_ref[0] % (LANES // rp) * rp
    eye = lax.broadcasted_iota(jnp.int32, (rp, LANES), 0) + shift == lax.broadcasted_iota(jnp.int32, (rp, LANES), 1)

    def column(s, r):
        return jnp.sum(jnp.where(eye, parts_ref[s, r:r + 1, :], 0.0), axis=1, keepdims=True)

    ms = [column(s, used) for s in range(n)]
    top = functools.reduce(jnp.maximum, ms)
    total = jnp.zeros((rp, 1), F32)
    acc = jnp.zeros((rp, HD), F32)
    for s in range(n):
        w = jnp.exp(ms[s] - top)
        total = total + w * column(s, used + 1)
        acc = acc + w * parts_ref[s]
    o = acc / total
    for t in range(steps):
        for i in range(per_device):
            r = t * per_device + i
            out_ref[t:t + 1, i * HD:(i + 1) * HD] = o[r:r + 1, :].astype(BF)


def swap(x, moves):
    return lax.ppermute(x, "seq", moves)


def on_device(
    cache_keys,
    cache_values,
    sketch_matrix,
    queries,
    fresh_keys,
    fresh_values,
    chosen,
    shard_counts,
    outliers,
):
    seq_len, width = cache_keys.shape
    devices = lax.axis_size("seq")
    myself = lax.axis_index("seq")
    length = seq_len * devices
    steps = queries.shape[0]
    rank = sketch_matrix.shape[1]
    per_device = QH // devices
    n_lists = steps * KVH
    most = 3 * chosen.shape[2] // devices
    slots_all = round_up(steps * most, LANES // SPAN)
    tok_all = slots_all * SPAN
    main = min(MAIN, tok_all)
    used = steps * per_device
    rp = round_up(used + 2, 8)
    n_dest = devices
    me = jnp.full((1,), myself, jnp.int32)

    keep, send = sketch_share(me, sketch_matrix.T, cache_keys, length)

    half_width = HD // 2
    exponents = jnp.arange(half_width, dtype=F32) * (2.0 / HD)
    inverse_freq = jnp.exp(-jnp.log(F32(500000.0)) * exponents)
    inverse_freq = jnp.concatenate([inverse_freq, inverse_freq])
    blk = 64
    coarse = (myself * seq_len + blk * jnp.arange(seq_len // blk, dtype=jnp.int32)).astype(F32)[:, None] * inverse_freq
    fine = jnp.arange(blk, dtype=jnp.int32).astype(F32)[:, None] * inverse_freq
    late = (length + jnp.arange(steps, dtype=jnp.int32)).astype(F32)[:, None] * inverse_freq
    turns = (jnp.cos(coarse), jnp.sin(coarse), jnp.cos(fine), jnp.sin(fine))

    shard = jnp.arange(devices, dtype=jnp.int32)
    place = jnp.stack([
        jnp.sum(jnp.where(shard < myself, shard_counts, 0), axis=2),
        jnp.sum(jnp.where(shard == myself, shard_counts, 0), axis=2),
    ]).reshape(2 * n_lists)

    tie_shape = jax.ShapeDtypeStruct((1, LANES), F32)

    def find_slots(after):
        return pl.pallas_call(
            functools.partial(slots_kernel, most=most, spans=seq_len // SPAN, steps=steps),
            in_specs=[smem()] * 4 + [anywhere()],
            out_specs=[smem()] * 2 + [vmem()],
            out_shape=[
                jax.ShapeDtypeStruct((KVH, slots_all + 4 * PART), jnp.int32),
                jax.ShapeDtypeStruct((KVH * (steps + 1) + 2 + OMOST,), jnp.int32),
                tie_shape,
            ],
            name="find_slots",
        )(me, chosen.reshape(n_lists, -1), place, outliers, after)

    def known(live, after):
        return pl.pallas_call(
            functools.partial(known_kernel, per_device=per_device, rp=rp),
            in_specs=[smem()] + [vmem()] * 8 + [hbm(), anywhere()],
            out_specs=[vmem()] * 3,
            out_shape=[
                jax.ShapeDtypeStruct((KVH, LANES, 2 * HD), BF),
                jax.ShapeDtypeStruct((n_dest * rp // LANES, 4 * HD, LANES), BF),
                tie_shape,
            ],
            scratch_shapes=[
                pltpu.VMEM((OMOST, 16, width), BF),
                pltpu.VMEM((LANES, HD), F32),
                pltpu.VMEM((n_dest * rp, HD), F32),
                pltpu.SemaphoreType.DMA((OMOST,)),
            ],
            compiler_params=pltpu.CompilerParams(vmem_limit_bytes=8 << 20),
            name="known_keys",
        )(live, queries, fresh_keys, *turns, jnp.cos(late), jnp.sin(late), in_hbm(cache_keys), after)

    def slot_values(slots, live, after):
        return pl.pallas_call(
            functools.partial(values_kernel, main=main),
            in_specs=[smem()] * 2 + [vmem(), hbm(), anywhere()],
            out_specs=[vmem()] * 2,
            out_shape=[jax.ShapeDtypeStruct((KVH, LANES + tok_all, HD), BF), tie_shape],
            scratch_shapes=[
                pltpu.VMEM((KVH, seq_len, HD), BF),
                pltpu.VMEM((LANES + tok_all, HD), F32),
                pltpu.SemaphoreType.DMA((KVH,)),
            ],
            compiler_params=pltpu.CompilerParams(vmem_limit_bytes=16 << 20),
            name="slot_values",
        )(slots, live, fresh_values, in_hbm(cache_values), after)

    z = keep + swap(send, [(i, i ^ 1) for i in range(devices)])
    hops = [1 << k for k in range(1, devices.bit_length() - 1)]
    for k in range(len(hops)):
        other = k ^ 1 if k < 2 and len(hops) >= 2 else k
        moves = [(i, i ^ hops[k if i % 2 == 0 else other]) for i in range(devices)]
        going = z.astype(BF)
        came = swap(going, moves).astype(F32)
        if k == 0:
            slots, live, tie = find_slots(going)
            came = came + tie[0, 0]
        if k == min(1, len(hops) - 1):
            kx, w, tie = known(live, going)
            came = came + tie[0, 0]
        if k == len(hops) - 1:
            vg, tie = slot_values(slots, live, going)
            came = came + tie[0, 0]
        z = z + came
    z = z.astype(BF)
    z_other = swap(z, [(i, i ^ 1) for i in range(devices)])

    kft, parts = attend_call(
        me, slots, live, z, z_other, kx, w, vg, *turns, cache_keys,
        steps=steps, per_device=per_device, main=main, rp=rp, n_dest=n_dest,
    )
    parts = lax.all_to_all(parts, "seq", 0, 0, tiled=True)
    attended = pl.pallas_call(
        functools.partial(merge_kernel, steps=steps, per_device=per_device),
        in_specs=[smem(), vmem()],
        out_specs=vmem(),
        out_shape=jax.ShapeDtypeStruct((steps, per_device * HD), BF),
        name="merge",
    )(me, parts)
    return (attended, kft.T)


def solution(mesh):
    in_specs = (
        P(("groups", "seq"), None),
        P(("groups", "seq"), None),
        P(),
        P("groups", None),
        P("groups", None),
        P("groups", None),
        P("groups", None, None),
        P("groups", None, None),
        P("groups"),
    )
    out_specs = (P("groups", "seq"), P(("groups", "seq"), None))
    return jax.shard_map(
        on_device, mesh=mesh, in_specs=in_specs, out_specs=out_specs, check_vma=False
    )
```

```python
import functools

import jax
import jax.numpy as jnp
from jax import lax
from jax.experimental import pallas as pl
from jax.experimental.pallas import tpu as pltpu
from jax.sharding import PartitionSpec as P

KVH = 8
HD = 128
QH = 64
SPAN = 8
OMOST = 4
BF = jnp.bfloat16
F32 = jnp.float32
DEAD = -1e30
LANES = 128
MAIN = 640
PART = 8
STRAIGHT = 2
EARLY = 3
AHEAD = 3
NT = (((1,), (1,)), ((), ()))
TN = (((0,), (0,)), ((), ()))


def vmem():
    return pl.BlockSpec(memory_space=pltpu.VMEM)


def smem():
    return pl.BlockSpec(memory_space=pltpu.SMEM)


def hbm():
    return pl.BlockSpec(memory_space=pltpu.HBM)


def in_hbm(x):
    return pltpu.with_memory_space_constraint(x, pltpu.HBM)


def anywhere():
    return pl.BlockSpec(memory_space=pl.ANY)


def round_up(x, m):
    return (x + m - 1) // m * m


def split2(x):
    high = x.astype(BF)
    return high, (x - high.astype(F32)).astype(BF)


def split3(x):
    high = x.astype(BF).astype(F32)
    rest = x - high
    middle = rest.astype(BF).astype(F32)
    return high, middle, rest - middle


def sketch_kernel(
    me_ref, st_hbm, keys_hbm, keep_ref, send_ref, st_ref, keys_ref, acc_ref, st_sem, sem, *, scale, chunk
):
    seq_len = keys_ref.shape[0]
    rank = st_ref.shape[0]
    half = rank // 2
    n = seq_len // chunk
    st_copy = pltpu.make_async_copy(st_hbm, st_ref, st_sem)
    st_copy.start()
    copies = [
        pltpu.make_async_copy(
            keys_hbm.at[pl.ds(i * chunk, chunk)], keys_ref.at[pl.ds(i * chunk, chunk)], sem.at[i]
        )
        for i in range(n)
    ]
    for c in copies[:AHEAD]:
        c.start()
    st_copy.wait()
    st = st_ref[...].astype(BF)

    def rows(i):
        return keys_ref[i * chunk:(i + 1) * chunk, :]

    def first(i):
        return lax.dot_general(st, rows(i), NT, preferred_element_type=F32).astype(BF)

    def second(i, y):
        return jnp.dot(y, rows(i), preferred_element_type=F32)

    def arrive(i):
        copies[i].wait()
        if i + AHEAD < n:
            copies[i + AHEAD].start()

    arrive(0)
    y = first(0)
    for i in range(1, n):
        arrive(i)
        y_next = first(i)
        z = second(i - 1, y)
        if i == 1:
            acc_ref[...] = z
        else:
            acc_ref[...] += z
        y = y_next
    acc_ref[...] = (acc_ref[...] + second(n - 1, y)) * scale
    core = me_ref[0] % 2
    keep_ref[...] = acc_ref[pl.ds(pl.multiple_of(core * half, 8), half), :]
    send_ref[...] = acc_ref[pl.ds(pl.multiple_of((1 - core) * half, 8), half), :]


def sketch_share(me, sketch_t, cache_keys, length):
    seq_len, width = cache_keys.shape
    rank = sketch_t.shape[0]
    chunk = min(512, seq_len)
    half = jax.ShapeDtypeStruct((rank // 2, width), F32)
    return pl.pallas_call(
        functools.partial(sketch_kernel, scale=1.0 / length, chunk=chunk),
        in_specs=[smem(), hbm(), hbm()],
        out_specs=[vmem(), vmem()],
        out_shape=[half, half],
        scratch_shapes=[
            pltpu.VMEM((rank, width), F32),
            pltpu.VMEM((seq_len, width), BF),
            pltpu.VMEM((rank, width), F32),
            pltpu.SemaphoreType.DMA,
            pltpu.SemaphoreType.DMA((seq_len // chunk,)),
        ],
        compiler_params=pltpu.CompilerParams(vmem_limit_bytes=24 << 20),
        name="sketch_share",
    )(me, in_hbm(sketch_t), in_hbm(cache_keys))


class Lists:
    def __init__(self, me_ref, chosen_ref, begin_ref, count_ref, outl_ref, spans, most=None):
        self.chosen, self.begin, self.counts, self.outl = chosen_ref, begin_ref, count_ref, outl_ref
        self.spans, self.most = spans, most
        self.base = me_ref[0] * spans

    def span(self, t, g, slot):
        i = t * KVH + g
        last = self.chosen.shape[1] - 1
        picked = self.chosen[i, jnp.minimum(self.begin[t, g] + slot, last)]
        return jnp.clip(picked - self.base, 0, self.spans - 1)

    def count(self, t, g):
        return jnp.minimum(self.counts[t, g], self.most)

    def starts(self, g, steps):
        at = [jnp.int32(0)]
        for t in range(steps):
            at.append(at[-1] + self.count(t, g))
        return at

    def outliers(self):
        n = self.outl.shape[0]
        first = jnp.int32(0)
        here = jnp.int32(0)
        for i in range(n):
            s = self.outl[i]
            first = first + (s < self.base).astype(jnp.int32)
            here = here + ((s >= self.base) & (s < self.base + self.spans)).astype(jnp.int32)
        found = [
            jnp.clip(self.outl[jnp.minimum(first + j, n - 1)] - self.base, 0, self.spans - 1) for j in range(OMOST)
        ]
        return jnp.minimum(here, OMOST), found

    def each_part(self, g, steps, copy):
        at = self.starts(g, steps)
        for t in range(steps):
            def part(k, _, t=t):
                copy([self.span(t, g, k * PART + j) for j in range(PART)], at[t] + k * PART)
                return 0

            for k in range(STRAIGHT):
                part(k, 0)
            lax.fori_loop(STRAIGHT, (self.count(t, g) + PART - 1) // PART, part, 0)
        return at


def known_kernel(
    me_ref, outl_ref, q_ref, fk_ref, ca_ref, sa_ref, cb_ref, sb_ref, cq_ref, sq_ref, keys_hbm, after_ref,
    kx_ref, w_ref, tie_ref,
    okeys_ref, xtmp_ref, qtmp_ref, osem, *, per_device, rp, spans
):
    steps = q_ref.shape[0]
    tie_ref[...] = jnp.zeros_like(tie_ref)
    _, o_span = Lists(me_ref, None, None, None, outl_ref, spans).outliers()
    o_copies = [
        pltpu.make_async_copy(
            keys_hbm.at[pl.ds(pl.multiple_of(o_span[j] // 2 * 16, 16), 16)], okeys_ref.at[j], osem.at[j]
        )
        for j in range(OMOST)
    ]
    for c in o_copies:
        c.start()

    lane = lax.broadcasted_iota(jnp.int32, (8, LANES), 1)
    sign = jnp.where(lane < HD // 2, -1.0, 1.0)

    qtmp_ref[...] = jnp.zeros_like(qtmp_ref)
    for t in range(steps):
        x = q_ref[t:t + 1, :].astype(F32)
        for h in range(QH):
            r = h // per_device * rp + t * per_device + h % per_device
            qtmp_ref[r:r + 1, :] = x[:, h * HD:(h + 1) * HD]
    scale = 1.0 / (HD ** 0.5)
    row = lax.broadcasted_iota(jnp.int32, (LANES, LANES), 0) % rp
    lane_r = lax.broadcasted_iota(jnp.int32, (LANES, LANES), 1)
    cq = jnp.zeros((LANES, LANES), F32)
    sq = jnp.zeros((LANES, LANES), F32)
    for t in range(steps):
        here = (row >= t * per_device) & (row < (t + 1) * per_device)
        cq = jnp.where(here, cq_ref[t:t + 1, :] * scale, cq)
        sq = jnp.where(here, sq_ref[t:t + 1, :] * scale, sq)
    sq = jnp.where(lane_r < HD // 2, -sq, sq)
    for pk in range(w_ref.shape[0]):
        x = qtmp_ref[pk * LANES:(pk + 1) * LANES, :]
        x = x * cq + pltpu.roll(x, HD // 2, 1) * sq
        z = jnp.where(lane_r < HD // 2, 1.0, -1.0) * pltpu.roll(x, HD // 2, 1)
        hi, lo = split2(jnp.concatenate([x.T, z.T], 0))
        w_ref[pk] = jnp.concatenate([hi, lo], 0)

    blk = cb_ref.shape[0] // SPAN
    turns = []
    for j in range(OMOST):
        a = o_span[j] // blk
        b = pl.ds(pl.multiple_of(o_span[j] % blk * SPAN, SPAN), SPAN)
        ca, sa = ca_ref[pl.ds(a, 1), :], sa_ref[pl.ds(a, 1), :]
        cb, sb = cb_ref[b, :], sb_ref[b, :]
        turns.append((ca * cb - sa * sb, (sa * cb + ca * sb) * sign))
    for c in o_copies:
        c.wait()
    x_rows = kx_ref.shape[1]
    xtmp_ref[...] = jnp.zeros_like(xtmp_ref)
    fs = sq_ref[:steps, :] * sign[:1]
    for g in range(KVH):
        sl = slice(g * HD, (g + 1) * HD)
        for j in range(OMOST):
            wide = okeys_ref[j, :, sl].astype(F32)
            x = jnp.where(o_span[j] % 2 == 0, wide[:8], wide[8:])
            xtmp_ref[j * SPAN:(j + 1) * SPAN, :] = x * turns[j][0] + pltpu.roll(x, HD // 2, 1) * turns[j][1]
        x = fk_ref[:, sl].astype(F32)
        o = OMOST * SPAN
        xtmp_ref[o:o + steps, :] = x * cq_ref[:steps, :] + pltpu.roll(x, HD // 2, 1) * fs
        kx_ref[g, :, :HD] = xtmp_ref[...].astype(BF)
        kx_ref[g, :, HD:] = jnp.zeros((x_rows, HD), BF)


def values_kernel(
    me_ref, chosen_ref, begin_ref, count_ref, outl_ref, fv_ref, values_hbm, after_ref, vg_ref, tie_ref,
    values_ref, vtmp_ref, sem, *, main, g0, most
):
    steps = fv_ref.shape[0]
    rows_all = vtmp_ref.shape[0]
    n = vg_ref.shape[0]
    copies = [
        pltpu.make_async_copy(values_hbm.at[:, pl.ds((g0 + i) * HD, HD)], values_ref.at[i], sem.at[i]) for i in range(n)
    ]
    for c in copies[:AHEAD]:
        c.start()
    tie_ref[...] = jnp.zeros_like(tie_ref)
    vtmp_ref[...] = jnp.zeros_like(vtmp_ref)
    lists = Lists(me_ref, chosen_ref, begin_ref, count_ref, outl_ref, values_ref.shape[1] // SPAN, most)
    _, o_span = lists.outliers()

    for i in range(n):
        g = g0 + i

        def rows_of(span, i=i):
            wide = values_ref[i, pl.ds(pl.multiple_of(span // 2 * 16, 16), 16), :].astype(F32)
            return jnp.where(span % 2 == 0, wide[:8], wide[8:])

        def put(spans, slot, rows_of=rows_of):
            dst = pl.ds(pl.multiple_of(LANES + slot * SPAN, SPAN), PART * SPAN)
            vtmp_ref[dst, :] = jnp.concatenate([rows_of(span) for span in spans], 0)

        copies[i].wait()
        if i + AHEAD < n:
            copies[i + AHEAD].start()
        for j in range(OMOST):
            vtmp_ref[j * SPAN:(j + 1) * SPAN, :] = rows_of(o_span[j])
        vtmp_ref[OMOST * SPAN:OMOST * SPAN + steps, :] = fv_ref[:, g * HD:(g + 1) * HD].astype(F32)
        total = lists.each_part(g, steps, put)[steps]
        vg_ref[i, :LANES + main, :] = vtmp_ref[:LANES + main, :].astype(BF)
        if LANES + main < rows_all:
            def more(k, _, i=i):
                at = pl.ds(pl.multiple_of(LANES + main + k * LANES, LANES), LANES)
                vg_ref[i, at, :] = vtmp_ref[at, :].astype(BF)
                return 0

            lax.fori_loop(0, (jnp.maximum(total * SPAN - main, 0) + LANES - 1) // LANES, more, 0)


def attend_kernel(
    me_ref, chosen_ref, begin_ref, count_ref, outl_ref, zmine_ref, zother_ref, kx_ref, w_ref, vga_ref, vgb_ref,
    ca_ref, sa_ref, cb_ref, sb_ref, keys_hbm,
    kft_hbm, out_ref,
    keys_ref, z_ref, a_ref, qt_ref, kf_ref, kft_ref, kg_ref, cg_ref, sg_ref, sc_ref, cc_ref, ss_ref, acc_ref,
    sem, out_sem, *, per_device, steps, main, most, stop=9
):
    rank, width = z_ref.shape
    half = rank // 2
    seq_len = keys_ref.shape[0]
    load = pltpu.make_async_copy(keys_hbm, keys_ref, sem)
    load.start()

    core = me_ref[0] % 2
    z_ref[pl.ds(pl.multiple_of(core * half, 16), half), :] = zmine_ref[...]
    z_ref[pl.ds(pl.multiple_of((1 - core) * half, 16), half), :] = zother_ref[...]
    turn_tables(ca_ref, sa_ref, cb_ref, sb_ref, cc_ref, ss_ref)
    basis(z_ref, a_ref, qt_ref)
    qt = qt_ref[...]

    load.wait()
    if stop == 1:
        return
    chunk = seq_len // KVH
    for i in range(KVH):
        rows = slice(i * chunk, (i + 1) * chunk)
        kf = lax.dot_general(keys_ref[rows, :], qt, NT, preferred_element_type=F32)
        kf_ref[rows, :] = kf
        kft_ref[:, rows] = kf.T
    store = pltpu.make_async_copy(kft_ref, kft_hbm, out_sem)
    store.start()
    if stop == 2:
        store.wait()
        return

    lists = Lists(me_ref, chosen_ref, begin_ref, count_ref, outl_ref, seq_len // SPAN, most)
    starts = []
    for g in range(KVH):
        def gather(spans, slot, g=g):
            got = []
            for span in spans:
                src = pl.ds(pl.multiple_of(span * SPAN, SPAN), SPAN)
                got.append((kf_ref[src, :], cc_ref[src, :], ss_ref[src, :]))
            dst = pl.ds(pl.multiple_of(slot * SPAN, SPAN), PART * SPAN)
            for ref, rows in zip((kg_ref, cg_ref, sg_ref), zip(*got)):
                ref[g, dst, :] = jnp.concatenate(rows, 0)

        starts.append(lists.each_part(g, steps, gather))
    totals = [at[steps] for at in starts]

    def values(g, rows):
        n = vga_ref.shape[0]
        return vga_ref[g, rows, :] if g < n else vgb_ref[g - n, rows, :]

    if stop == 3:
        store.wait()
        return

    n_dest, rp, _ = out_ref.shape
    dests = n_dest // KVH
    qr = dests * rp
    heads = LANES // qr
    packs = w_ref.shape[0]
    o_live = lists.outliers()[0] * SPAN
    first_shard = me_ref[0] == 0
    column = lax.broadcasted_iota(jnp.int32, (8, LANES), 1)[:1]
    col_head = column // qr
    col_row = column % rp
    col_step = col_row // per_device

    def bounds(pk, h):
        first = jnp.full((1, LANES), 1 << 30, jnp.int32)
        last = jnp.zeros((1, LANES), jnp.int32)
        for t in range(steps):
            at = starts[pk * heads + h]
            here = (col_head == h) & (col_step == t)
            first = jnp.where(here, at[t] * SPAN, first)
            last = jnp.where(here, at[t + 1] * SPAN, last)
        return first, last

    def product(pk, y):
        r = jnp.dot(y, w_ref[pk, :2 * HD, :], preferred_element_type=F32)
        return r + jnp.dot(y, w_ref[pk, 2 * HD:, :], preferred_element_type=F32)

    token = lax.broadcasted_iota(jnp.int32, (LANES, LANES), 0)

    def slot_scores(pk, at, n, limits):
        rows = pl.ds(at, n)
        ys = []
        for h in range(heads):
            g = pk * heads + h
            x = jnp.dot(kg_ref[g, rows, :].astype(BF), qt_ref[:, g * HD:(g + 1) * HD], preferred_element_type=F32)
            ys.append(jnp.concatenate([(x * cg_ref[g, rows, :]).astype(BF), (x * sg_ref[g, rows, :]).astype(BF)], 1))
        r = product(pk, jnp.concatenate(ys, 0))
        s = jnp.full((n, LANES), DEAD, F32)
        here = lax.broadcasted_iota(jnp.int32, (n, LANES), 0) + at
        for h in range(heads):
            first, last = limits[h]
            s = jnp.where((here >= first) & (here < last), r[h * n:(h + 1) * n], s)
        return s

    def known_scores(pk):
        s = jnp.full((LANES, LANES), DEAD, F32)
        new = token - OMOST * SPAN
        is_live = (token < o_live) | (first_shard & (new >= 0) & (new <= col_step))
        is_live = is_live & (new < steps) & (col_row < steps * per_device)
        r = product(pk, kx_ref[pk * heads:(pk + 1) * heads].reshape(heads * LANES, 2 * HD))
        for h in range(heads):
            s = jnp.where(is_live & (col_head == h), r[h * LANES:(h + 1) * LANES], s)
        return s

    limits = [[bounds(pk, h) for h in range(heads)] for pk in range(packs)]
    extra = kg_ref.shape[1] - main
    blocks = []
    for pk in range(packs):
        longest = functools.reduce(jnp.maximum, totals[pk * heads:(pk + 1) * heads])
        blocks.append((jnp.maximum(longest * SPAN - main, 0) + LANES - 1) // LANES)

    tops = []
    for pk in range(packs):
        s = known_scores(pk)
        sc_ref[pk, :LANES, :] = s
        top = jnp.max(s, axis=0, keepdims=True)
        s = slot_scores(pk, 0, main, limits[pk])
        sc_ref[pk, LANES:LANES + main, :] = s
        tops.append(jnp.maximum(top, jnp.max(s, axis=0, keepdims=True)))
    if extra > 0:
        for pk in range(packs):
            def more(k, top, pk=pk):
                at = pl.multiple_of(main + k * LANES, LANES)
                s = slot_scores(pk, at, LANES, limits[pk])
                sc_ref[pk, pl.ds(pl.multiple_of(LANES + at, LANES), LANES), :] = s
                return jnp.maximum(top, jnp.max(s, axis=0, keepdims=True))

            tops[pk] = lax.fori_loop(0, blocks[pk], more, tops[pk])
    if stop == 4:
        store.wait()
        return

    used = steps * per_device

    def weights(s, top):
        return jnp.where(s > 0.5 * DEAD, jnp.exp(s - top), 0.0)

    def weighted(pt, h, values):
        hi, lo = split2(pt[h * qr:(h + 1) * qr, :])
        r = jnp.dot(jnp.concatenate([hi, lo], 0), values, preferred_element_type=F32)
        return r[:qr] + r[qr:]

    sums = []
    for pk in range(packs):
        pts = []
        total = jnp.zeros((LANES, LANES), F32)
        for at in range(0, LANES + main, LANES):
            p = weights(sc_ref[pk, at:at + LANES, :], tops[pk])
            total = total + p
            pts.append(p.T)
        sums.append(jnp.sum(total, axis=0, keepdims=True))
        pt = jnp.concatenate(pts, 1)
        for h in range(heads):
            g = pk * heads + h
            acc = weighted(pt, h, values(g, slice(0, LANES + main)))
            for a in range(dests):
                acc_ref[g * dests + a] = acc[a * rp:(a + 1) * rp]
    if extra > 0:
        for pk in range(packs):
            def add(k, total, pk=pk):
                at = pl.multiple_of(LANES + main + k * LANES, LANES)
                p = weights(sc_ref[pk, pl.ds(at, LANES), :], tops[pk])
                pt = p.T
                for h in range(heads):
                    g = pk * heads + h

                    @pl.when(totals[g] * SPAN > main + k * LANES)
                    def _():
                        acc = weighted(pt, h, values(g, pl.ds(at, LANES)))
                        for a in range(dests):
                            acc_ref[g * dests + a] += acc[a * rp:(a + 1) * rp]

                return total + jnp.sum(p, axis=0, keepdims=True)

            sums[pk] = lax.fori_loop(0, blocks[pk], add, sums[pk])
    for d in range(n_dest):
        pk = d // (heads * dests)
        row = lax.broadcasted_iota(jnp.int32, (rp, LANES), 0)
        r = acc_ref[d]
        for k, extra_row in enumerate((*split3(tops[pk]), sums[pk])):
            r = jnp.where(row == used + k, extra_row, r)
        out_ref[d] = r.astype(BF)
    store.wait()


def turn_tables(ca_ref, sa_ref, cb_ref, sb_ref, cc_ref, ss_ref):
    blk = cb_ref.shape[0]
    cb = cb_ref[...]
    sb = sb_ref[...]
    for a in range(cc_ref.shape[0] // blk):
        ca = ca_ref[a:a + 1, :]
        sa = sa_ref[a:a + 1, :]
        cc_ref[a * blk:(a + 1) * blk, :] = ca * cb - sa * sb
        ss_ref[a * blk:(a + 1) * blk, :] = sa * cb + ca * sb


def basis(z_ref, a_ref, qt_ref):
    rank = z_ref.shape[0]
    wide = round_up(rank, LANES)
    z = z_ref[...]
    c = lax.dot_general(z, z, NT, preferred_element_type=F32)
    rows = lax.broadcasted_iota(jnp.int32, (rank, wide), 0)
    cols = lax.broadcasted_iota(jnp.int32, (rank, wide), 1)
    a_ref[:, :wide] = jnp.where(rows == cols, 1.0, 0.0)
    a_ref[:, wide:wide + rank] = c
    a_ref[:, wide + rank:] = jnp.zeros((rank, wide - rank), F32)
    nb = 32
    half_tiles = wide // LANES
    for j0 in range(0, rank, nb):
        tiles = [t for t in range(half_tiles) if t * LANES < j0 + nb]
        tiles += [half_tiles + t for t in range(half_tiles) if (t + 1) * LANES > j0]
        part = {t: a_ref[j0:j0 + nb, t * LANES:(t + 1) * LANES] for t in tiles}
        row = lax.broadcasted_iota(jnp.int32, (nb, LANES), 0)
        column = []
        for j in range(nb):
            t, o = divmod(j0 + j, LANES)
            column.append(jnp.broadcast_to(part[half_tiles + t][:, o:o + 1], (nb, LANES)))
        for j in range(nb):
            inverse = lax.rsqrt(jnp.broadcast_to(column[j][j:j + 1, :], (nb, LANES)))
            low = jnp.where(row > j, column[j] * inverse, 0.0)
            for k in range(j + 1, nb):
                column[k] = column[k] - low * jnp.broadcast_to(low[k:k + 1, :], (nb, LANES))
            for t in tiles:
                upper = jnp.broadcast_to(part[t][j:j + 1, :], (nb, LANES)) * inverse
                part[t] = jnp.where(row == j, upper, part[t] - low * upper)
        for t in tiles:
            a_ref[j0:j0 + nb, t * LANES:(t + 1) * LANES] = part[t]
        if j0 + nb < rank:
            upper = jnp.concatenate(
                [part[t] if t in part else jnp.zeros((nb, LANES), F32) for t in range(2 * half_tiles)], 1
            )
            h, m, l = split3(upper)
            left = jnp.concatenate([h, h, m, m, h, l], 0)[:, wide:].astype(BF)
            right = jnp.concatenate([h, m, h, m, l, h], 0).astype(BF)
            for s in range(2):
                d = lax.dot_general(left, right[:, s * wide:(s + 1) * wide], TN, preferred_element_type=F32)
                a_ref[j0 + nb:, s * wide:(s + 1) * wide] -= d[j0 + nb:rank]
    h, m, _ = split3(a_ref[:, :rank])
    q = jnp.dot(jnp.concatenate([h, m], 0).astype(BF), z, preferred_element_type=F32)
    qt_ref[...] = (q[:rank] + q[rank:]).astype(BF)


def attend_call(
    me, lists, z, z_other, kx, w, vga, vgb, ca, sa, cb, sb, cache_keys,
    *, steps, per_device, main, most, rp, n_dest, stop=9
):
    seq_len, width = cache_keys.shape
    rank = 2 * z.shape[0]
    tok_all = vga.shape[1] - LANES
    return pl.pallas_call(
        functools.partial(attend_kernel, per_device=per_device, steps=steps, main=main, most=most, stop=stop),
        in_specs=[smem()] * 5 + [vmem()] * 10 + [hbm()],
        out_specs=[hbm(), vmem()],
        out_shape=[
            jax.ShapeDtypeStruct((rank, seq_len), F32),
            jax.ShapeDtypeStruct((n_dest, rp, HD), BF),
        ],
        scratch_shapes=[
            pltpu.VMEM((seq_len, width), BF),
            pltpu.VMEM((rank, width), BF),
            pltpu.VMEM((rank, 2 * round_up(rank, LANES)), F32),
            pltpu.VMEM((rank, width), BF),
            pltpu.VMEM((seq_len, rank), F32),
            pltpu.VMEM((rank, seq_len), F32),
            pltpu.VMEM((KVH, tok_all, rank), F32),
            pltpu.VMEM((KVH, tok_all, HD), F32),
            pltpu.VMEM((KVH, tok_all, HD), F32),
            pltpu.VMEM((w.shape[0], LANES + tok_all, LANES), F32),
            pltpu.VMEM((seq_len, HD), F32),
            pltpu.VMEM((seq_len, HD), F32),
            pltpu.VMEM((n_dest, rp, HD), F32),
            pltpu.SemaphoreType.DMA,
            pltpu.SemaphoreType.DMA,
        ],
        compiler_params=pltpu.CompilerParams(vmem_limit_bytes=42 << 20),
        name="attend",
    )(me, *lists, z, z_other, kx, w, vga, vgb, ca, sa, cb, sb, in_hbm(cache_keys))


def merge_kernel(me_ref, parts_ref, out_ref, top_ref, sum_ref, *, steps, per_device):
    n, rp, _ = parts_ref.shape
    used = steps * per_device
    parts = parts_ref[...].astype(F32)
    rows = pl.ds(pl.multiple_of(me_ref[0] % (LANES // rp) * rp, 8), rp)
    top_ref[...] = (parts[:, used, :] + parts[:, used + 1, :] + parts[:, used + 2, :]).T
    sum_ref[...] = parts[:, used + 3, :].T
    tops = top_ref[rows, :]
    w = jnp.exp(tops - jnp.max(tops, axis=1, keepdims=True))
    w = w / jnp.sum(w * sum_ref[rows, :], axis=1, keepdims=True)
    o = jnp.zeros((rp, HD), F32)
    for s in range(n):
        o = o + w[:, s:s + 1] * parts[s]
    for t in range(steps):
        for i in range(per_device):
            r = t * per_device + i
            out_ref[t:t + 1, i * HD:(i + 1) * HD] = o[r:r + 1, :].astype(BF)


def swap(x, moves):
    return lax.ppermute(x, "seq", moves)


def on_device(
    cache_keys,
    cache_values,
    sketch_matrix,
    queries,
    fresh_keys,
    fresh_values,
    chosen,
    shard_counts,
    outliers,
):
    seq_len, width = cache_keys.shape
    devices = lax.axis_size("seq")
    myself = lax.axis_index("seq")
    length = seq_len * devices
    steps = queries.shape[0]
    rank = sketch_matrix.shape[1]
    per_device = QH // devices
    n_lists = steps * KVH
    most = 3 * chosen.shape[2] // devices
    slots_all = round_up(max(steps * most, steps * STRAIGHT * PART), LANES // SPAN)
    tok_all = slots_all * SPAN
    main = min(MAIN, tok_all)
    used = steps * per_device
    rp = round_up(used + 4, 16)
    n_dest = devices
    me = jnp.full((1,), myself, jnp.int32)

    keep, send = sketch_share(me, sketch_matrix.T, cache_keys, length)

    half_width = HD // 2
    exponents = jnp.arange(half_width, dtype=F32) * (2.0 / HD)
    inverse_freq = jnp.exp(-jnp.log(F32(500000.0)) * exponents)
    inverse_freq = jnp.concatenate([inverse_freq, inverse_freq])
    blk = 64
    coarse = (myself * seq_len + blk * jnp.arange(seq_len // blk, dtype=jnp.int32)).astype(F32)[:, None] * inverse_freq
    fine = jnp.arange(blk, dtype=jnp.int32).astype(F32)[:, None] * inverse_freq
    late = (length + jnp.arange(steps, dtype=jnp.int32)).astype(F32)[:, None] * inverse_freq
    turns = (jnp.cos(coarse), jnp.sin(coarse), jnp.cos(fine), jnp.sin(fine))

    shard = jnp.arange(devices, dtype=jnp.int32)
    begin = jnp.sum(jnp.where(shard < myself, shard_counts, 0), axis=2)
    count = jnp.sum(jnp.where(shard == myself, shard_counts, 0), axis=2)
    lists = (chosen.reshape(n_lists, -1), begin, count, outliers)
    tie_shape = jax.ShapeDtypeStruct((1, LANES), F32)

    def known(after):
        return pl.pallas_call(
            functools.partial(known_kernel, per_device=per_device, rp=rp, spans=seq_len // SPAN),
            in_specs=[smem()] * 2 + [vmem()] * 8 + [hbm(), anywhere()],
            out_specs=[vmem()] * 3,
            out_shape=[
                jax.ShapeDtypeStruct((KVH, LANES, 2 * HD), BF),
                jax.ShapeDtypeStruct((n_dest * rp // LANES, 4 * HD, LANES), BF),
                tie_shape,
            ],
            scratch_shapes=[
                pltpu.VMEM((OMOST, 16, width), BF),
                pltpu.VMEM((LANES, HD), F32),
                pltpu.VMEM((n_dest * rp, HD), F32),
                pltpu.SemaphoreType.DMA((OMOST,)),
            ],
            compiler_params=pltpu.CompilerParams(vmem_limit_bytes=8 << 20),
            name="known_keys",
        )(me, outliers, queries, fresh_keys, *turns, jnp.cos(late), jnp.sin(late), in_hbm(cache_keys), after)

    def slot_values(g0, n, after):
        return pl.pallas_call(
            functools.partial(values_kernel, main=main, g0=g0, most=most),
            in_specs=[smem()] * 5 + [vmem(), hbm(), anywhere()],
            out_specs=[vmem()] * 2,
            out_shape=[jax.ShapeDtypeStruct((n, LANES + tok_all, HD), BF), tie_shape],
            scratch_shapes=[
                pltpu.VMEM((n, seq_len, HD), BF),
                pltpu.VMEM((LANES + tok_all, HD), F32),
                pltpu.SemaphoreType.DMA((n,)),
            ],
            compiler_params=pltpu.CompilerParams(vmem_limit_bytes=16 << 20),
            name="slot_values",
        )(me, *lists, fresh_values, in_hbm(cache_values), after)

    z = keep + swap(send, [(i, i ^ 1) for i in range(devices)])
    hops = [1 << k for k in range(1, devices.bit_length() - 1)]
    for k in range(len(hops)):
        other = k ^ 1 if k < 2 and len(hops) >= 2 else k
        moves = [(i, i ^ hops[k if i % 2 == 0 else other]) for i in range(devices)]
        going = z.astype(BF)
        came = swap(going, moves).astype(F32)
        if k == 0:
            kx, w, tie = known(going)
            came = came + tie[0, 0]
        if k == min(1, len(hops) - 1):
            vga, tie = slot_values(0, EARLY, going)
            came = came + tie[0, 0]
        if k == len(hops) - 1:
            vgb, tie = slot_values(EARLY, KVH - EARLY, going)
            came = came + tie[0, 0]
        z = z + came
    z = z.astype(BF)
    z_other = swap(z, [(i, i ^ 1) for i in range(devices)])

    kft, parts = attend_call(
        me, lists, z, z_other, kx, w, vga, vgb, *turns, cache_keys,
        steps=steps, per_device=per_device, main=main, most=most, rp=rp, n_dest=n_dest,
    )
    parts = lax.all_to_all(parts, "seq", 0, 0, tiled=True)
    attended = pl.pallas_call(
        functools.partial(merge_kernel, steps=steps, per_device=per_device),
        in_specs=[smem(), vmem()],
        out_specs=vmem(),
        out_shape=jax.ShapeDtypeStruct((steps, per_device * HD), BF),
        scratch_shapes=[pltpu.VMEM((LANES, devices), F32)] * 2,
        name="merge",
    )(me, parts)
    return (attended, kft.T)


def solution(mesh):
    in_specs = (
        P(("groups", "seq"), None),
        P(("groups", "seq"), None),
        P(),
        P("groups", None),
        P("groups", None),
        P("groups", None),
        P("groups", None, None),
        P("groups", None, None),
        P("groups"),
    )
    out_specs = (P("groups", "seq"), P(("groups", "seq"), None))
    return jax.shard_map(
        on_device, mesh=mesh, in_specs=in_specs, out_specs=out_specs, check_vma=False
    )
```

```python
import functools

import jax
import jax.numpy as jnp
from jax import lax
from jax.experimental import pallas as pl
from jax.experimental.pallas import tpu as pltpu
from jax.sharding import PartitionSpec as P

KVH = 8
HD = 128
QH = 64
SPAN = 8
OMOST = 4
BF = jnp.bfloat16
F32 = jnp.float32
DEAD = -1e30
LANES = 128
MAIN = 640
PART = 8
STRAIGHT = 6
EARLY = 4
AHEAD = 3
NT = (((1,), (1,)), ((), ()))
TN = (((0,), (0,)), ((), ()))


def vmem():
    return pl.BlockSpec(memory_space=pltpu.VMEM)


def smem():
    return pl.BlockSpec(memory_space=pltpu.SMEM)


def hbm():
    return pl.BlockSpec(memory_space=pltpu.HBM)


def in_hbm(x):
    return pltpu.with_memory_space_constraint(x, pltpu.HBM)


def anywhere():
    return pl.BlockSpec(memory_space=pl.ANY)


def round_up(x, m):
    return (x + m - 1) // m * m


def split2(x):
    high = x.astype(BF)
    return high, (x - high.astype(F32)).astype(BF)


def split3(x):
    high = x.astype(BF).astype(F32)
    rest = x - high
    middle = rest.astype(BF).astype(F32)
    return high, middle, rest - middle


def sketch_kernel(
    me_ref, st_hbm, keys_hbm, keep_ref, send_ref, st_ref, keys_ref, acc_ref, st_sem, sem, *, scale, chunk
):
    seq_len = keys_ref.shape[0]
    rank = st_ref.shape[0]
    half = rank // 2
    n = seq_len // chunk
    st_copy = pltpu.make_async_copy(st_hbm, st_ref, st_sem)
    st_copy.start()
    copies = [
        pltpu.make_async_copy(
            keys_hbm.at[pl.ds(i * chunk, chunk)], keys_ref.at[pl.ds(i * chunk, chunk)], sem.at[i]
        )
        for i in range(n)
    ]
    for c in copies[:AHEAD]:
        c.start()
    st_copy.wait()
    st = st_ref[...].astype(BF)

    def rows(i):
        return keys_ref[i * chunk:(i + 1) * chunk, :]

    def first(i):
        return lax.dot_general(st, rows(i), NT, preferred_element_type=F32).astype(BF)

    def second(i, y):
        return jnp.dot(y, rows(i), preferred_element_type=F32)

    def arrive(i):
        copies[i].wait()
        if i + AHEAD < n:
            copies[i + AHEAD].start()

    arrive(0)
    y = first(0)
    for i in range(1, n):
        arrive(i)
        y_next = first(i)
        z = second(i - 1, y)
        if i == 1:
            acc_ref[...] = z
        else:
            acc_ref[...] += z
        y = y_next
    acc_ref[...] = (acc_ref[...] + second(n - 1, y)) * scale
    core = me_ref[0] % 2
    keep_ref[...] = acc_ref[pl.ds(pl.multiple_of(core * half, 8), half), :]
    send_ref[...] = acc_ref[pl.ds(pl.multiple_of((1 - core) * half, 8), half), :]


def sketch_share(me, sketch_t, cache_keys, length):
    seq_len, width = cache_keys.shape
    rank = sketch_t.shape[0]
    chunk = min(512, seq_len)
    half = jax.ShapeDtypeStruct((rank // 2, width), F32)
    return pl.pallas_call(
        functools.partial(sketch_kernel, scale=1.0 / length, chunk=chunk),
        in_specs=[smem(), hbm(), hbm()],
        out_specs=[vmem(), vmem()],
        out_shape=[half, half],
        scratch_shapes=[
            pltpu.VMEM((rank, width), F32),
            pltpu.VMEM((seq_len, width), BF),
            pltpu.VMEM((rank, width), F32),
            pltpu.SemaphoreType.DMA,
            pltpu.SemaphoreType.DMA((seq_len // chunk,)),
        ],
        compiler_params=pltpu.CompilerParams(vmem_limit_bytes=24 << 20),
        name="sketch_share",
    )(me, in_hbm(sketch_t), in_hbm(cache_keys))


class Lists:
    def __init__(self, me_ref, chosen_ref, begin_ref, count_ref, outl_ref, spans, most=None):
        self.chosen, self.begin, self.counts, self.outl = chosen_ref, begin_ref, count_ref, outl_ref
        self.spans, self.most = spans, most
        self.base = me_ref[0] * spans

    def span(self, t, g, slot):
        i = t * KVH + g
        last = self.chosen.shape[1] - 1
        picked = self.chosen[i, jnp.minimum(self.begin[t, g] + slot, last)]
        return jnp.clip(picked - self.base, 0, self.spans - 1)

    def count(self, t, g):
        return jnp.minimum(self.counts[t, g], self.most)

    def starts(self, g, steps):
        at = [jnp.int32(0)]
        for t in range(steps):
            at.append(at[-1] + self.count(t, g))
        return at

    def outliers(self):
        n = self.outl.shape[0]
        first = jnp.int32(0)
        here = jnp.int32(0)
        for i in range(n):
            s = self.outl[i]
            first = first + (s < self.base).astype(jnp.int32)
            here = here + ((s >= self.base) & (s < self.base + self.spans)).astype(jnp.int32)
        found = [
            jnp.clip(self.outl[jnp.minimum(first + j, n - 1)] - self.base, 0, self.spans - 1) for j in range(OMOST)
        ]
        return jnp.minimum(here, OMOST), found

    def find(self, g, steps, put):
        at = self.starts(g, steps)
        for t in range(steps):
            def part(k, _, t=t):
                found = [self.span(t, g, k * PART + j) for j in range(PART)]
                for j in range(PART):
                    put(at[t] + (k * PART + j), found[j])
                return 0

            for k in range(2):
                part(k, 0)
            lax.fori_loop(2, (self.count(t, g) + PART - 1) // PART, part, 0)
        for j in range(PART):
            put(at[steps] + j, 0)


def each_part(slots_ref, g, total, parts_all, spans, copy):
    def part(k, _):
        copy([jnp.clip(slots_ref[g, k * PART + j], 0, spans - 1) for j in range(PART)], k * PART)
        return 0

    straight = min(STRAIGHT, parts_all)
    for k in range(straight):
        part(k, 0)
    lax.fori_loop(straight, (total + PART - 1) // PART, part, 0)


def slots_kernel(me_ref, chosen_ref, begin_ref, count_ref, after_ref, slots_ref, tie_ref, *, spans, most):
    steps = begin_ref.shape[0]
    tie_ref[...] = jnp.zeros_like(tie_ref)
    lists = Lists(me_ref, chosen_ref, begin_ref, count_ref, None, spans, most)
    for g in range(slots_ref.shape[0]):
        def put(slot, span, g=g):
            slots_ref[g, slot] = span

        lists.find(g, steps, put)


def known_kernel(
    me_ref, chosen_ref, begin_ref, count_ref, outl_ref, q_ref, fk_ref, ca_ref, sa_ref, cb_ref, sb_ref, cq_ref, sq_ref, keys_hbm, after_ref,
    slots_ref, kx_ref, w_ref, tie_ref,
    okeys_ref, xtmp_ref, qtmp_ref, osem, *, per_device, rp, spans, most
):
    steps = q_ref.shape[0]
    tie_ref[...] = jnp.zeros_like(tie_ref)
    lists = Lists(me_ref, chosen_ref, begin_ref, count_ref, outl_ref, spans, most)
    _, o_span = lists.outliers()
    o_copies = [
        pltpu.make_async_copy(
            keys_hbm.at[pl.ds(pl.multiple_of(o_span[j] // 2 * 16, 16), 16)], okeys_ref.at[j], osem.at[j]
        )
        for j in range(OMOST)
    ]
    for c in o_copies:
        c.start()

    lane = lax.broadcasted_iota(jnp.int32, (8, LANES), 1)
    sign = jnp.where(lane < HD // 2, -1.0, 1.0)

    qtmp_ref[...] = jnp.zeros_like(qtmp_ref)
    for t in range(steps):
        x = q_ref[t:t + 1, :].astype(F32)
        for h in range(QH):
            r = h // per_device * rp + t * per_device + h % per_device
            qtmp_ref[r:r + 1, :] = x[:, h * HD:(h + 1) * HD]
    scale = 1.0 / (HD ** 0.5)
    row = lax.broadcasted_iota(jnp.int32, (LANES, LANES), 0) % rp
    lane_r = lax.broadcasted_iota(jnp.int32, (LANES, LANES), 1)
    cq = jnp.zeros((LANES, LANES), F32)
    sq = jnp.zeros((LANES, LANES), F32)
    for t in range(steps):
        here = (row >= t * per_device) & (row < (t + 1) * per_device)
        cq = jnp.where(here, cq_ref[t:t + 1, :] * scale, cq)
        sq = jnp.where(here, sq_ref[t:t + 1, :] * scale, sq)
    sq = jnp.where(lane_r < HD // 2, -sq, sq)
    for pk in range(w_ref.shape[0]):
        x = qtmp_ref[pk * LANES:(pk + 1) * LANES, :]
        x = x * cq + pltpu.roll(x, HD // 2, 1) * sq
        z = jnp.where(lane_r < HD // 2, 1.0, -1.0) * pltpu.roll(x, HD // 2, 1)
        hi, lo = split2(jnp.concatenate([x.T, z.T], 0))
        w_ref[pk] = jnp.concatenate([hi, lo], 0)

    for i in range(slots_ref.shape[0]):
        def put(slot, span, i=i):
            slots_ref[i, slot] = span

        lists.find(KVH - slots_ref.shape[0] + i, steps, put)

    blk = cb_ref.shape[0] // SPAN
    turns = []
    for j in range(OMOST):
        a = o_span[j] // blk
        b = pl.ds(pl.multiple_of(o_span[j] % blk * SPAN, SPAN), SPAN)
        ca, sa = ca_ref[pl.ds(a, 1), :], sa_ref[pl.ds(a, 1), :]
        cb, sb = cb_ref[b, :], sb_ref[b, :]
        turns.append((ca * cb - sa * sb, (sa * cb + ca * sb) * sign))
    for c in o_copies:
        c.wait()
    x_rows = kx_ref.shape[1]
    xtmp_ref[...] = jnp.zeros_like(xtmp_ref)
    fs = sq_ref[:steps, :] * sign[:1]
    for g in range(KVH):
        sl = slice(g * HD, (g + 1) * HD)
        for j in range(OMOST):
            wide = okeys_ref[j, :, sl].astype(F32)
            x = jnp.where(o_span[j] % 2 == 0, wide[:8], wide[8:])
            xtmp_ref[j * SPAN:(j + 1) * SPAN, :] = x * turns[j][0] + pltpu.roll(x, HD // 2, 1) * turns[j][1]
        x = fk_ref[:, sl].astype(F32)
        o = OMOST * SPAN
        xtmp_ref[o:o + steps, :] = x * cq_ref[:steps, :] + pltpu.roll(x, HD // 2, 1) * fs
        kx_ref[g, :, :HD] = xtmp_ref[...].astype(BF)
        kx_ref[g, :, HD:] = jnp.zeros((x_rows, HD), BF)


def values_kernel(
    me_ref, count_ref, outl_ref, slotsa_ref, slotsb_ref, fv_ref, values_hbm, after_ref, vg_ref, tie_ref,
    values_ref, vtmp_ref, sem, *, main, most
):
    steps = fv_ref.shape[0]
    rows_all = vtmp_ref.shape[0]
    n = vg_ref.shape[0]
    copies = [
        pltpu.make_async_copy(values_hbm.at[:, pl.ds(i * HD, HD)], values_ref.at[i], sem.at[i]) for i in range(n)
    ]
    for c in copies[:2]:
        c.start()
    tie_ref[...] = jnp.zeros_like(tie_ref)
    vtmp_ref[...] = jnp.zeros_like(vtmp_ref)
    spans = values_ref.shape[1] // SPAN
    lists = Lists(me_ref, None, None, count_ref, outl_ref, spans, most)
    _, o_span = lists.outliers()

    for i in range(n):
        def rows_of(span, i=i):
            wide = values_ref[i, pl.ds(pl.multiple_of(span // 2 * 16, 16), 16), :].astype(F32)
            return jnp.where(span % 2 == 0, wide[:8], wide[8:])

        def put(spans, slot, rows_of=rows_of):
            dst = pl.ds(pl.multiple_of(LANES + slot * SPAN, SPAN), PART * SPAN)
            vtmp_ref[dst, :] = jnp.concatenate([rows_of(span) for span in spans], 0)

        copies[i].wait()
        if i + 2 < n:
            copies[i + 2].start()
        for j in range(OMOST):
            vtmp_ref[j * SPAN:(j + 1) * SPAN, :] = rows_of(o_span[j])
        vtmp_ref[OMOST * SPAN:OMOST * SPAN + steps, :] = fv_ref[:, i * HD:(i + 1) * HD].astype(F32)
        total = lists.starts(i, steps)[steps]
        early = slotsa_ref.shape[0]
        held, h = (slotsa_ref, i) if i < early else (slotsb_ref, i - early)
        each_part(held, h, total, (rows_all - LANES) // (PART * SPAN), spans, put)
        vg_ref[i, :LANES + main, :] = vtmp_ref[:LANES + main, :].astype(BF)
        if LANES + main < rows_all:
            def more(k, _, i=i):
                at = pl.ds(pl.multiple_of(LANES + main + k * LANES, LANES), LANES)
                vg_ref[i, at, :] = vtmp_ref[at, :].astype(BF)
                return 0

            lax.fori_loop(0, (jnp.maximum(total * SPAN - main, 0) + LANES - 1) // LANES, more, 0)


def attend_kernel(
    me_ref, count_ref, outl_ref, slotsa_ref, slotsb_ref, zmine_ref, zother_ref, kx_ref, w_ref, vg_ref,
    ca_ref, sa_ref, cb_ref, sb_ref, keys_hbm,
    kft_hbm, out_ref,
    keys_ref, z_ref, a_ref, qt_ref, kf_ref, kft_ref, kg_ref, cg_ref, sg_ref, sc_ref, cc_ref, ss_ref, acc_ref,
    sem, out_sem, *, per_device, steps, main, most, stop=9
):
    rank, width = z_ref.shape
    half = rank // 2
    seq_len = keys_ref.shape[0]
    load = pltpu.make_async_copy(keys_hbm, keys_ref, sem)
    load.start()

    core = me_ref[0] % 2
    z_ref[pl.ds(pl.multiple_of(core * half, 16), half), :] = zmine_ref[...]
    z_ref[pl.ds(pl.multiple_of((1 - core) * half, 16), half), :] = zother_ref[...]
    turn_tables(ca_ref, sa_ref, cb_ref, sb_ref, cc_ref, ss_ref)
    basis(z_ref, a_ref, qt_ref)
    qt = qt_ref[...]

    load.wait()
    if stop == 1:
        return
    chunk = seq_len // KVH
    for i in range(KVH):
        rows = slice(i * chunk, (i + 1) * chunk)
        kf = lax.dot_general(keys_ref[rows, :], qt, NT, preferred_element_type=F32)
        kf_ref[rows, :] = kf
        kft_ref[:, rows] = kf.T
    store = pltpu.make_async_copy(kft_ref, kft_hbm, out_sem)
    store.start()
    if stop == 2:
        store.wait()
        return

    spans = seq_len // SPAN
    lists = Lists(me_ref, None, None, count_ref, outl_ref, spans, most)
    starts = []
    for g in range(KVH):
        def gather(spans, slot, g=g):
            got = []
            for span in spans:
                src = pl.ds(pl.multiple_of(span * SPAN, SPAN), SPAN)
                got.append((kf_ref[src, :], cc_ref[src, :], ss_ref[src, :]))
            dst = pl.ds(pl.multiple_of(slot * SPAN, SPAN), PART * SPAN)
            for ref, rows in zip((kg_ref, cg_ref, sg_ref), zip(*got)):
                ref[g, dst, :] = jnp.concatenate(rows, 0)

        starts.append(lists.starts(g, steps))
        early = slotsa_ref.shape[0]
        held, h = (slotsa_ref, g) if g < early else (slotsb_ref, g - early)
        each_part(held, h, starts[g][steps], kg_ref.shape[1] // (PART * SPAN), spans, gather)
    totals = [at[steps] for at in starts]

    if stop == 3:
        store.wait()
        return

    n_dest, rp, _ = out_ref.shape
    dests = n_dest // KVH
    qr = dests * rp
    heads = LANES // qr
    packs = w_ref.shape[0]
    o_live = lists.outliers()[0] * SPAN
    first_shard = me_ref[0] == 0
    column = lax.broadcasted_iota(jnp.int32, (8, LANES), 1)[:1]
    col_head = column // qr
    col_row = column % rp
    col_step = col_row // per_device

    def bounds(pk, h):
        first = jnp.full((1, LANES), 1 << 30, jnp.int32)
        last = jnp.zeros((1, LANES), jnp.int32)
        for t in range(steps):
            at = starts[pk * heads + h]
            here = (col_head == h) & (col_step == t)
            first = jnp.where(here, at[t] * SPAN, first)
            last = jnp.where(here, at[t + 1] * SPAN, last)
        return first, last

    def product(pk, y):
        r = jnp.dot(y, w_ref[pk, :2 * HD, :], preferred_element_type=F32)
        return r + jnp.dot(y, w_ref[pk, 2 * HD:, :], preferred_element_type=F32)

    token = lax.broadcasted_iota(jnp.int32, (LANES, LANES), 0)

    def slot_scores(pk, at, n, limits):
        rows = pl.ds(at, n)
        ys = []
        for h in range(heads):
            g = pk * heads + h
            x = jnp.dot(kg_ref[g, rows, :].astype(BF), qt_ref[:, g * HD:(g + 1) * HD], preferred_element_type=F32)
            ys.append(jnp.concatenate([(x * cg_ref[g, rows, :]).astype(BF), (x * sg_ref[g, rows, :]).astype(BF)], 1))
        r = product(pk, jnp.concatenate(ys, 0))
        s = jnp.full((n, LANES), DEAD, F32)
        here = lax.broadcasted_iota(jnp.int32, (n, LANES), 0) + at
        for h in range(heads):
            first, last = limits[h]
            s = jnp.where((here >= first) & (here < last), r[h * n:(h + 1) * n], s)
        return s

    def known_scores(pk):
        s = jnp.full((LANES, LANES), DEAD, F32)
        new = token - OMOST * SPAN
        is_live = (token < o_live) | (first_shard & (new >= 0) & (new <= col_step))
        is_live = is_live & (new < steps) & (col_row < steps * per_device)
        r = product(pk, kx_ref[pk * heads:(pk + 1) * heads].reshape(heads * LANES, 2 * HD))
        for h in range(heads):
            s = jnp.where(is_live & (col_head == h), r[h * LANES:(h + 1) * LANES], s)
        return s

    limits = [[bounds(pk, h) for h in range(heads)] for pk in range(packs)]
    extra = kg_ref.shape[1] - main
    blocks = []
    for pk in range(packs):
        longest = functools.reduce(jnp.maximum, totals[pk * heads:(pk + 1) * heads])
        blocks.append((jnp.maximum(longest * SPAN - main, 0) + LANES - 1) // LANES)

    tops = []
    for pk in range(packs):
        s = known_scores(pk)
        sc_ref[pk, :LANES, :] = s
        top = jnp.max(s, axis=0, keepdims=True)
        s = slot_scores(pk, 0, main, limits[pk])
        sc_ref[pk, LANES:LANES + main, :] = s
        tops.append(jnp.maximum(top, jnp.max(s, axis=0, keepdims=True)))
    if extra > 0:
        for pk in range(packs):
            def more(k, top, pk=pk):
                at = pl.multiple_of(main + k * LANES, LANES)
                s = slot_scores(pk, at, LANES, limits[pk])
                sc_ref[pk, pl.ds(pl.multiple_of(LANES + at, LANES), LANES), :] = s
                return jnp.maximum(top, jnp.max(s, axis=0, keepdims=True))

            tops[pk] = lax.fori_loop(0, blocks[pk], more, tops[pk])
    if stop == 4:
        store.wait()
        return

    used = steps * per_device

    def weights(s, top):
        return jnp.where(s > 0.5 * DEAD, jnp.exp(s - top), 0.0)

    def weighted(pt, h, values):
        hi, lo = split2(pt[h * qr:(h + 1) * qr, :])
        r = jnp.dot(jnp.concatenate([hi, lo], 0), values, preferred_element_type=F32)
        return r[:qr] + r[qr:]

    sums = []
    for pk in range(packs):
        pts = []
        total = jnp.zeros((LANES, LANES), F32)
        for at in range(0, LANES + main, LANES):
            p = weights(sc_ref[pk, at:at + LANES, :], tops[pk])
            total = total + p
            pts.append(p.T)
        sums.append(jnp.sum(total, axis=0, keepdims=True))
        pt = jnp.concatenate(pts, 1)
        for h in range(heads):
            g = pk * heads + h
            acc = weighted(pt, h, vg_ref[g, :LANES + main, :])
            for a in range(dests):
                acc_ref[g * dests + a] = acc[a * rp:(a + 1) * rp]
    if extra > 0:
        for pk in range(packs):
            def add(k, total, pk=pk):
                at = pl.multiple_of(LANES + main + k * LANES, LANES)
                p = weights(sc_ref[pk, pl.ds(at, LANES), :], tops[pk])
                pt = p.T
                for h in range(heads):
                    g = pk * heads + h

                    @pl.when(totals[g] * SPAN > main + k * LANES)
                    def _():
                        acc = weighted(pt, h, vg_ref[g, pl.ds(at, LANES), :])
                        for a in range(dests):
                            acc_ref[g * dests + a] += acc[a * rp:(a + 1) * rp]

                return total + jnp.sum(p, axis=0, keepdims=True)

            sums[pk] = lax.fori_loop(0, blocks[pk], add, sums[pk])
    for d in range(n_dest):
        pk = d // (heads * dests)
        row = lax.broadcasted_iota(jnp.int32, (rp, LANES), 0)
        r = acc_ref[d]
        for k, extra_row in enumerate((*split3(tops[pk]), sums[pk])):
            r = jnp.where(row == used + k, extra_row, r)
        out_ref[d] = r.astype(BF)
    store.wait()


def turn_tables(ca_ref, sa_ref, cb_ref, sb_ref, cc_ref, ss_ref):
    blk = cb_ref.shape[0]
    cb = cb_ref[...]
    sb = sb_ref[...]
    for a in range(cc_ref.shape[0] // blk):
        ca = ca_ref[a:a + 1, :]
        sa = sa_ref[a:a + 1, :]
        cc_ref[a * blk:(a + 1) * blk, :] = ca * cb - sa * sb
        ss_ref[a * blk:(a + 1) * blk, :] = sa * cb + ca * sb


def basis(z_ref, a_ref, qt_ref):
    rank = z_ref.shape[0]
    wide = round_up(rank, LANES)
    z = z_ref[...]
    c = lax.dot_general(z, z, NT, preferred_element_type=F32)
    rows = lax.broadcasted_iota(jnp.int32, (rank, wide), 0)
    cols = lax.broadcasted_iota(jnp.int32, (rank, wide), 1)
    a_ref[:, :wide] = jnp.where(rows == cols, 1.0, 0.0)
    a_ref[:, wide:wide + rank] = c
    a_ref[:, wide + rank:] = jnp.zeros((rank, wide - rank), F32)
    nb = 32
    half_tiles = wide // LANES
    for j0 in range(0, rank, nb):
        tiles = [t for t in range(half_tiles) if t * LANES < j0 + nb]
        tiles += [half_tiles + t for t in range(half_tiles) if (t + 1) * LANES > j0]
        part = {t: a_ref[j0:j0 + nb, t * LANES:(t + 1) * LANES] for t in tiles}
        row = lax.broadcasted_iota(jnp.int32, (nb, LANES), 0)
        column = []
        for j in range(nb):
            t, o = divmod(j0 + j, LANES)
            column.append(jnp.broadcast_to(part[half_tiles + t][:, o:o + 1], (nb, LANES)))
        for j in range(nb):
            inverse = lax.rsqrt(jnp.broadcast_to(column[j][j:j + 1, :], (nb, LANES)))
            low = jnp.where(row > j, column[j] * inverse, 0.0)
            for k in range(j + 1, nb):
                column[k] = column[k] - low * jnp.broadcast_to(low[k:k + 1, :], (nb, LANES))
            for t in tiles:
                upper = jnp.broadcast_to(part[t][j:j + 1, :], (nb, LANES)) * inverse
                part[t] = jnp.where(row == j, upper, part[t] - low * upper)
        for t in tiles:
            a_ref[j0:j0 + nb, t * LANES:(t + 1) * LANES] = part[t]
        if j0 + nb < rank:
            upper = jnp.concatenate(
                [part[t] if t in part else jnp.zeros((nb, LANES), F32) for t in range(2 * half_tiles)], 1
            )
            h, m, l = split3(upper)
            left = jnp.concatenate([h, h, m, m, h, l], 0)[:, wide:].astype(BF)
            right = jnp.concatenate([h, m, h, m, l, h], 0).astype(BF)
            for s in range(2):
                d = lax.dot_general(left, right[:, s * wide:(s + 1) * wide], TN, preferred_element_type=F32)
                a_ref[j0 + nb:, s * wide:(s + 1) * wide] -= d[j0 + nb:rank]
    h, m, _ = split3(a_ref[:, :rank])
    q = jnp.dot(jnp.concatenate([h, m], 0).astype(BF), z, preferred_element_type=F32)
    qt_ref[...] = (q[:rank] + q[rank:]).astype(BF)


def attend_call(
    me, lists, z, z_other, kx, w, vg, ca, sa, cb, sb, cache_keys,
    *, steps, per_device, main, most, rp, n_dest, stop=9
):
    seq_len, width = cache_keys.shape
    rank = 2 * z.shape[0]
    tok_all = vg.shape[1] - LANES
    return pl.pallas_call(
        functools.partial(attend_kernel, per_device=per_device, steps=steps, main=main, most=most, stop=stop),
        in_specs=[smem()] * 5 + [vmem()] * 9 + [hbm()],
        out_specs=[hbm(), vmem()],
        out_shape=[
            jax.ShapeDtypeStruct((rank, seq_len), F32),
            jax.ShapeDtypeStruct((n_dest, rp, HD), BF),
        ],
        scratch_shapes=[
            pltpu.VMEM((seq_len, width), BF),
            pltpu.VMEM((rank, width), BF),
            pltpu.VMEM((rank, 2 * round_up(rank, LANES)), F32),
            pltpu.VMEM((rank, width), BF),
            pltpu.VMEM((seq_len, rank), F32),
            pltpu.VMEM((rank, seq_len), F32),
            pltpu.VMEM((KVH, tok_all, rank), F32),
            pltpu.VMEM((KVH, tok_all, HD), F32),
            pltpu.VMEM((KVH, tok_all, HD), F32),
            pltpu.VMEM((w.shape[0], LANES + tok_all, LANES), F32),
            pltpu.VMEM((seq_len, HD), F32),
            pltpu.VMEM((seq_len, HD), F32),
            pltpu.VMEM((n_dest, rp, HD), F32),
            pltpu.SemaphoreType.DMA,
            pltpu.SemaphoreType.DMA,
        ],
        compiler_params=pltpu.CompilerParams(vmem_limit_bytes=42 << 20),
        name="attend",
    )(me, *lists, z, z_other, kx, w, vg, ca, sa, cb, sb, in_hbm(cache_keys))


def merge_kernel(me_ref, parts_ref, out_ref, top_ref, sum_ref, *, steps, per_device):
    n, rp, _ = parts_ref.shape
    used = steps * per_device
    parts = parts_ref[...].astype(F32)
    rows = pl.ds(pl.multiple_of(me_ref[0] % (LANES // rp) * rp, 8), rp)
    top_ref[...] = (parts[:, used, :] + parts[:, used + 1, :] + parts[:, used + 2, :]).T
    sum_ref[...] = parts[:, used + 3, :].T
    tops = top_ref[rows, :]
    w = jnp.exp(tops - jnp.max(tops, axis=1, keepdims=True))
    w = w / jnp.sum(w * sum_ref[rows, :], axis=1, keepdims=True)
    o = jnp.zeros((rp, HD), F32)
    for s in range(n):
        o = o + w[:, s:s + 1] * parts[s]
    for t in range(steps):
        for i in range(per_device):
            r = t * per_device + i
            out_ref[t:t + 1, i * HD:(i + 1) * HD] = o[r:r + 1, :].astype(BF)


def swap(x, moves):
    return lax.ppermute(x, "seq", moves)


def on_device(
    cache_keys,
    cache_values,
    sketch_matrix,
    queries,
    fresh_keys,
    fresh_values,
    chosen,
    shard_counts,
    outliers,
):
    seq_len, width = cache_keys.shape
    devices = lax.axis_size("seq")
    myself = lax.axis_index("seq")
    length = seq_len * devices
    steps = queries.shape[0]
    rank = sketch_matrix.shape[1]
    per_device = QH // devices
    n_lists = steps * KVH
    most = 3 * chosen.shape[2] // devices
    slots_all = round_up(max(steps * most, steps * STRAIGHT * PART), LANES // SPAN)
    tok_all = slots_all * SPAN
    main = min(MAIN, tok_all)
    used = steps * per_device
    rp = round_up(used + 4, 16)
    n_dest = devices
    me = jnp.full((1,), myself, jnp.int32)

    keep, send = sketch_share(me, sketch_matrix.T, cache_keys, length)

    half_width = HD // 2
    exponents = jnp.arange(half_width, dtype=F32) * (2.0 / HD)
    inverse_freq = jnp.exp(-jnp.log(F32(500000.0)) * exponents)
    inverse_freq = jnp.concatenate([inverse_freq, inverse_freq])
    blk = 64
    coarse = (myself * seq_len + blk * jnp.arange(seq_len // blk, dtype=jnp.int32)).astype(F32)[:, None] * inverse_freq
    fine = jnp.arange(blk, dtype=jnp.int32).astype(F32)[:, None] * inverse_freq
    late = (length + jnp.arange(steps, dtype=jnp.int32)).astype(F32)[:, None] * inverse_freq
    turns = (jnp.cos(coarse), jnp.sin(coarse), jnp.cos(fine), jnp.sin(fine))

    shard = jnp.arange(devices, dtype=jnp.int32)
    begin = jnp.sum(jnp.where(shard < myself, shard_counts, 0), axis=2)
    count = jnp.sum(jnp.where(shard == myself, shard_counts, 0), axis=2)
    lists = (chosen.reshape(n_lists, -1), begin, count)
    places = slots_all + 4 * PART
    tie_shape = jax.ShapeDtypeStruct((1, LANES), F32)

    def early_slots(after):
        return pl.pallas_call(
            functools.partial(slots_kernel, spans=seq_len // SPAN, most=most),
            in_specs=[smem()] * 4 + [anywhere()],
            out_specs=[smem(), vmem()],
            out_shape=[jax.ShapeDtypeStruct((EARLY, places), jnp.int32), tie_shape],
            name="early_slots",
        )(me, *lists, after)

    def known(after):
        return pl.pallas_call(
            functools.partial(known_kernel, per_device=per_device, rp=rp, spans=seq_len // SPAN, most=most),
            in_specs=[smem()] * 5 + [vmem()] * 8 + [hbm(), anywhere()],
            out_specs=[smem()] + [vmem()] * 3,
            out_shape=[
                jax.ShapeDtypeStruct((KVH - EARLY, places), jnp.int32),
                jax.ShapeDtypeStruct((KVH, LANES, 2 * HD), BF),
                jax.ShapeDtypeStruct((n_dest * rp // LANES, 4 * HD, LANES), BF),
                tie_shape,
            ],
            scratch_shapes=[
                pltpu.VMEM((OMOST, 16, width), BF),
                pltpu.VMEM((LANES, HD), F32),
                pltpu.VMEM((n_dest * rp, HD), F32),
                pltpu.SemaphoreType.DMA((OMOST,)),
            ],
            compiler_params=pltpu.CompilerParams(vmem_limit_bytes=8 << 20),
            name="known_keys",
        )(me, *lists, outliers, queries, fresh_keys, *turns, jnp.cos(late), jnp.sin(late), in_hbm(cache_keys), after)

    def slot_values(held, after):
        return pl.pallas_call(
            functools.partial(values_kernel, main=main, most=most),
            in_specs=[smem()] * 5 + [vmem(), hbm(), anywhere()],
            out_specs=[vmem()] * 2,
            out_shape=[jax.ShapeDtypeStruct((KVH, LANES + tok_all, HD), BF), tie_shape],
            scratch_shapes=[
                pltpu.VMEM((KVH, seq_len, HD), BF),
                pltpu.VMEM((LANES + tok_all, HD), F32),
                pltpu.SemaphoreType.DMA((KVH,)),
            ],
            compiler_params=pltpu.CompilerParams(vmem_limit_bytes=16 << 20),
            name="slot_values",
        )(me, *held, fresh_values, in_hbm(cache_values), after)

    z = keep + swap(send, [(i, i ^ 1) for i in range(devices)])
    hops = [1 << k for k in range(1, devices.bit_length() - 1)]
    for k in range(len(hops)):
        other = k ^ 1 if k < 2 and len(hops) >= 2 else k
        moves = [(i, i ^ hops[k if i % 2 == 0 else other]) for i in range(devices)]
        going = z.astype(BF)
        came = swap(going, moves).astype(F32)
        if k == 0:
            slots_a, tie = early_slots(going)
            came = came + tie[0, 0]
        if k == min(1, len(hops) - 1):
            slots_b, kx, w, tie = known(going)
            came = came + tie[0, 0]
        if k == len(hops) - 1:
            held = (count, outliers, slots_a, slots_b)
            vg, tie = slot_values(held, going)
            came = came + tie[0, 0]
        z = z + came
    z = z.astype(BF)
    z_other = swap(z, [(i, i ^ 1) for i in range(devices)])

    kft, parts = attend_call(
        me, held, z, z_other, kx, w, vg, *turns, cache_keys,
        steps=steps, per_device=per_device, main=main, most=most, rp=rp, n_dest=n_dest,
    )
    parts = lax.all_to_all(parts, "seq", 0, 0, tiled=True)
    attended = pl.pallas_call(
        functools.partial(merge_kernel, steps=steps, per_device=per_device),
        in_specs=[smem(), vmem()],
        out_specs=vmem(),
        out_shape=jax.ShapeDtypeStruct((steps, per_device * HD), BF),
        scratch_shapes=[pltpu.VMEM((LANES, devices), F32)] * 2,
        name="merge",
    )(me, parts)
    return (attended, kft.T)


def solution(mesh):
    in_specs = (
        P(("groups", "seq"), None),
        P(("groups", "seq"), None),
        P(),
        P("groups", None),
        P("groups", None),
        P("groups", None),
        P("groups", None, None),
        P("groups", None, None),
        P("groups"),
    )
    out_specs = (P("groups", "seq"), P(("groups", "seq"), None))
    return jax.shard_map(
        on_device, mesh=mesh, in_specs=in_specs, out_specs=out_specs, check_vma=False
    )
```

```python
import functools

import jax
import jax.numpy as jnp
from jax import lax
from jax.experimental import pallas as pl
from jax.experimental.pallas import tpu as pltpu
from jax.sharding import PartitionSpec as P

KVH = 8
HD = 128
QH = 64
SPAN = 8
OMOST = 4
BF = jnp.bfloat16
F32 = jnp.float32
DEAD = -1e30
LANES = 128
MAIN = 896
ROWS = 512
PART = 8
STRAIGHT = 6
EARLY = 3
AHEAD = 3
NT = (((1,), (1,)), ((), ()))
TN = (((0,), (0,)), ((), ()))


def vmem():
    return pl.BlockSpec(memory_space=pltpu.VMEM)


def smem():
    return pl.BlockSpec(memory_space=pltpu.SMEM)


def hbm():
    return pl.BlockSpec(memory_space=pltpu.HBM)


def in_hbm(x):
    return pltpu.with_memory_space_constraint(x, pltpu.HBM)


def anywhere():
    return pl.BlockSpec(memory_space=pl.ANY)


def round_up(x, m):
    return (x + m - 1) // m * m


def split2(x):
    high = x.astype(BF)
    return high, (x - high.astype(F32)).astype(BF)


def split3(x):
    high = x.astype(BF).astype(F32)
    rest = x - high
    middle = rest.astype(BF).astype(F32)
    return high, middle, rest - middle


def sketch_kernel(
    me_ref, st_hbm, keys_hbm, keep_ref, send_ref, st_ref, keys_ref, acc_ref, st_sem, sem, *, scale, chunk
):
    seq_len = keys_ref.shape[0]
    rank = st_ref.shape[0]
    half = rank // 2
    n = seq_len // chunk
    st_copy = pltpu.make_async_copy(st_hbm, st_ref, st_sem)
    st_copy.start()
    copies = [
        pltpu.make_async_copy(
            keys_hbm.at[pl.ds(i * chunk, chunk)], keys_ref.at[pl.ds(i * chunk, chunk)], sem.at[i]
        )
        for i in range(n)
    ]
    for c in copies[:AHEAD]:
        c.start()
    st_copy.wait()
    st = st_ref[...].astype(BF)

    def rows(i):
        return keys_ref[i * chunk:(i + 1) * chunk, :]

    def first(i):
        return lax.dot_general(st, rows(i), NT, preferred_element_type=F32).astype(BF)

    def second(i, y):
        return jnp.dot(y, rows(i), preferred_element_type=F32)

    def arrive(i):
        copies[i].wait()
        if i + AHEAD < n:
            copies[i + AHEAD].start()

    arrive(0)
    y = first(0)
    for i in range(1, n):
        arrive(i)
        y_next = first(i)
        z = second(i - 1, y)
        if i == 1:
            acc_ref[...] = z
        else:
            acc_ref[...] += z
        y = y_next
    acc_ref[...] = (acc_ref[...] + second(n - 1, y)) * scale
    core = me_ref[0] % 2
    keep_ref[...] = acc_ref[pl.ds(pl.multiple_of(core * half, 8), half), :]
    send_ref[...] = acc_ref[pl.ds(pl.multiple_of((1 - core) * half, 8), half), :]


def sketch_share(me, sketch_t, cache_keys, length):
    seq_len, width = cache_keys.shape
    rank = sketch_t.shape[0]
    chunk = min(512, seq_len)
    half = jax.ShapeDtypeStruct((rank // 2, width), F32)
    return pl.pallas_call(
        functools.partial(sketch_kernel, scale=1.0 / length, chunk=chunk),
        in_specs=[smem(), hbm(), hbm()],
        out_specs=[vmem(), vmem()],
        out_shape=[half, half],
        scratch_shapes=[
            pltpu.VMEM((rank, width), F32),
            pltpu.VMEM((seq_len, width), BF),
            pltpu.VMEM((rank, width), F32),
            pltpu.SemaphoreType.DMA,
            pltpu.SemaphoreType.DMA((seq_len // chunk,)),
        ],
        compiler_params=pltpu.CompilerParams(vmem_limit_bytes=24 << 20),
        name="sketch_share",
    )(me, in_hbm(sketch_t), in_hbm(cache_keys))


class Lists:
    def __init__(self, me_ref, chosen_ref, begin_ref, count_ref, outl_ref, spans, most=None):
        self.chosen, self.begin, self.counts, self.outl = chosen_ref, begin_ref, count_ref, outl_ref
        self.spans, self.most = spans, most
        self.base = me_ref[0] * spans

    def span(self, t, g, slot):
        i = t * KVH + g
        last = self.chosen.shape[1] - 1
        picked = self.chosen[i, jnp.minimum(self.begin[t, g] + slot, last)]
        return jnp.clip(picked - self.base, 0, self.spans - 1)

    def count(self, t, g):
        return jnp.minimum(self.counts[t, g], self.most)

    def starts(self, g, steps):
        at = [jnp.int32(0)]
        for t in range(steps):
            at.append(at[-1] + self.count(t, g))
        return at

    def outliers(self):
        n = self.outl.shape[0]
        first = jnp.int32(0)
        here = jnp.int32(0)
        for i in range(n):
            s = self.outl[i]
            first = first + (s < self.base).astype(jnp.int32)
            here = here + ((s >= self.base) & (s < self.base + self.spans)).astype(jnp.int32)
        found = [
            jnp.clip(self.outl[jnp.minimum(first + j, n - 1)] - self.base, 0, self.spans - 1) for j in range(OMOST)
        ]
        return jnp.minimum(here, OMOST), found

    def find(self, g, steps, copy):
        at = self.starts(g, steps)
        for t in range(steps):
            def part(k, _, t=t):
                copy([self.span(t, g, k * PART + j) for j in range(PART)], at[t] + k * PART)
                return 0

            for k in range(2):
                part(k, 0)
            lax.fori_loop(2, (self.count(t, g) + PART - 1) // PART, part, 0)
        return at


def each_part(slots_ref, g, total, parts_all, spans, copy):
    def part(k, _):
        copy([jnp.clip(slots_ref[g, k * PART + j], 0, spans - 1) for j in range(PART)], k * PART)
        return 0

    straight = min(STRAIGHT, parts_all)
    for k in range(straight):
        part(k, 0)
    lax.fori_loop(straight, (total + PART - 1) // PART, part, 0)


def known_kernel(
    me_ref, outl_ref, q_ref, fk_ref, ca_ref, sa_ref, cb_ref, sb_ref, cq_ref, sq_ref, keys_hbm, after_ref,
    kx_ref, w_ref, tie_ref,
    okeys_ref, xtmp_ref, qtmp_ref, osem, *, per_device, rp, spans
):
    steps = q_ref.shape[0]
    tie_ref[...] = jnp.zeros_like(tie_ref)
    _, o_span = Lists(me_ref, None, None, None, outl_ref, spans).outliers()
    o_copies = [
        pltpu.make_async_copy(
            keys_hbm.at[pl.ds(pl.multiple_of(o_span[j] // 2 * 16, 16), 16)], okeys_ref.at[j], osem.at[j]
        )
        for j in range(OMOST)
    ]
    for c in o_copies:
        c.start()

    lane = lax.broadcasted_iota(jnp.int32, (8, LANES), 1)
    sign = jnp.where(lane < HD // 2, -1.0, 1.0)

    qtmp_ref[...] = jnp.zeros_like(qtmp_ref)
    for t in range(steps):
        x = q_ref[t:t + 1, :].astype(F32)
        for h in range(QH):
            r = h // per_device * rp + t * per_device + h % per_device
            qtmp_ref[r:r + 1, :] = x[:, h * HD:(h + 1) * HD]
    scale = 1.0 / (HD ** 0.5)
    row = lax.broadcasted_iota(jnp.int32, (LANES, LANES), 0) % rp
    lane_r = lax.broadcasted_iota(jnp.int32, (LANES, LANES), 1)
    cq = jnp.zeros((LANES, LANES), F32)
    sq = jnp.zeros((LANES, LANES), F32)
    for t in range(steps):
        here = (row >= t * per_device) & (row < (t + 1) * per_device)
        cq = jnp.where(here, cq_ref[t:t + 1, :] * scale, cq)
        sq = jnp.where(here, sq_ref[t:t + 1, :] * scale, sq)
    sq = jnp.where(lane_r < HD // 2, -sq, sq)
    for pk in range(w_ref.shape[0]):
        x = qtmp_ref[pk * LANES:(pk + 1) * LANES, :]
        x = x * cq + pltpu.roll(x, HD // 2, 1) * sq
        z = jnp.where(lane_r < HD // 2, 1.0, -1.0) * pltpu.roll(x, HD // 2, 1)
        hi, lo = split2(jnp.concatenate([x.T, z.T], 0))
        w_ref[pk] = jnp.concatenate([hi, lo], 0)

    blk = cb_ref.shape[0] // SPAN
    turns = []
    for j in range(OMOST):
        a = o_span[j] // blk
        b = pl.ds(pl.multiple_of(o_span[j] % blk * SPAN, SPAN), SPAN)
        ca, sa = ca_ref[pl.ds(a, 1), :], sa_ref[pl.ds(a, 1), :]
        cb, sb = cb_ref[b, :], sb_ref[b, :]
        turns.append((ca * cb - sa * sb, (sa * cb + ca * sb) * sign))
    for c in o_copies:
        c.wait()
    x_rows = kx_ref.shape[1]
    xtmp_ref[...] = jnp.zeros_like(xtmp_ref)
    fs = sq_ref[:steps, :] * sign[:1]
    for g in range(KVH):
        sl = slice(g * HD, (g + 1) * HD)
        for j in range(OMOST):
            wide = okeys_ref[j, :, sl].astype(F32)
            x = jnp.where(o_span[j] % 2 == 0, wide[:8], wide[8:])
            xtmp_ref[j * SPAN:(j + 1) * SPAN, :] = x * turns[j][0] + pltpu.roll(x, HD // 2, 1) * turns[j][1]
        x = fk_ref[:, sl].astype(F32)
        o = OMOST * SPAN
        xtmp_ref[o:o + steps, :] = x * cq_ref[:steps, :] + pltpu.roll(x, HD // 2, 1) * fs
        kx_ref[g, :, :HD] = xtmp_ref[...].astype(BF)
        kx_ref[g, :, HD:] = jnp.zeros((x_rows, HD), BF)


def values_kernel(
    me_ref, chosen_ref, begin_ref, count_ref, outl_ref, fv_ref, values_hbm, after_ref, slots_ref, vg_ref, tie_ref,
    values_ref, vtmp_ref, sem, *, main, g0, most
):
    steps = fv_ref.shape[0]
    rows_all = vtmp_ref.shape[0]
    n = vg_ref.shape[0]
    copies = [
        pltpu.make_async_copy(values_hbm.at[:, pl.ds((g0 + i) * HD, HD)], values_ref.at[i], sem.at[i]) for i in range(n)
    ]
    for c in copies[:2]:
        c.start()
    tie_ref[...] = jnp.zeros_like(tie_ref)
    vtmp_ref[...] = jnp.zeros_like(vtmp_ref)
    spans = values_ref.shape[1] // SPAN
    lists = Lists(me_ref, chosen_ref, begin_ref, count_ref, outl_ref, spans, most)
    _, o_span = lists.outliers()

    for i in range(n):
        def rows_of(span, i=i):
            wide = values_ref[i, pl.ds(pl.multiple_of(span // 2 * 16, 16), 16), :].astype(F32)
            return jnp.where(span % 2 == 0, wide[:8], wide[8:])

        def put(spans, slot, i=i, rows_of=rows_of):
            for j, span in enumerate(spans):
                slots_ref[i, slot + j] = span
            dst = pl.ds(pl.multiple_of(LANES + slot * SPAN, SPAN), PART * SPAN)
            vtmp_ref[dst, :] = jnp.concatenate([rows_of(span) for span in spans], 0)

        copies[i].wait()
        if i + 2 < n:
            copies[i + 2].start()
        for j in range(OMOST):
            vtmp_ref[j * SPAN:(j + 1) * SPAN, :] = rows_of(o_span[j])
        vtmp_ref[OMOST * SPAN:OMOST * SPAN + steps, :] = fv_ref[:, (g0 + i) * HD:(g0 + i + 1) * HD].astype(F32)
        total = lists.find(g0 + i, steps, put)[steps]
        vg_ref[i, :LANES + main, :] = vtmp_ref[:LANES + main, :].astype(BF)
        if LANES + main < rows_all:
            def more(k, _, i=i):
                at = pl.ds(pl.multiple_of(LANES + main + k * LANES, LANES), LANES)
                vg_ref[i, at, :] = vtmp_ref[at, :].astype(BF)
                return 0

            lax.fori_loop(0, (jnp.maximum(total * SPAN - main, 0) + LANES - 1) // LANES, more, 0)


def attend_kernel(
    me_ref, count_ref, outl_ref, slotsa_ref, slotsb_ref, zmine_ref, zother_ref, kx_ref, w_ref, vga_ref, vgb_ref,
    ca_ref, sa_ref, cb_ref, sb_ref, keys_hbm,
    kft_hbm, out_ref,
    keys_ref, z_ref, a_ref, qt_ref, kf_ref, kft_ref, kg_ref, cg_ref, sg_ref, sc_ref, cc_ref, ss_ref, acc_ref,
    sem, out_sem, *, per_device, steps, main, most, stop=9
):
    rank, width = z_ref.shape
    half = rank // 2
    seq_len = keys_ref.shape[0]
    load = pltpu.make_async_copy(keys_hbm, keys_ref, sem)
    load.start()

    core = me_ref[0] % 2
    z_ref[pl.ds(pl.multiple_of(core * half, 16), half), :] = zmine_ref[...]
    z_ref[pl.ds(pl.multiple_of((1 - core) * half, 16), half), :] = zother_ref[...]
    turn_tables(ca_ref, sa_ref, cb_ref, sb_ref, cc_ref, ss_ref)
    basis(z_ref, a_ref, qt_ref)
    qt = qt_ref[...]

    load.wait()
    if stop == 1:
        return
    chunk = seq_len // KVH
    for i in range(KVH):
        rows = slice(i * chunk, (i + 1) * chunk)
        kf = lax.dot_general(keys_ref[rows, :], qt, NT, preferred_element_type=F32)
        kf_ref[rows, :] = kf
        kft_ref[:, rows] = kf.T
    store = pltpu.make_async_copy(kft_ref, kft_hbm, out_sem)
    store.start()
    if stop == 2:
        store.wait()
        return

    spans = seq_len // SPAN
    lists = Lists(me_ref, None, None, count_ref, outl_ref, spans, most)
    starts = []

    def values(g, rows):
        n = vga_ref.shape[0]
        return vga_ref[g, rows, :] if g < n else vgb_ref[g - n, rows, :]

    for g in range(KVH):
        def gather(spans, slot, g=g):
            got = []
            for span in spans:
                src = pl.ds(pl.multiple_of(span * SPAN, SPAN), SPAN)
                got.append((kf_ref[src, :], cc_ref[src, :], ss_ref[src, :]))
            dst = pl.ds(pl.multiple_of(slot * SPAN, SPAN), PART * SPAN)
            for ref, rows in zip((kg_ref, cg_ref, sg_ref), zip(*got)):
                ref[g, dst, :] = jnp.concatenate(rows, 0)

        starts.append(lists.starts(g, steps))
        early = slotsa_ref.shape[0]
        held, h = (slotsa_ref, g) if g < early else (slotsb_ref, g - early)
        each_part(held, h, starts[g][steps], kg_ref.shape[1] // (PART * SPAN), spans, gather)
    totals = [at[steps] for at in starts]

    if stop == 3:
        store.wait()
        return

    n_dest, rp, _ = out_ref.shape
    dests = n_dest // KVH
    qr = dests * rp
    heads = LANES // qr
    packs = w_ref.shape[0]
    o_live = lists.outliers()[0] * SPAN
    first_shard = me_ref[0] == 0
    column = lax.broadcasted_iota(jnp.int32, (8, LANES), 1)[:1]
    col_head = column // qr
    col_row = column % rp
    col_step = col_row // per_device

    def bounds(pk, h):
        first = jnp.full((1, LANES), 1 << 30, jnp.int32)
        last = jnp.zeros((1, LANES), jnp.int32)
        for t in range(steps):
            at = starts[pk * heads + h]
            here = (col_head == h) & (col_step == t)
            first = jnp.where(here, at[t] * SPAN, first)
            last = jnp.where(here, at[t + 1] * SPAN, last)
        return first, last

    def product(pk, y):
        r = jnp.dot(y, w_ref[pk, :2 * HD, :], preferred_element_type=F32)
        return r + jnp.dot(y, w_ref[pk, 2 * HD:, :], preferred_element_type=F32)

    token = lax.broadcasted_iota(jnp.int32, (LANES, LANES), 0)

    def slot_scores(pk, at, n, limits):
        rows = pl.ds(at, n)
        ys = []
        for h in range(heads):
            g = pk * heads + h
            x = jnp.dot(kg_ref[g, rows, :].astype(BF), qt_ref[:, g * HD:(g + 1) * HD], preferred_element_type=F32)
            ys.append(jnp.concatenate([(x * cg_ref[g, rows, :]).astype(BF), (x * sg_ref[g, rows, :]).astype(BF)], 1))
        r = product(pk, jnp.concatenate(ys, 0))
        s = jnp.full((n, LANES), DEAD, F32)
        here = lax.broadcasted_iota(jnp.int32, (n, LANES), 0) + at
        for h in range(heads):
            first, last = limits[h]
            s = jnp.where((here >= first) & (here < last), r[h * n:(h + 1) * n], s)
        return s

    def known_scores(pk):
        s = jnp.full((LANES, LANES), DEAD, F32)
        new = token - OMOST * SPAN
        is_live = (token < o_live) | (first_shard & (new >= 0) & (new <= col_step))
        is_live = is_live & (new < steps) & (col_row < steps * per_device)
        r = product(pk, kx_ref[pk * heads:(pk + 1) * heads].reshape(heads * LANES, 2 * HD))
        for h in range(heads):
            s = jnp.where(is_live & (col_head == h), r[h * LANES:(h + 1) * LANES], s)
        return s

    limits = [[bounds(pk, h) for h in range(heads)] for pk in range(packs)]
    extra = kg_ref.shape[1] - main
    blocks = []
    for pk in range(packs):
        longest = functools.reduce(jnp.maximum, totals[pk * heads:(pk + 1) * heads])
        blocks.append((jnp.maximum(longest * SPAN - main, 0) + LANES - 1) // LANES)

    tops = []
    for pk in range(packs):
        s = known_scores(pk)
        sc_ref[pk, :LANES, :] = s
        top = jnp.max(s, axis=0, keepdims=True)
        for at in range(0, main, ROWS):
            n = min(ROWS, main - at)
            s = slot_scores(pk, at, n, limits[pk])
            sc_ref[pk, LANES + at:LANES + at + n, :] = s
            top = jnp.maximum(top, jnp.max(s, axis=0, keepdims=True))
        tops.append(top)
    if extra > 0:
        for pk in range(packs):
            def more(k, top, pk=pk):
                at = pl.multiple_of(main + k * LANES, LANES)
                s = slot_scores(pk, at, LANES, limits[pk])
                sc_ref[pk, pl.ds(pl.multiple_of(LANES + at, LANES), LANES), :] = s
                return jnp.maximum(top, jnp.max(s, axis=0, keepdims=True))

            tops[pk] = lax.fori_loop(0, blocks[pk], more, tops[pk])
    if stop == 4:
        store.wait()
        return

    used = steps * per_device

    def weights(s, top):
        return jnp.where(s > 0.5 * DEAD, jnp.exp(s - top), 0.0)

    def weighted(pt, h, values):
        hi, lo = split2(pt[h * qr:(h + 1) * qr, :])
        r = jnp.dot(jnp.concatenate([hi, lo], 0), values, preferred_element_type=F32)
        return r[:qr] + r[qr:]

    sums = []
    for pk in range(packs):
        pts = []
        total = jnp.zeros((LANES, LANES), F32)
        for at in range(0, LANES + main, LANES):
            p = weights(sc_ref[pk, at:at + LANES, :], tops[pk])
            total = total + p
            pts.append(p.T)
        sums.append(jnp.sum(total, axis=0, keepdims=True))
        pt = jnp.concatenate(pts, 1)
        for h in range(heads):
            g = pk * heads + h
            acc = weighted(pt, h, values(g, slice(0, LANES + main)))
            for a in range(dests):
                acc_ref[g * dests + a] = acc[a * rp:(a + 1) * rp]
    if extra > 0:
        for pk in range(packs):
            def add(k, total, pk=pk):
                at = pl.multiple_of(LANES + main + k * LANES, LANES)
                p = weights(sc_ref[pk, pl.ds(at, LANES), :], tops[pk])
                pt = p.T
                for h in range(heads):
                    g = pk * heads + h

                    @pl.when(totals[g] * SPAN > main + k * LANES)
                    def _():
                        acc = weighted(pt, h, values(g, pl.ds(at, LANES)))
                        for a in range(dests):
                            acc_ref[g * dests + a] += acc[a * rp:(a + 1) * rp]

                return total + jnp.sum(p, axis=0, keepdims=True)

            sums[pk] = lax.fori_loop(0, blocks[pk], add, sums[pk])
    for d in range(n_dest):
        pk = d // (heads * dests)
        row = lax.broadcasted_iota(jnp.int32, (rp, LANES), 0)
        r = acc_ref[d]
        for k, extra_row in enumerate((*split3(tops[pk]), sums[pk])):
            r = jnp.where(row == used + k, extra_row, r)
        out_ref[d] = r.astype(BF)
    store.wait()


def turn_tables(ca_ref, sa_ref, cb_ref, sb_ref, cc_ref, ss_ref):
    blk = cb_ref.shape[0]
    cb = cb_ref[...]
    sb = sb_ref[...]
    for a in range(cc_ref.shape[0] // blk):
        ca = ca_ref[a:a + 1, :]
        sa = sa_ref[a:a + 1, :]
        cc_ref[a * blk:(a + 1) * blk, :] = ca * cb - sa * sb
        ss_ref[a * blk:(a + 1) * blk, :] = sa * cb + ca * sb


def basis(z_ref, a_ref, qt_ref):
    rank = z_ref.shape[0]
    wide = round_up(rank, LANES)
    z = z_ref[...]
    c = lax.dot_general(z, z, NT, preferred_element_type=F32)
    rows = lax.broadcasted_iota(jnp.int32, (rank, wide), 0)
    cols = lax.broadcasted_iota(jnp.int32, (rank, wide), 1)
    a_ref[:, :wide] = jnp.where(rows == cols, 1.0, 0.0)
    a_ref[:, wide:wide + rank] = c
    a_ref[:, wide + rank:] = jnp.zeros((rank, wide - rank), F32)
    nb = 32
    half_tiles = wide // LANES
    for j0 in range(0, rank, nb):
        tiles = [t for t in range(half_tiles) if t * LANES < j0 + nb]
        tiles += [half_tiles + t for t in range(half_tiles) if (t + 1) * LANES > j0]
        part = {t: a_ref[j0:j0 + nb, t * LANES:(t + 1) * LANES] for t in tiles}
        row = lax.broadcasted_iota(jnp.int32, (nb, LANES), 0)
        column = []
        for j in range(nb):
            t, o = divmod(j0 + j, LANES)
            column.append(jnp.broadcast_to(part[half_tiles + t][:, o:o + 1], (nb, LANES)))
        for j in range(nb):
            inverse = lax.rsqrt(jnp.broadcast_to(column[j][j:j + 1, :], (nb, LANES)))
            low = jnp.where(row > j, column[j] * inverse, 0.0)
            for k in range(j + 1, nb):
                column[k] = column[k] - low * jnp.broadcast_to(low[k:k + 1, :], (nb, LANES))
            for t in tiles:
                upper = jnp.broadcast_to(part[t][j:j + 1, :], (nb, LANES)) * inverse
                part[t] = jnp.where(row == j, upper, part[t] - low * upper)
        for t in tiles:
            a_ref[j0:j0 + nb, t * LANES:(t + 1) * LANES] = part[t]
        if j0 + nb < rank:
            upper = jnp.concatenate(
                [part[t] if t in part else jnp.zeros((nb, LANES), F32) for t in range(2 * half_tiles)], 1
            )
            h, m, l = split3(upper)
            left = jnp.concatenate([h, h, m, m, h, l], 0)[:, wide:].astype(BF)
            right = jnp.concatenate([h, m, h, m, l, h], 0).astype(BF)
            for s in range(2):
                d = lax.dot_general(left, right[:, s * wide:(s + 1) * wide], TN, preferred_element_type=F32)
                a_ref[j0 + nb:, s * wide:(s + 1) * wide] -= d[j0 + nb:rank]
    h, m, _ = split3(a_ref[:, :rank])
    q = jnp.dot(jnp.concatenate([h, m], 0).astype(BF), z, preferred_element_type=F32)
    qt_ref[...] = (q[:rank] + q[rank:]).astype(BF)


def attend_call(
    me, lists, z, z_other, kx, w, vga, vgb, ca, sa, cb, sb, cache_keys,
    *, steps, per_device, main, most, rp, n_dest, stop=9
):
    seq_len, width = cache_keys.shape
    rank = 2 * z.shape[0]
    tok_all = vga.shape[1] - LANES
    return pl.pallas_call(
        functools.partial(attend_kernel, per_device=per_device, steps=steps, main=main, most=most, stop=stop),
        in_specs=[smem()] * 5 + [vmem()] * 10 + [hbm()],
        out_specs=[hbm(), vmem()],
        out_shape=[
            jax.ShapeDtypeStruct((rank, seq_len), F32),
            jax.ShapeDtypeStruct((n_dest, rp, HD), BF),
        ],
        scratch_shapes=[
            pltpu.VMEM((seq_len, width), BF),
            pltpu.VMEM((rank, width), BF),
            pltpu.VMEM((rank, 2 * round_up(rank, LANES)), F32),
            pltpu.VMEM((rank, width), BF),
            pltpu.VMEM((seq_len, rank), F32),
            pltpu.VMEM((rank, seq_len), F32),
            pltpu.VMEM((KVH, tok_all, rank), F32),
            pltpu.VMEM((KVH, tok_all, HD), F32),
            pltpu.VMEM((KVH, tok_all, HD), F32),
            pltpu.VMEM((w.shape[0], LANES + tok_all, LANES), F32),
            pltpu.VMEM((seq_len, HD), F32),
            pltpu.VMEM((seq_len, HD), F32),
            pltpu.VMEM((n_dest, rp, HD), F32),
            pltpu.SemaphoreType.DMA,
            pltpu.SemaphoreType.DMA,
        ],
        compiler_params=pltpu.CompilerParams(vmem_limit_bytes=46 << 20),
        name="attend",
    )(me, *lists, z, z_other, kx, w, vga, vgb, ca, sa, cb, sb, in_hbm(cache_keys))


def merge_kernel(me_ref, parts_ref, out_ref, top_ref, sum_ref, *, steps, per_device):
    n, rp, _ = parts_ref.shape
    used = steps * per_device
    parts = parts_ref[...].astype(F32)
    rows = pl.ds(pl.multiple_of(me_ref[0] % (LANES // rp) * rp, 8), rp)
    top_ref[...] = (parts[:, used, :] + parts[:, used + 1, :] + parts[:, used + 2, :]).T
    sum_ref[...] = parts[:, used + 3, :].T
    tops = top_ref[rows, :]
    w = jnp.exp(tops - jnp.max(tops, axis=1, keepdims=True))
    w = w / jnp.sum(w * sum_ref[rows, :], axis=1, keepdims=True)
    o = jnp.zeros((rp, HD), F32)
    for s in range(n):
        o = o + w[:, s:s + 1] * parts[s]
    for t in range(steps):
        for i in range(per_device):
            r = t * per_device + i
            out_ref[t:t + 1, i * HD:(i + 1) * HD] = o[r:r + 1, :].astype(BF)


def swap(x, moves):
    return lax.ppermute(x, "seq", moves)


def on_device(
    cache_keys,
    cache_values,
    sketch_matrix,
    queries,
    fresh_keys,
    fresh_values,
    chosen,
    shard_counts,
    outliers,
):
    seq_len, width = cache_keys.shape
    devices = lax.axis_size("seq")
    myself = lax.axis_index("seq")
    length = seq_len * devices
    steps = queries.shape[0]
    rank = sketch_matrix.shape[1]
    per_device = QH // devices
    n_lists = steps * KVH
    most = 3 * chosen.shape[2] // devices
    slots_all = round_up(max(steps * most, steps * STRAIGHT * PART), LANES // SPAN)
    tok_all = slots_all * SPAN
    main = min(MAIN, tok_all)
    used = steps * per_device
    rp = round_up(used + 4, 16)
    n_dest = devices
    me = jnp.full((1,), myself, jnp.int32)

    keep, send = sketch_share(me, sketch_matrix.T, cache_keys, length)

    half_width = HD // 2
    exponents = jnp.arange(half_width, dtype=F32) * (2.0 / HD)
    inverse_freq = jnp.exp(-jnp.log(F32(500000.0)) * exponents)
    inverse_freq = jnp.concatenate([inverse_freq, inverse_freq])
    blk = 64
    coarse = (myself * seq_len + blk * jnp.arange(seq_len // blk, dtype=jnp.int32)).astype(F32)[:, None] * inverse_freq
    fine = jnp.arange(blk, dtype=jnp.int32).astype(F32)[:, None] * inverse_freq
    late = (length + jnp.arange(steps, dtype=jnp.int32)).astype(F32)[:, None] * inverse_freq
    turns = (jnp.cos(coarse), jnp.sin(coarse), jnp.cos(fine), jnp.sin(fine))

    shard = jnp.arange(devices, dtype=jnp.int32)
    begin = jnp.sum(jnp.where(shard < myself, shard_counts, 0), axis=2)
    count = jnp.sum(jnp.where(shard == myself, shard_counts, 0), axis=2)
    lists = (chosen.reshape(n_lists, -1), begin, count)
    places = slots_all + 4 * PART
    tie_shape = jax.ShapeDtypeStruct((1, LANES), F32)

    def known(after):
        return pl.pallas_call(
            functools.partial(known_kernel, per_device=per_device, rp=rp, spans=seq_len // SPAN),
            in_specs=[smem()] * 2 + [vmem()] * 8 + [hbm(), anywhere()],
            out_specs=[vmem()] * 3,
            out_shape=[
                jax.ShapeDtypeStruct((KVH, LANES, 2 * HD), BF),
                jax.ShapeDtypeStruct((n_dest * rp // LANES, 4 * HD, LANES), BF),
                tie_shape,
            ],
            scratch_shapes=[
                pltpu.VMEM((OMOST, 16, width), BF),
                pltpu.VMEM((LANES, HD), F32),
                pltpu.VMEM((n_dest * rp, HD), F32),
                pltpu.SemaphoreType.DMA((OMOST,)),
            ],
            compiler_params=pltpu.CompilerParams(vmem_limit_bytes=8 << 20),
            name="known_keys",
        )(me, outliers, queries, fresh_keys, *turns, jnp.cos(late), jnp.sin(late), in_hbm(cache_keys), after)

    def slot_values(g0, n, after):
        return pl.pallas_call(
            functools.partial(values_kernel, main=main, g0=g0, most=most),
            in_specs=[smem()] * 5 + [vmem(), hbm(), anywhere()],
            out_specs=[smem(), vmem(), vmem()],
            out_shape=[
                jax.ShapeDtypeStruct((n, places), jnp.int32),
                jax.ShapeDtypeStruct((n, LANES + tok_all, HD), BF),
                tie_shape,
            ],
            scratch_shapes=[
                pltpu.VMEM((n, seq_len, HD), BF),
                pltpu.VMEM((LANES + tok_all, HD), F32),
                pltpu.SemaphoreType.DMA((n,)),
            ],
            compiler_params=pltpu.CompilerParams(vmem_limit_bytes=16 << 20),
            name="slot_values",
        )(me, *lists, outliers, fresh_values, in_hbm(cache_values), after)

    z = keep + swap(send, [(i, i ^ 1) for i in range(devices)])
    hops = [1 << k for k in range(1, devices.bit_length() - 1)]
    for k in range(len(hops)):
        other = k ^ 1 if k < 2 and len(hops) >= 2 else k
        moves = [(i, i ^ hops[k if i % 2 == 0 else other]) for i in range(devices)]
        going = z.astype(BF)
        came = swap(going, moves).astype(F32)
        if k == 0:
            kx, w, tie = known(going)
            came = came + tie[0, 0]
        if k == min(1, len(hops) - 1):
            slots_a, vga, tie = slot_values(0, EARLY, going)
            came = came + tie[0, 0]
        if k == len(hops) - 1:
            slots_b, vgb, tie = slot_values(EARLY, KVH - EARLY, going)
            came = came + tie[0, 0]
        z = z + came
    z = z.astype(BF)
    z_other = swap(z, [(i, i ^ 1) for i in range(devices)])

    kft, parts = attend_call(
        me, (count, outliers, slots_a, slots_b), z, z_other, kx, w, vga, vgb, *turns, cache_keys,
        steps=steps, per_device=per_device, main=main, most=most, rp=rp, n_dest=n_dest,
    )
    parts = lax.all_to_all(parts, "seq", 0, 0, tiled=True)
    attended = pl.pallas_call(
        functools.partial(merge_kernel, steps=steps, per_device=per_device),
        in_specs=[smem(), vmem()],
        out_specs=vmem(),
        out_shape=jax.ShapeDtypeStruct((steps, per_device * HD), BF),
        scratch_shapes=[pltpu.VMEM((LANES, devices), F32)] * 2,
        name="merge",
    )(me, parts)
    return (attended, kft.T)


def solution(mesh):
    in_specs = (
        P(("groups", "seq"), None),
        P(("groups", "seq"), None),
        P(),
        P("groups", None),
        P("groups", None),
        P("groups", None),
        P("groups", None, None),
        P("groups", None, None),
        P("groups"),
    )
    out_specs = (P("groups", "seq"), P(("groups", "seq"), None))
    return jax.shard_map(
        on_device, mesh=mesh, in_specs=in_specs, out_specs=out_specs, check_vma=False
    )
```

```python
import functools

import jax
import jax.numpy as jnp
from jax import lax
from jax.experimental import pallas as pl
from jax.experimental.pallas import tpu as pltpu
from jax.sharding import PartitionSpec as P

KVH = 8
HD = 128
QH = 64
SPAN = 8
OMOST = 4
BF = jnp.bfloat16
F32 = jnp.float32
DEAD = -1e30
LANES = 128
MAIN = 896
ROWS = 512
PART = 8
STRAIGHT = 6
EARLY = 3
AHEAD = 3
NT = (((1,), (1,)), ((), ()))
TN = (((0,), (0,)), ((), ()))


def vmem():
    return pl.BlockSpec(memory_space=pltpu.VMEM)


def smem():
    return pl.BlockSpec(memory_space=pltpu.SMEM)


def hbm():
    return pl.BlockSpec(memory_space=pltpu.HBM)


def in_hbm(x):
    return pltpu.with_memory_space_constraint(x, pltpu.HBM)


def anywhere():
    return pl.BlockSpec(memory_space=pl.ANY)


def round_up(x, m):
    return (x + m - 1) // m * m


def split2(x):
    high = x.astype(BF)
    return high, (x - high.astype(F32)).astype(BF)


def split3(x):
    high = x.astype(BF).astype(F32)
    rest = x - high
    middle = rest.astype(BF).astype(F32)
    return high, middle, rest - middle


def sketch_kernel(
    me_ref, st_hbm, keys_hbm, keep_ref, send_ref, st_ref, keys_ref, acc_ref, st_sem, sem, *, scale, chunk
):
    seq_len = keys_ref.shape[0]
    rank = st_ref.shape[0]
    half = rank // 2
    n = seq_len // chunk
    st_copy = pltpu.make_async_copy(st_hbm, st_ref, st_sem)
    st_copy.start()
    copies = [
        pltpu.make_async_copy(
            keys_hbm.at[pl.ds(i * chunk, chunk)], keys_ref.at[pl.ds(i * chunk, chunk)], sem.at[i]
        )
        for i in range(n)
    ]
    for c in copies[:AHEAD]:
        c.start()
    st_copy.wait()
    st = st_ref[...].astype(BF)

    def rows(i):
        return keys_ref[i * chunk:(i + 1) * chunk, :]

    def first(i):
        return lax.dot_general(st, rows(i), NT, preferred_element_type=F32).astype(BF)

    def second(i, y):
        return jnp.dot(y, rows(i), preferred_element_type=F32)

    def arrive(i):
        copies[i].wait()
        if i + AHEAD < n:
            copies[i + AHEAD].start()

    arrive(0)
    y = first(0)
    for i in range(1, n):
        arrive(i)
        y_next = first(i)
        z = second(i - 1, y)
        if i == 1:
            acc_ref[...] = z
        else:
            acc_ref[...] += z
        y = y_next
    acc_ref[...] = (acc_ref[...] + second(n - 1, y)) * scale
    core = me_ref[0] % 2
    keep_ref[...] = acc_ref[pl.ds(pl.multiple_of(core * half, 8), half), :]
    send_ref[...] = acc_ref[pl.ds(pl.multiple_of((1 - core) * half, 8), half), :]


def sketch_share(me, sketch_t, cache_keys, length):
    seq_len, width = cache_keys.shape
    rank = sketch_t.shape[0]
    chunk = min(512, seq_len)
    half = jax.ShapeDtypeStruct((rank // 2, width), F32)
    return pl.pallas_call(
        functools.partial(sketch_kernel, scale=1.0 / length, chunk=chunk),
        in_specs=[smem(), hbm(), hbm()],
        out_specs=[vmem(), vmem()],
        out_shape=[half, half],
        scratch_shapes=[
            pltpu.VMEM((rank, width), F32),
            pltpu.VMEM((seq_len, width), BF),
            pltpu.VMEM((rank, width), F32),
            pltpu.SemaphoreType.DMA,
            pltpu.SemaphoreType.DMA((seq_len // chunk,)),
        ],
        compiler_params=pltpu.CompilerParams(vmem_limit_bytes=24 << 20),
        name="sketch_share",
    )(me, in_hbm(sketch_t), in_hbm(cache_keys))


class Lists:
    def __init__(self, me_ref, chosen_ref, begin_ref, count_ref, outl_ref, spans, most=None):
        self.chosen, self.begin, self.counts, self.outl = chosen_ref, begin_ref, count_ref, outl_ref
        self.spans, self.most = spans, most
        self.base = me_ref[0] * spans

    def span(self, t, g, slot):
        i = t * KVH + g
        last = self.chosen.shape[1] - 1
        picked = self.chosen[i, jnp.minimum(self.begin[t, g] + slot, last)]
        return jnp.clip(picked - self.base, 0, self.spans - 1)

    def count(self, t, g):
        return jnp.minimum(self.counts[t, g], self.most)

    def starts(self, g, steps):
        at = [jnp.int32(0)]
        for t in range(steps):
            at.append(at[-1] + self.count(t, g))
        return at

    def outliers(self):
        n = self.outl.shape[0]
        first = jnp.int32(0)
        here = jnp.int32(0)
        for i in range(n):
            s = self.outl[i]
            first = first + (s < self.base).astype(jnp.int32)
            here = here + ((s >= self.base) & (s < self.base + self.spans)).astype(jnp.int32)
        found = [
            jnp.clip(self.outl[jnp.minimum(first + j, n - 1)] - self.base, 0, self.spans - 1) for j in range(OMOST)
        ]
        return jnp.minimum(here, OMOST), found

    def find(self, g, steps, copy):
        at = self.starts(g, steps)
        for t in range(steps):
            def part(k, _, t=t):
                copy([self.span(t, g, k * PART + j) for j in range(PART)], at[t] + k * PART)
                return 0

            copy([self.span(t, g, j) for j in range(2 * PART)], at[t])
            lax.fori_loop(2, (self.count(t, g) + PART - 1) // PART, part, 0)
        return at


def each_part(slots_ref, g, total, parts_all, spans, copy):
    def part(k, _):
        copy([jnp.clip(slots_ref[g, k * PART + j], 0, spans - 1) for j in range(PART)], k * PART)
        return 0

    straight = min(STRAIGHT, parts_all)
    for k in range(straight):
        part(k, 0)
    lax.fori_loop(straight, (total + PART - 1) // PART, part, 0)


def known_kernel(
    me_ref, outl_ref, q_ref, fk_ref, ca_ref, sa_ref, cb_ref, sb_ref, cq_ref, sq_ref, keys_hbm, after_ref,
    kx_ref, w_ref, tie_ref,
    okeys_ref, xtmp_ref, qtmp_ref, osem, *, per_device, rp, spans
):
    steps = q_ref.shape[0]
    tie_ref[...] = jnp.zeros_like(tie_ref)
    _, o_span = Lists(me_ref, None, None, None, outl_ref, spans).outliers()
    o_copies = [
        pltpu.make_async_copy(
            keys_hbm.at[pl.ds(pl.multiple_of(o_span[j] // 2 * 16, 16), 16)], okeys_ref.at[j], osem.at[j]
        )
        for j in range(OMOST)
    ]
    for c in o_copies:
        c.start()

    lane = lax.broadcasted_iota(jnp.int32, (8, LANES), 1)
    sign = jnp.where(lane < HD // 2, -1.0, 1.0)

    qtmp_ref[...] = jnp.zeros_like(qtmp_ref)
    for t in range(steps):
        x = q_ref[t:t + 1, :].astype(F32)
        for h in range(QH):
            r = h // per_device * rp + t * per_device + h % per_device
            qtmp_ref[r:r + 1, :] = x[:, h * HD:(h + 1) * HD]
    scale = 1.0 / (HD ** 0.5)
    row = lax.broadcasted_iota(jnp.int32, (LANES, LANES), 0) % rp
    lane_r = lax.broadcasted_iota(jnp.int32, (LANES, LANES), 1)
    cq = jnp.zeros((LANES, LANES), F32)
    sq = jnp.zeros((LANES, LANES), F32)
    for t in range(steps):
        here = (row >= t * per_device) & (row < (t + 1) * per_device)
        cq = jnp.where(here, cq_ref[t:t + 1, :] * scale, cq)
        sq = jnp.where(here, sq_ref[t:t + 1, :] * scale, sq)
    sq = jnp.where(lane_r < HD // 2, -sq, sq)
    for pk in range(w_ref.shape[0]):
        x = qtmp_ref[pk * LANES:(pk + 1) * LANES, :]
        x = x * cq + pltpu.roll(x, HD // 2, 1) * sq
        z = jnp.where(lane_r < HD // 2, 1.0, -1.0) * pltpu.roll(x, HD // 2, 1)
        hi, lo = split2(jnp.concatenate([x.T, z.T], 0))
        w_ref[pk] = jnp.concatenate([hi, lo], 0)

    blk = cb_ref.shape[0] // SPAN
    turns = []
    for j in range(OMOST):
        a = o_span[j] // blk
        b = pl.ds(pl.multiple_of(o_span[j] % blk * SPAN, SPAN), SPAN)
        ca, sa = ca_ref[pl.ds(a, 1), :], sa_ref[pl.ds(a, 1), :]
        cb, sb = cb_ref[b, :], sb_ref[b, :]
        turns.append((ca * cb - sa * sb, (sa * cb + ca * sb) * sign))
    for c in o_copies:
        c.wait()
    x_rows = kx_ref.shape[1]
    xtmp_ref[...] = jnp.zeros_like(xtmp_ref)
    fs = sq_ref[:steps, :] * sign[:1]
    for g in range(KVH):
        sl = slice(g * HD, (g + 1) * HD)
        for j in range(OMOST):
            wide = okeys_ref[j, :, sl].astype(F32)
            x = jnp.where(o_span[j] % 2 == 0, wide[:8], wide[8:])
            xtmp_ref[j * SPAN:(j + 1) * SPAN, :] = x * turns[j][0] + pltpu.roll(x, HD // 2, 1) * turns[j][1]
        x = fk_ref[:, sl].astype(F32)
        o = OMOST * SPAN
        xtmp_ref[o:o + steps, :] = x * cq_ref[:steps, :] + pltpu.roll(x, HD // 2, 1) * fs
        kx_ref[g, :, :HD] = xtmp_ref[...].astype(BF)
        kx_ref[g, :, HD:] = jnp.zeros((x_rows, HD), BF)


def values_kernel(
    me_ref, chosen_ref, begin_ref, count_ref, outl_ref, fv_ref, values_hbm, after_ref, slots_ref, vg_ref, tie_ref,
    values_ref, vtmp_ref, sem, *, main, g0, most
):
    steps = fv_ref.shape[0]
    rows_all = vtmp_ref.shape[0]
    n = vg_ref.shape[0]
    copies = [
        pltpu.make_async_copy(values_hbm.at[:, pl.ds((g0 + i) * HD, HD)], values_ref.at[i], sem.at[i]) for i in range(n)
    ]
    for c in copies[:2]:
        c.start()
    tie_ref[...] = jnp.zeros_like(tie_ref)
    vtmp_ref[...] = jnp.zeros_like(vtmp_ref)
    spans = values_ref.shape[1] // SPAN
    lists = Lists(me_ref, chosen_ref, begin_ref, count_ref, outl_ref, spans, most)
    _, o_span = lists.outliers()

    for i in range(n):
        def rows_of(span, i=i):
            wide = values_ref[i, pl.ds(pl.multiple_of(span // 2 * 16, 16), 16), :].astype(F32)
            return jnp.where(span % 2 == 0, wide[:8], wide[8:])

        def put(spans, slot, i=i, rows_of=rows_of):
            rows = jnp.concatenate([rows_of(span) for span in spans], 0)
            dst = pl.ds(pl.multiple_of(LANES + slot * SPAN, SPAN), len(spans) * SPAN)
            vtmp_ref[dst, :] = rows
            for j, span in enumerate(spans):
                slots_ref[i, slot + j] = span

        copies[i].wait()
        if i + 2 < n:
            copies[i + 2].start()
        for j in range(OMOST):
            vtmp_ref[j * SPAN:(j + 1) * SPAN, :] = rows_of(o_span[j])
        vtmp_ref[OMOST * SPAN:OMOST * SPAN + steps, :] = fv_ref[:, (g0 + i) * HD:(g0 + i + 1) * HD].astype(F32)
        total = lists.find(g0 + i, steps, put)[steps]
        vg_ref[i, :LANES + main, :] = vtmp_ref[:LANES + main, :].astype(BF)
        if LANES + main < rows_all:
            def more(k, _, i=i):
                at = pl.ds(pl.multiple_of(LANES + main + k * LANES, LANES), LANES)
                vg_ref[i, at, :] = vtmp_ref[at, :].astype(BF)
                return 0

            lax.fori_loop(0, (jnp.maximum(total * SPAN - main, 0) + LANES - 1) // LANES, more, 0)


def attend_kernel(
    me_ref, count_ref, outl_ref, slotsa_ref, slotsb_ref, zmine_ref, zother_ref, kx_ref, w_ref, vga_ref, vgb_ref,
    ca_ref, sa_ref, cb_ref, sb_ref, keys_hbm,
    kft_hbm, out_ref,
    keys_ref, z_ref, a_ref, qt_ref, kf_ref, kft_ref, kg_ref, cg_ref, sg_ref, sc_ref, cc_ref, ss_ref, acc_ref,
    sem, out_sem, *, per_device, steps, main, most, stop=9
):
    rank, width = z_ref.shape
    half = rank // 2
    seq_len = keys_ref.shape[0]
    load = pltpu.make_async_copy(keys_hbm, keys_ref, sem)
    load.start()

    core = me_ref[0] % 2
    z_ref[pl.ds(pl.multiple_of(core * half, 16), half), :] = zmine_ref[...]
    z_ref[pl.ds(pl.multiple_of((1 - core) * half, 16), half), :] = zother_ref[...]
    turn_tables(ca_ref, sa_ref, cb_ref, sb_ref, cc_ref, ss_ref)
    basis(z_ref, a_ref, qt_ref)
    qt = qt_ref[...]

    load.wait()
    if stop == 1:
        return
    chunk = seq_len // KVH
    for i in range(KVH):
        rows = slice(i * chunk, (i + 1) * chunk)
        kf = lax.dot_general(keys_ref[rows, :], qt, NT, preferred_element_type=F32)
        kf_ref[rows, :] = kf
        kft_ref[:, rows] = kf.T
    store = pltpu.make_async_copy(kft_ref, kft_hbm, out_sem)
    store.start()
    if stop == 2:
        store.wait()
        return

    spans = seq_len // SPAN
    lists = Lists(me_ref, None, None, count_ref, outl_ref, spans, most)
    starts = []

    def values(g, rows):
        n = vga_ref.shape[0]
        return vga_ref[g, rows, :] if g < n else vgb_ref[g - n, rows, :]

    for g in range(KVH):
        def gather(spans, slot, g=g):
            got = []
            for span in spans:
                src = pl.ds(pl.multiple_of(span * SPAN, SPAN), SPAN)
                got.append((kf_ref[src, :], cc_ref[src, :], ss_ref[src, :]))
            dst = pl.ds(pl.multiple_of(slot * SPAN, SPAN), PART * SPAN)
            for ref, rows in zip((kg_ref, cg_ref, sg_ref), zip(*got)):
                ref[g, dst, :] = jnp.concatenate(rows, 0)

        starts.append(lists.starts(g, steps))
        early = slotsa_ref.shape[0]
        held, h = (slotsa_ref, g) if g < early else (slotsb_ref, g - early)
        each_part(held, h, starts[g][steps], kg_ref.shape[1] // (PART * SPAN), spans, gather)
    totals = [at[steps] for at in starts]

    if stop == 3:
        store.wait()
        return

    n_dest, rp, _ = out_ref.shape
    dests = n_dest // KVH
    qr = dests * rp
    heads = LANES // qr
    packs = w_ref.shape[0]
    o_live = lists.outliers()[0] * SPAN
    first_shard = me_ref[0] == 0
    column = lax.broadcasted_iota(jnp.int32, (8, LANES), 1)[:1]
    col_head = column // qr
    col_row = column % rp
    col_step = col_row // per_device

    def bounds(pk, h):
        first = jnp.full((1, LANES), 1 << 30, jnp.int32)
        last = jnp.zeros((1, LANES), jnp.int32)
        for t in range(steps):
            at = starts[pk * heads + h]
            here = (col_head == h) & (col_step == t)
            first = jnp.where(here, at[t] * SPAN, first)
            last = jnp.where(here, at[t + 1] * SPAN, last)
        return first, last

    def product(pk, y):
        r = jnp.dot(y, w_ref[pk, :2 * HD, :], preferred_element_type=F32)
        return r + jnp.dot(y, w_ref[pk, 2 * HD:, :], preferred_element_type=F32)

    token = lax.broadcasted_iota(jnp.int32, (LANES, LANES), 0)

    def slot_scores(pk, at, n, limits):
        rows = pl.ds(at, n)
        ys = []
        for h in range(heads):
            g = pk * heads + h
            x = jnp.dot(kg_ref[g, rows, :].astype(BF), qt_ref[:, g * HD:(g + 1) * HD], preferred_element_type=F32)
            ys.append(jnp.concatenate([(x * cg_ref[g, rows, :]).astype(BF), (x * sg_ref[g, rows, :]).astype(BF)], 1))
        r = product(pk, jnp.concatenate(ys, 0))
        s = jnp.full((n, LANES), DEAD, F32)
        here = lax.broadcasted_iota(jnp.int32, (n, LANES), 0) + at
        for h in range(heads):
            first, last = limits[h]
            s = jnp.where((here >= first) & (here < last), r[h * n:(h + 1) * n], s)
        return s

    def known_scores(pk):
        s = jnp.full((LANES, LANES), DEAD, F32)
        new = token - OMOST * SPAN
        is_live = (token < o_live) | (first_shard & (new >= 0) & (new <= col_step))
        is_live = is_live & (new < steps) & (col_row < steps * per_device)
        r = product(pk, kx_ref[pk * heads:(pk + 1) * heads].reshape(heads * LANES, 2 * HD))
        for h in range(heads):
            s = jnp.where(is_live & (col_head == h), r[h * LANES:(h + 1) * LANES], s)
        return s

    limits = [[bounds(pk, h) for h in range(heads)] for pk in range(packs)]
    extra = kg_ref.shape[1] - main
    blocks = []
    for pk in range(packs):
        longest = functools.reduce(jnp.maximum, totals[pk * heads:(pk + 1) * heads])
        blocks.append((jnp.maximum(longest * SPAN - main, 0) + LANES - 1) // LANES)

    tops = []
    for pk in range(packs):
        s = known_scores(pk)
        sc_ref[pk, :LANES, :] = s
        top = jnp.max(s, axis=0, keepdims=True)
        for at in range(0, main, ROWS):
            n = min(ROWS, main - at)
            s = slot_scores(pk, at, n, limits[pk])
            sc_ref[pk, LANES + at:LANES + at + n, :] = s
            top = jnp.maximum(top, jnp.max(s, axis=0, keepdims=True))
        tops.append(top)
    if extra > 0:
        for pk in range(packs):
            def more(k, top, pk=pk):
                at = pl.multiple_of(main + k * LANES, LANES)
                s = slot_scores(pk, at, LANES, limits[pk])
                sc_ref[pk, pl.ds(pl.multiple_of(LANES + at, LANES), LANES), :] = s
                return jnp.maximum(top, jnp.max(s, axis=0, keepdims=True))

            tops[pk] = lax.fori_loop(0, blocks[pk], more, tops[pk])
    if stop == 4:
        store.wait()
        return

    used = steps * per_device

    def weights(s, top):
        return jnp.where(s > 0.5 * DEAD, jnp.exp(s - top), 0.0)

    def weighted(pt, h, values):
        hi, lo = split2(pt[h * qr:(h + 1) * qr, :])
        r = jnp.dot(jnp.concatenate([hi, lo], 0), values, preferred_element_type=F32)
        return r[:qr] + r[qr:]

    sums = []
    for pk in range(packs):
        pts = []
        total = jnp.zeros((LANES, LANES), F32)
        for at in range(0, LANES + main, LANES):
            p = weights(sc_ref[pk, at:at + LANES, :], tops[pk])
            total = total + p
            pts.append(p.T)
        sums.append(jnp.sum(total, axis=0, keepdims=True))
        pt = jnp.concatenate(pts, 1)
        for h in range(heads):
            g = pk * heads + h
            acc = weighted(pt, h, values(g, slice(0, LANES + main)))
            for a in range(dests):
                acc_ref[g * dests + a] = acc[a * rp:(a + 1) * rp]
    if extra > 0:
        for pk in range(packs):
            def add(k, total, pk=pk):
                at = pl.multiple_of(LANES + main + k * LANES, LANES)
                p = weights(sc_ref[pk, pl.ds(at, LANES), :], tops[pk])
                pt = p.T
                for h in range(heads):
                    g = pk * heads + h

                    @pl.when(totals[g] * SPAN > main + k * LANES)
                    def _():
                        acc = weighted(pt, h, values(g, pl.ds(at, LANES)))
                        for a in range(dests):
                            acc_ref[g * dests + a] += acc[a * rp:(a + 1) * rp]

                return total + jnp.sum(p, axis=0, keepdims=True)

            sums[pk] = lax.fori_loop(0, blocks[pk], add, sums[pk])
    for d in range(n_dest):
        pk = d // (heads * dests)
        row = lax.broadcasted_iota(jnp.int32, (rp, LANES), 0)
        r = acc_ref[d]
        for k, extra_row in enumerate((*split3(tops[pk]), sums[pk])):
            r = jnp.where(row == used + k, extra_row, r)
        out_ref[d] = r.astype(BF)
    store.wait()


def turn_tables(ca_ref, sa_ref, cb_ref, sb_ref, cc_ref, ss_ref):
    blk = cb_ref.shape[0]
    cb = cb_ref[...]
    sb = sb_ref[...]
    for a in range(cc_ref.shape[0] // blk):
        ca = ca_ref[a:a + 1, :]
        sa = sa_ref[a:a + 1, :]
        cc_ref[a * blk:(a + 1) * blk, :] = ca * cb - sa * sb
        ss_ref[a * blk:(a + 1) * blk, :] = sa * cb + ca * sb


def basis(z_ref, a_ref, qt_ref):
    rank = z_ref.shape[0]
    wide = round_up(rank, LANES)
    z = z_ref[...]
    c = lax.dot_general(z, z, NT, preferred_element_type=F32)
    rows = lax.broadcasted_iota(jnp.int32, (rank, wide), 0)
    cols = lax.broadcasted_iota(jnp.int32, (rank, wide), 1)
    a_ref[:, :wide] = jnp.where(rows == cols, 1.0, 0.0)
    a_ref[:, wide:wide + rank] = c
    a_ref[:, wide + rank:] = jnp.zeros((rank, wide - rank), F32)
    nb = 32
    half_tiles = wide // LANES
    for j0 in range(0, rank, nb):
        tiles = [t for t in range(half_tiles) if t * LANES < j0 + nb]
        tiles += [half_tiles + t for t in range(half_tiles) if (t + 1) * LANES > j0]
        part = {t: a_ref[j0:j0 + nb, t * LANES:(t + 1) * LANES] for t in tiles}
        row = lax.broadcasted_iota(jnp.int32, (nb, LANES), 0)
        column = []
        for j in range(nb):
            t, o = divmod(j0 + j, LANES)
            column.append(jnp.broadcast_to(part[half_tiles + t][:, o:o + 1], (nb, LANES)))
        for j in range(nb):
            inverse = lax.rsqrt(jnp.broadcast_to(column[j][j:j + 1, :], (nb, LANES)))
            low = jnp.where(row > j, column[j] * inverse, 0.0)
            for k in range(j + 1, nb):
                column[k] = column[k] - low * jnp.broadcast_to(low[k:k + 1, :], (nb, LANES))
            for t in tiles:
                upper = jnp.broadcast_to(part[t][j:j + 1, :], (nb, LANES)) * inverse
                part[t] = jnp.where(row == j, upper, part[t] - low * upper)
        for t in tiles:
            a_ref[j0:j0 + nb, t * LANES:(t + 1) * LANES] = part[t]
        if j0 + nb < rank:
            upper = jnp.concatenate(
                [part[t] if t in part else jnp.zeros((nb, LANES), F32) for t in range(2 * half_tiles)], 1
            )
            h, m, l = split3(upper)
            left = jnp.concatenate([h, h, m, m, h, l], 0)[:, wide:].astype(BF)
            right = jnp.concatenate([h, m, h, m, l, h], 0).astype(BF)
            for s in range(2):
                d = lax.dot_general(left, right[:, s * wide:(s + 1) * wide], TN, preferred_element_type=F32)
                a_ref[j0 + nb:, s * wide:(s + 1) * wide] -= d[j0 + nb:rank]
    h, m, _ = split3(a_ref[:, :rank])
    q = jnp.dot(jnp.concatenate([h, m], 0).astype(BF), z, preferred_element_type=F32)
    qt_ref[...] = (q[:rank] + q[rank:]).astype(BF)


def attend_call(
    me, lists, z, z_other, kx, w, vga, vgb, ca, sa, cb, sb, cache_keys,
    *, steps, per_device, main, most, rp, n_dest, stop=9
):
    seq_len, width = cache_keys.shape
    rank = 2 * z.shape[0]
    tok_all = vga.shape[1] - LANES
    return pl.pallas_call(
        functools.partial(attend_kernel, per_device=per_device, steps=steps, main=main, most=most, stop=stop),
        in_specs=[smem()] * 5 + [vmem()] * 10 + [hbm()],
        out_specs=[hbm(), vmem()],
        out_shape=[
            jax.ShapeDtypeStruct((rank, seq_len), F32),
            jax.ShapeDtypeStruct((n_dest, rp, HD), BF),
        ],
        scratch_shapes=[
            pltpu.VMEM((seq_len, width), BF),
            pltpu.VMEM((rank, width), BF),
            pltpu.VMEM((rank, 2 * round_up(rank, LANES)), F32),
            pltpu.VMEM((rank, width), BF),
            pltpu.VMEM((seq_len, rank), F32),
            pltpu.VMEM((rank, seq_len), F32),
            pltpu.VMEM((KVH, tok_all, rank), F32),
            pltpu.VMEM((KVH, tok_all, HD), F32),
            pltpu.VMEM((KVH, tok_all, HD), F32),
            pltpu.VMEM((w.shape[0], LANES + tok_all, LANES), F32),
            pltpu.VMEM((seq_len, HD), F32),
            pltpu.VMEM((seq_len, HD), F32),
            pltpu.VMEM((n_dest, rp, HD), F32),
            pltpu.SemaphoreType.DMA,
            pltpu.SemaphoreType.DMA,
        ],
        compiler_params=pltpu.CompilerParams(vmem_limit_bytes=46 << 20),
        name="attend",
    )(me, *lists, z, z_other, kx, w, vga, vgb, ca, sa, cb, sb, in_hbm(cache_keys))


def merge_kernel(me_ref, parts_ref, out_ref, top_ref, sum_ref, *, steps, per_device):
    n, rp, _ = parts_ref.shape
    used = steps * per_device
    parts = parts_ref[...].astype(F32)
    rows = pl.ds(pl.multiple_of(me_ref[0] % (LANES // rp) * rp, 8), rp)
    top_ref[...] = (parts[:, used, :] + parts[:, used + 1, :] + parts[:, used + 2, :]).T
    sum_ref[...] = parts[:, used + 3, :].T
    tops = top_ref[rows, :]
    w = jnp.exp(tops - jnp.max(tops, axis=1, keepdims=True))
    w = w / jnp.sum(w * sum_ref[rows, :], axis=1, keepdims=True)
    o = jnp.zeros((rp, HD), F32)
    for s in range(n):
        o = o + w[:, s:s + 1] * parts[s]
    for t in range(steps):
        for i in range(per_device):
            r = t * per_device + i
            out_ref[t:t + 1, i * HD:(i + 1) * HD] = o[r:r + 1, :].astype(BF)


def swap(x, moves):
    return lax.ppermute(x, "seq", moves)


def on_device(
    cache_keys,
    cache_values,
    sketch_matrix,
    queries,
    fresh_keys,
    fresh_values,
    chosen,
    shard_counts,
    outliers,
):
    seq_len, width = cache_keys.shape
    devices = lax.axis_size("seq")
    myself = lax.axis_index("seq")
    length = seq_len * devices
    steps = queries.shape[0]
    rank = sketch_matrix.shape[1]
    per_device = QH // devices
    n_lists = steps * KVH
    most = 3 * chosen.shape[2] // devices
    slots_all = round_up(max(steps * most, steps * STRAIGHT * PART), LANES // SPAN)
    tok_all = slots_all * SPAN
    main = min(MAIN, tok_all)
    used = steps * per_device
    rp = round_up(used + 4, 16)
    n_dest = devices
    me = jnp.full((1,), myself, jnp.int32)

    keep, send = sketch_share(me, sketch_matrix.T, cache_keys, length)

    half_width = HD // 2
    exponents = jnp.arange(half_width, dtype=F32) * (2.0 / HD)
    inverse_freq = jnp.exp(-jnp.log(F32(500000.0)) * exponents)
    inverse_freq = jnp.concatenate([inverse_freq, inverse_freq])
    blk = 64
    coarse = (myself * seq_len + blk * jnp.arange(seq_len // blk, dtype=jnp.int32)).astype(F32)[:, None] * inverse_freq
    fine = jnp.arange(blk, dtype=jnp.int32).astype(F32)[:, None] * inverse_freq
    late = (length + jnp.arange(steps, dtype=jnp.int32)).astype(F32)[:, None] * inverse_freq
    turns = (jnp.cos(coarse), jnp.sin(coarse), jnp.cos(fine), jnp.sin(fine))

    shard = jnp.arange(devices, dtype=jnp.int32)
    begin = jnp.sum(jnp.where(shard < myself, shard_counts, 0), axis=2)
    count = jnp.sum(jnp.where(shard == myself, shard_counts, 0), axis=2)
    lists = (chosen.reshape(n_lists, -1), begin, count)
    places = slots_all + 4 * PART
    tie_shape = jax.ShapeDtypeStruct((1, LANES), F32)

    def known(after):
        return pl.pallas_call(
            functools.partial(known_kernel, per_device=per_device, rp=rp, spans=seq_len // SPAN),
            in_specs=[smem()] * 2 + [vmem()] * 8 + [hbm(), anywhere()],
            out_specs=[vmem()] * 3,
            out_shape=[
                jax.ShapeDtypeStruct((KVH, LANES, 2 * HD), BF),
                jax.ShapeDtypeStruct((n_dest * rp // LANES, 4 * HD, LANES), BF),
                tie_shape,
            ],
            scratch_shapes=[
                pltpu.VMEM((OMOST, 16, width), BF),
                pltpu.VMEM((LANES, HD), F32),
                pltpu.VMEM((n_dest * rp, HD), F32),
                pltpu.SemaphoreType.DMA((OMOST,)),
            ],
            compiler_params=pltpu.CompilerParams(vmem_limit_bytes=8 << 20),
            name="known_keys",
        )(me, outliers, queries, fresh_keys, *turns, jnp.cos(late), jnp.sin(late), in_hbm(cache_keys), after)

    def slot_values(g0, n, after):
        return pl.pallas_call(
            functools.partial(values_kernel, main=main, g0=g0, most=most),
            in_specs=[smem()] * 5 + [vmem(), hbm(), anywhere()],
            out_specs=[smem(), vmem(), vmem()],
            out_shape=[
                jax.ShapeDtypeStruct((n, places), jnp.int32),
                jax.ShapeDtypeStruct((n, LANES + tok_all, HD), BF),
                tie_shape,
            ],
            scratch_shapes=[
                pltpu.VMEM((n, seq_len, HD), BF),
                pltpu.VMEM((LANES + tok_all, HD), F32),
                pltpu.SemaphoreType.DMA((n,)),
            ],
            compiler_params=pltpu.CompilerParams(vmem_limit_bytes=16 << 20),
            name="slot_values",
        )(me, *lists, outliers, fresh_values, in_hbm(cache_values), after)

    z = keep + swap(send, [(i, i ^ 1) for i in range(devices)])
    hops = [1 << k for k in range(1, devices.bit_length() - 1)]
    for k in range(len(hops)):
        other = k ^ 1 if k < 2 and len(hops) >= 2 else k
        moves = [(i, i ^ hops[k if i % 2 == 0 else other]) for i in range(devices)]
        going = z.astype(BF)
        came = swap(going, moves).astype(F32)
        if k == 0:
            kx, w, tie = known(going)
            came = came + tie[0, 0]
        if k == min(1, len(hops) - 1):
            slots_a, vga, tie = slot_values(0, EARLY, going)
            came = came + tie[0, 0]
        if k == len(hops) - 1:
            slots_b, vgb, tie = slot_values(EARLY, KVH - EARLY, going)
            came = came + tie[0, 0]
        z = z + came
    z = z.astype(BF)
    z_other = swap(z, [(i, i ^ 1) for i in range(devices)])

    kft, parts = attend_call(
        me, (count, outliers, slots_a, slots_b), z, z_other, kx, w, vga, vgb, *turns, cache_keys,
        steps=steps, per_device=per_device, main=main, most=most, rp=rp, n_dest=n_dest,
    )
    parts = lax.all_to_all(parts, "seq", 0, 0, tiled=True)
    attended = pl.pallas_call(
        functools.partial(merge_kernel, steps=steps, per_device=per_device),
        in_specs=[smem(), vmem()],
        out_specs=vmem(),
        out_shape=jax.ShapeDtypeStruct((steps, per_device * HD), BF),
        scratch_shapes=[pltpu.VMEM((LANES, devices), F32)] * 2,
        name="merge",
    )(me, parts)
    return (attended, kft.T)


def solution(mesh):
    in_specs = (
        P(("groups", "seq"), None),
        P(("groups", "seq"), None),
        P(),
        P("groups", None),
        P("groups", None),
        P("groups", None),
        P("groups", None, None),
        P("groups", None, None),
        P("groups"),
    )
    out_specs = (P("groups", "seq"), P(("groups", "seq"), None))
    return jax.shard_map(
        on_device, mesh=mesh, in_specs=in_specs, out_specs=out_specs, check_vma=False
    )
```

```python
import functools

import jax
import jax.numpy as jnp
from jax import lax
from jax.experimental import pallas as pl
from jax.experimental.pallas import tpu as pltpu
from jax.sharding import PartitionSpec as P

KVH = 8
HD = 128
QH = 64
SPAN = 8
OMOST = 4
BF = jnp.bfloat16
F32 = jnp.float32
DEAD = -1e30
LANES = 128
MAIN = 896
ROWS = 512
PART = 8
STRAIGHT = 6
EARLY = 3
AHEAD = 3
NT = (((1,), (1,)), ((), ()))
TN = (((0,), (0,)), ((), ()))


def vmem():
    return pl.BlockSpec(memory_space=pltpu.VMEM)


def smem():
    return pl.BlockSpec(memory_space=pltpu.SMEM)


def hbm():
    return pl.BlockSpec(memory_space=pltpu.HBM)


def in_hbm(x):
    return pltpu.with_memory_space_constraint(x, pltpu.HBM)


def anywhere():
    return pl.BlockSpec(memory_space=pl.ANY)


def round_up(x, m):
    return (x + m - 1) // m * m


def split2(x):
    high = x.astype(BF)
    return high, (x - high.astype(F32)).astype(BF)


def split3(x):
    high = x.astype(BF).astype(F32)
    rest = x - high
    middle = rest.astype(BF).astype(F32)
    return high, middle, rest - middle


def sketch_kernel(
    me_ref, st_hbm, keys_hbm, keep_ref, send_ref, st_ref, keys_ref, acc_ref, st_sem, sem, *, scale, chunk
):
    seq_len = keys_ref.shape[0]
    rank = st_ref.shape[0]
    half = rank // 2
    n = seq_len // chunk
    st_copy = pltpu.make_async_copy(st_hbm, st_ref, st_sem)
    st_copy.start()
    copies = [
        pltpu.make_async_copy(
            keys_hbm.at[pl.ds(i * chunk, chunk)], keys_ref.at[pl.ds(i * chunk, chunk)], sem.at[i]
        )
        for i in range(n)
    ]
    for c in copies[:AHEAD]:
        c.start()
    st_copy.wait()
    st = st_ref[...].astype(BF)

    def rows(i):
        return keys_ref[i * chunk:(i + 1) * chunk, :]

    def first(i):
        return lax.dot_general(st, rows(i), NT, preferred_element_type=F32).astype(BF)

    def second(i, y):
        return jnp.dot(y, rows(i), preferred_element_type=F32)

    def arrive(i):
        copies[i].wait()
        if i + AHEAD < n:
            copies[i + AHEAD].start()

    arrive(0)
    y = first(0)
    for i in range(1, n):
        arrive(i)
        y_next = first(i)
        z = second(i - 1, y)
        if i == 1:
            acc_ref[...] = z
        else:
            acc_ref[...] += z
        y = y_next
    acc_ref[...] = (acc_ref[...] + second(n - 1, y)) * scale
    core = me_ref[0] % 2
    keep_ref[...] = acc_ref[pl.ds(pl.multiple_of(core * half, 8), half), :]
    send_ref[...] = acc_ref[pl.ds(pl.multiple_of((1 - core) * half, 8), half), :]


def sketch_share(me, sketch_t, cache_keys, length):
    seq_len, width = cache_keys.shape
    rank = sketch_t.shape[0]
    chunk = min(512, seq_len)
    half = jax.ShapeDtypeStruct((rank // 2, width), F32)
    return pl.pallas_call(
        functools.partial(sketch_kernel, scale=1.0 / length, chunk=chunk),
        in_specs=[smem(), hbm(), hbm()],
        out_specs=[vmem(), vmem()],
        out_shape=[half, half],
        scratch_shapes=[
            pltpu.VMEM((rank, width), F32),
            pltpu.VMEM((seq_len, width), BF),
            pltpu.VMEM((rank, width), F32),
            pltpu.SemaphoreType.DMA,
            pltpu.SemaphoreType.DMA((seq_len // chunk,)),
        ],
        compiler_params=pltpu.CompilerParams(vmem_limit_bytes=24 << 20),
        name="sketch_share",
    )(me, in_hbm(sketch_t), in_hbm(cache_keys))


class Lists:
    def __init__(self, me_ref, chosen_ref, begin_ref, count_ref, outl_ref, spans, most=None):
        self.chosen, self.begin, self.counts, self.outl = chosen_ref, begin_ref, count_ref, outl_ref
        self.spans, self.most = spans, most
        self.base = me_ref[0] * spans

    def span(self, t, g, slot):
        i = t * KVH + g
        last = self.chosen.shape[1] - 1
        picked = self.chosen[i, jnp.minimum(self.begin[t, g] + slot, last)]
        return jnp.clip(picked - self.base, 0, self.spans - 1)

    def count(self, t, g):
        return jnp.minimum(self.counts[t, g], self.most)

    def starts(self, g, steps):
        at = [jnp.int32(0)]
        for t in range(steps):
            at.append(at[-1] + self.count(t, g))
        return at

    def outliers(self):
        n = self.outl.shape[0]
        first = jnp.int32(0)
        here = jnp.int32(0)
        for i in range(n):
            s = self.outl[i]
            first = first + (s < self.base).astype(jnp.int32)
            here = here + ((s >= self.base) & (s < self.base + self.spans)).astype(jnp.int32)
        found = [
            jnp.clip(self.outl[jnp.minimum(first + j, n - 1)] - self.base, 0, self.spans - 1) for j in range(OMOST)
        ]
        return jnp.minimum(here, OMOST), found

    def find(self, g, steps, copy):
        at = self.starts(g, steps)
        for t in range(steps):
            def part(k, _, t=t):
                copy([self.span(t, g, k * PART + j) for j in range(PART)], at[t] + k * PART)
                return 0

            for k in range(2):
                part(k, 0)
            lax.fori_loop(2, (self.count(t, g) + PART - 1) // PART, part, 0)
        return at


def each_part(slots_ref, g, total, parts_all, spans, copy):
    def part(k, _):
        copy([jnp.clip(slots_ref[g, k * PART + j], 0, spans - 1) for j in range(PART)], k * PART)
        return 0

    straight = min(STRAIGHT, parts_all)
    for k in range(straight):
        part(k, 0)
    lax.fori_loop(straight, (total + PART - 1) // PART, part, 0)


def known_kernel(
    me_ref, outl_ref, q_ref, fk_ref, ca_ref, sa_ref, cb_ref, sb_ref, cq_ref, sq_ref, keys_hbm, after_ref,
    kx_ref, w_ref, tie_ref,
    okeys_ref, xtmp_ref, qtmp_ref, osem, *, per_device, rp, spans
):
    steps = q_ref.shape[0]
    tie_ref[...] = jnp.zeros_like(tie_ref)
    _, o_span = Lists(me_ref, None, None, None, outl_ref, spans).outliers()
    o_copies = [
        pltpu.make_async_copy(
            keys_hbm.at[pl.ds(pl.multiple_of(o_span[j] // 2 * 16, 16), 16)], okeys_ref.at[j], osem.at[j]
        )
        for j in range(OMOST)
    ]
    for c in o_copies:
        c.start()

    lane = lax.broadcasted_iota(jnp.int32, (8, LANES), 1)
    sign = jnp.where(lane < HD // 2, -1.0, 1.0)

    qtmp_ref[...] = jnp.zeros_like(qtmp_ref)
    for t in range(steps):
        x = q_ref[t:t + 1, :].astype(F32)
        for h in range(QH):
            r = h // per_device * rp + t * per_device + h % per_device
            qtmp_ref[r:r + 1, :] = x[:, h * HD:(h + 1) * HD]
    scale = 1.0 / (HD ** 0.5)
    row = lax.broadcasted_iota(jnp.int32, (LANES, LANES), 0) % rp
    lane_r = lax.broadcasted_iota(jnp.int32, (LANES, LANES), 1)
    cq = jnp.zeros((LANES, LANES), F32)
    sq = jnp.zeros((LANES, LANES), F32)
    for t in range(steps):
        here = (row >= t * per_device) & (row < (t + 1) * per_device)
        cq = jnp.where(here, cq_ref[t:t + 1, :] * scale, cq)
        sq = jnp.where(here, sq_ref[t:t + 1, :] * scale, sq)
    sq = jnp.where(lane_r < HD // 2, -sq, sq)
    for pk in range(w_ref.shape[0]):
        x = qtmp_ref[pk * LANES:(pk + 1) * LANES, :]
        x = x * cq + pltpu.roll(x, HD // 2, 1) * sq
        z = jnp.where(lane_r < HD // 2, 1.0, -1.0) * pltpu.roll(x, HD // 2, 1)
        hi, lo = split2(jnp.concatenate([x.T, z.T], 0))
        w_ref[pk] = jnp.concatenate([hi, lo], 0)

    blk = cb_ref.shape[0] // SPAN
    turns = []
    for j in range(OMOST):
        a = o_span[j] // blk
        b = pl.ds(pl.multiple_of(o_span[j] % blk * SPAN, SPAN), SPAN)
        ca, sa = ca_ref[pl.ds(a, 1), :], sa_ref[pl.ds(a, 1), :]
        cb, sb = cb_ref[b, :], sb_ref[b, :]
        turns.append((ca * cb - sa * sb, (sa * cb + ca * sb) * sign))
    for c in o_copies:
        c.wait()
    x_rows = kx_ref.shape[1]
    xtmp_ref[...] = jnp.zeros_like(xtmp_ref)
    fs = sq_ref[:steps, :] * sign[:1]
    for g in range(KVH):
        sl = slice(g * HD, (g + 1) * HD)
        for j in range(OMOST):
            wide = okeys_ref[j, :, sl].astype(F32)
            x = jnp.where(o_span[j] % 2 == 0, wide[:8], wide[8:])
            xtmp_ref[j * SPAN:(j + 1) * SPAN, :] = x * turns[j][0] + pltpu.roll(x, HD // 2, 1) * turns[j][1]
        x = fk_ref[:, sl].astype(F32)
        o = OMOST * SPAN
        xtmp_ref[o:o + steps, :] = x * cq_ref[:steps, :] + pltpu.roll(x, HD // 2, 1) * fs
        kx_ref[g, :, :HD] = xtmp_ref[...].astype(BF)
        kx_ref[g, :, HD:] = jnp.zeros((x_rows, HD), BF)


def values_kernel(
    me_ref, chosen_ref, begin_ref, count_ref, outl_ref, fv_ref, values_hbm, after_ref, slots_ref, vg_ref, tie_ref,
    values_ref, vtmp_ref, sem, *, main, g0, most
):
    steps = fv_ref.shape[0]
    rows_all = vtmp_ref.shape[0]
    n = vg_ref.shape[0]
    copies = [
        pltpu.make_async_copy(values_hbm.at[:, pl.ds((g0 + i) * HD, HD)], values_ref.at[i], sem.at[i]) for i in range(n)
    ]
    for c in copies[:AHEAD + 1]:
        c.start()
    tie_ref[...] = jnp.zeros_like(tie_ref)
    vtmp_ref[...] = jnp.zeros_like(vtmp_ref)
    spans = values_ref.shape[1] // SPAN
    lists = Lists(me_ref, chosen_ref, begin_ref, count_ref, outl_ref, spans, most)
    _, o_span = lists.outliers()

    for i in range(n):
        def rows_of(span, i=i):
            wide = values_ref[i, pl.ds(pl.multiple_of(span // 2 * 16, 16), 16), :].astype(F32)
            return jnp.where(span % 2 == 0, wide[:8], wide[8:])

        def put(spans, slot, i=i, rows_of=rows_of):
            for j, span in enumerate(spans):
                slots_ref[i, slot + j] = span
            dst = pl.ds(pl.multiple_of(LANES + slot * SPAN, SPAN), PART * SPAN)
            vtmp_ref[dst, :] = jnp.concatenate([rows_of(span) for span in spans], 0)

        copies[i].wait()
        if i + AHEAD + 1 < n:
            copies[i + AHEAD + 1].start()
        for j in range(OMOST):
            vtmp_ref[j * SPAN:(j + 1) * SPAN, :] = rows_of(o_span[j])
        vtmp_ref[OMOST * SPAN:OMOST * SPAN + steps, :] = fv_ref[:, (g0 + i) * HD:(g0 + i + 1) * HD].astype(F32)
        total = lists.find(g0 + i, steps, put)[steps]
        vg_ref[i, :LANES + main, :] = vtmp_ref[:LANES + main, :].astype(BF)
        if LANES + main < rows_all:
            def more(k, _, i=i):
                at = pl.ds(pl.multiple_of(LANES + main + k * LANES, LANES), LANES)
                vg_ref[i, at, :] = vtmp_ref[at, :].astype(BF)
                return 0

            lax.fori_loop(0, (jnp.maximum(total * SPAN - main, 0) + LANES - 1) // LANES, more, 0)


def attend_kernel(
    me_ref, count_ref, outl_ref, slotsa_ref, slotsb_ref, zmine_ref, zother_ref, kx_ref, w_ref, vga_ref, vgb_ref,
    ca_ref, sa_ref, cb_ref, sb_ref, keys_hbm,
    kft_hbm, out_ref,
    keys_ref, z_ref, a_ref, qt_ref, kf_ref, kft_ref, kg_ref, cg_ref, sg_ref, sc_ref, cc_ref, ss_ref, acc_ref,
    sem, out_sem, *, per_device, steps, main, most, stop=9
):
    rank, width = z_ref.shape
    half = rank // 2
    seq_len = keys_ref.shape[0]
    load = pltpu.make_async_copy(keys_hbm, keys_ref, sem)
    load.start()

    core = me_ref[0] % 2
    z_ref[pl.ds(pl.multiple_of(core * half, 16), half), :] = zmine_ref[...]
    z_ref[pl.ds(pl.multiple_of((1 - core) * half, 16), half), :] = zother_ref[...]
    turn_tables(ca_ref, sa_ref, cb_ref, sb_ref, cc_ref, ss_ref)
    basis(z_ref, a_ref, qt_ref)
    qt = qt_ref[...]

    load.wait()
    if stop == 1:
        return
    chunk = seq_len // KVH
    for i in range(KVH):
        rows = slice(i * chunk, (i + 1) * chunk)
        kf = lax.dot_general(keys_ref[rows, :], qt, NT, preferred_element_type=F32)
        kf_ref[rows, :] = kf
        kft_ref[:, rows] = kf.T
    store = pltpu.make_async_copy(kft_ref, kft_hbm, out_sem)
    store.start()
    if stop == 2:
        store.wait()
        return

    spans = seq_len // SPAN
    lists = Lists(me_ref, None, None, count_ref, outl_ref, spans, most)
    starts = []

    def values(g, rows):
        n = vga_ref.shape[0]
        return vga_ref[g, rows, :] if g < n else vgb_ref[g - n, rows, :]

    for g in range(KVH):
        def gather(spans, slot, g=g):
            got = []
            for span in spans:
                src = pl.ds(pl.multiple_of(span * SPAN, SPAN), SPAN)
                got.append((kf_ref[src, :], cc_ref[src, :], ss_ref[src, :]))
            dst = pl.ds(pl.multiple_of(slot * SPAN, SPAN), PART * SPAN)
            for ref, rows in zip((kg_ref, cg_ref, sg_ref), zip(*got)):
                ref[g, dst, :] = jnp.concatenate(rows, 0)

        starts.append(lists.starts(g, steps))
        early = slotsa_ref.shape[0]
        held, h = (slotsa_ref, g) if g < early else (slotsb_ref, g - early)
        each_part(held, h, starts[g][steps], kg_ref.shape[1] // (PART * SPAN), spans, gather)
    totals = [at[steps] for at in starts]

    if stop == 3:
        store.wait()
        return

    n_dest, rp, _ = out_ref.shape
    dests = n_dest // KVH
    qr = dests * rp
    heads = LANES // qr
    packs = w_ref.shape[0]
    o_live = lists.outliers()[0] * SPAN
    first_shard = me_ref[0] == 0
    column = lax.broadcasted_iota(jnp.int32, (8, LANES), 1)[:1]
    col_head = column // qr
    col_row = column % rp
    col_step = col_row // per_device

    def bounds(pk, h):
        first = jnp.full((1, LANES), 1 << 30, jnp.int32)
        last = jnp.zeros((1, LANES), jnp.int32)
        for t in range(steps):
            at = starts[pk * heads + h]
            here = (col_head == h) & (col_step == t)
            first = jnp.where(here, at[t] * SPAN, first)
            last = jnp.where(here, at[t + 1] * SPAN, last)
        return first, last

    def product(pk, y):
        r = jnp.dot(y, w_ref[pk, :2 * HD, :], preferred_element_type=F32)
        return r + jnp.dot(y, w_ref[pk, 2 * HD:, :], preferred_element_type=F32)

    token = lax.broadcasted_iota(jnp.int32, (LANES, LANES), 0)

    def slot_scores(pk, at, n, limits):
        rows = pl.ds(at, n)
        ys = []
        for h in range(heads):
            g = pk * heads + h
            x = jnp.dot(kg_ref[g, rows, :].astype(BF), qt_ref[:, g * HD:(g + 1) * HD], preferred_element_type=F32)
            ys.append(jnp.concatenate([(x * cg_ref[g, rows, :]).astype(BF), (x * sg_ref[g, rows, :]).astype(BF)], 1))
        r = product(pk, jnp.concatenate(ys, 0))
        s = jnp.full((n, LANES), DEAD, F32)
        here = lax.broadcasted_iota(jnp.int32, (n, LANES), 0) + at
        for h in range(heads):
            first, last = limits[h]
            s = jnp.where((here >= first) & (here < last), r[h * n:(h + 1) * n], s)
        return s

    def known_scores(pk):
        s = jnp.full((LANES, LANES), DEAD, F32)
        new = token - OMOST * SPAN
        is_live = (token < o_live) | (first_shard & (new >= 0) & (new <= col_step))
        is_live = is_live & (new < steps) & (col_row < steps * per_device)
        r = product(pk, kx_ref[pk * heads:(pk + 1) * heads].reshape(heads * LANES, 2 * HD))
        for h in range(heads):
            s = jnp.where(is_live & (col_head == h), r[h * LANES:(h + 1) * LANES], s)
        return s

    limits = [[bounds(pk, h) for h in range(heads)] for pk in range(packs)]
    extra = kg_ref.shape[1] - main
    blocks = []
    for pk in range(packs):
        longest = functools.reduce(jnp.maximum, totals[pk * heads:(pk + 1) * heads])
        blocks.append((jnp.maximum(longest * SPAN - main, 0) + LANES - 1) // LANES)

    tops = []
    for pk in range(packs):
        s = known_scores(pk)
        sc_ref[pk, :LANES, :] = s
        top = jnp.max(s, axis=0, keepdims=True)
        for at in range(0, main, ROWS):
            n = min(ROWS, main - at)
            s = slot_scores(pk, at, n, limits[pk])
            sc_ref[pk, LANES + at:LANES + at + n, :] = s
            top = jnp.maximum(top, jnp.max(s, axis=0, keepdims=True))
        tops.append(top)
    if extra > 0:
        for pk in range(packs):
            def more(k, top, pk=pk):
                at = pl.multiple_of(main + k * LANES, LANES)
                s = slot_scores(pk, at, LANES, limits[pk])
                sc_ref[pk, pl.ds(pl.multiple_of(LANES + at, LANES), LANES), :] = s
                return jnp.maximum(top, jnp.max(s, axis=0, keepdims=True))

            tops[pk] = lax.fori_loop(0, blocks[pk], more, tops[pk])
    if stop == 4:
        store.wait()
        return

    used = steps * per_device

    def weights(s, top):
        return jnp.where(s > 0.5 * DEAD, jnp.exp(s - top), 0.0)

    def weighted(pt, h, values):
        hi, lo = split2(pt[h * qr:(h + 1) * qr, :])
        r = jnp.dot(jnp.concatenate([hi, lo], 0), values, preferred_element_type=F32)
        return r[:qr] + r[qr:]

    sums = []
    for pk in range(packs):
        pts = []
        total = jnp.zeros((LANES, LANES), F32)
        for at in range(0, LANES + main, LANES):
            p = weights(sc_ref[pk, at:at + LANES, :], tops[pk])
            total = total + p
            pts.append(p.T)
        sums.append(jnp.sum(total, axis=0, keepdims=True))
        pt = jnp.concatenate(pts, 1)
        for h in range(heads):
            g = pk * heads + h
            acc = weighted(pt, h, values(g, slice(0, LANES + main)))
            for a in range(dests):
                acc_ref[g * dests + a] = acc[a * rp:(a + 1) * rp]
    if extra > 0:
        for pk in range(packs):
            def add(k, total, pk=pk):
                at = pl.multiple_of(LANES + main + k * LANES, LANES)
                p = weights(sc_ref[pk, pl.ds(at, LANES), :], tops[pk])
                pt = p.T
                for h in range(heads):
                    g = pk * heads + h

                    @pl.when(totals[g] * SPAN > main + k * LANES)
                    def _():
                        acc = weighted(pt, h, values(g, pl.ds(at, LANES)))
                        for a in range(dests):
                            acc_ref[g * dests + a] += acc[a * rp:(a + 1) * rp]

                return total + jnp.sum(p, axis=0, keepdims=True)

            sums[pk] = lax.fori_loop(0, blocks[pk], add, sums[pk])
    for d in range(n_dest):
        pk = d // (heads * dests)
        row = lax.broadcasted_iota(jnp.int32, (rp, LANES), 0)
        r = acc_ref[d]
        for k, extra_row in enumerate((*split3(tops[pk]), sums[pk])):
            r = jnp.where(row == used + k, extra_row, r)
        out_ref[d] = r.astype(BF)
    store.wait()


def turn_tables(ca_ref, sa_ref, cb_ref, sb_ref, cc_ref, ss_ref):
    blk = cb_ref.shape[0]
    cb = cb_ref[...]
    sb = sb_ref[...]
    for a in range(cc_ref.shape[0] // blk):
        ca = ca_ref[a:a + 1, :]
        sa = sa_ref[a:a + 1, :]
        cc_ref[a * blk:(a + 1) * blk, :] = ca * cb - sa * sb
        ss_ref[a * blk:(a + 1) * blk, :] = sa * cb + ca * sb


def basis(z_ref, a_ref, qt_ref):
    rank = z_ref.shape[0]
    wide = round_up(rank, LANES)
    z = z_ref[...]
    c = lax.dot_general(z, z, NT, preferred_element_type=F32)
    rows = lax.broadcasted_iota(jnp.int32, (rank, wide), 0)
    cols = lax.broadcasted_iota(jnp.int32, (rank, wide), 1)
    a_ref[:, :wide] = jnp.where(rows == cols, 1.0, 0.0)
    a_ref[:, wide:wide + rank] = c
    a_ref[:, wide + rank:] = jnp.zeros((rank, wide - rank), F32)
    nb = 32
    half_tiles = wide // LANES
    for j0 in range(0, rank, nb):
        tiles = [t for t in range(half_tiles) if t * LANES < j0 + nb]
        tiles += [half_tiles + t for t in range(half_tiles) if (t + 1) * LANES > j0]
        part = {t: a_ref[j0:j0 + nb, t * LANES:(t + 1) * LANES] for t in tiles}
        row = lax.broadcasted_iota(jnp.int32, (nb, LANES), 0)
        column = []
        for j in range(nb):
            t, o = divmod(j0 + j, LANES)
            column.append(jnp.broadcast_to(part[half_tiles + t][:, o:o + 1], (nb, LANES)))
        for j in range(nb):
            inverse = lax.rsqrt(jnp.broadcast_to(column[j][j:j + 1, :], (nb, LANES)))
            low = jnp.where(row > j, column[j] * inverse, 0.0)
            for k in range(j + 1, nb):
                column[k] = column[k] - low * jnp.broadcast_to(low[k:k + 1, :], (nb, LANES))
            for t in tiles:
                upper = jnp.broadcast_to(part[t][j:j + 1, :], (nb, LANES)) * inverse
                part[t] = jnp.where(row == j, upper, part[t] - low * upper)
        for t in tiles:
            a_ref[j0:j0 + nb, t * LANES:(t + 1) * LANES] = part[t]
        if j0 + nb < rank:
            upper = jnp.concatenate(
                [part[t] if t in part else jnp.zeros((nb, LANES), F32) for t in range(2 * half_tiles)], 1
            )
            h, m, l = split3(upper)
            left = jnp.concatenate([h, h, m, m, h, l], 0)[:, wide:].astype(BF)
            right = jnp.concatenate([h, m, h, m, l, h], 0).astype(BF)
            for s in range(2):
                d = lax.dot_general(left, right[:, s * wide:(s + 1) * wide], TN, preferred_element_type=F32)
                a_ref[j0 + nb:, s * wide:(s + 1) * wide] -= d[j0 + nb:rank]
    h, m, _ = split3(a_ref[:, :rank])
    q = jnp.dot(jnp.concatenate([h, m], 0).astype(BF), z, preferred_element_type=F32)
    qt_ref[...] = (q[:rank] + q[rank:]).astype(BF)


def attend_call(
    me, lists, z, z_other, kx, w, vga, vgb, ca, sa, cb, sb, cache_keys,
    *, steps, per_device, main, most, rp, n_dest, stop=9
):
    seq_len, width = cache_keys.shape
    rank = 2 * z.shape[0]
    tok_all = vga.shape[1] - LANES
    return pl.pallas_call(
        functools.partial(attend_kernel, per_device=per_device, steps=steps, main=main, most=most, stop=stop),
        in_specs=[smem()] * 5 + [vmem()] * 10 + [hbm()],
        out_specs=[hbm(), vmem()],
        out_shape=[
            jax.ShapeDtypeStruct((rank, seq_len), F32),
            jax.ShapeDtypeStruct((n_dest, rp, HD), BF),
        ],
        scratch_shapes=[
            pltpu.VMEM((seq_len, width), BF),
            pltpu.VMEM((rank, width), BF),
            pltpu.VMEM((rank, 2 * round_up(rank, LANES)), F32),
            pltpu.VMEM((rank, width), BF),
            pltpu.VMEM((seq_len, rank), F32),
            pltpu.VMEM((rank, seq_len), F32),
            pltpu.VMEM((KVH, tok_all, rank), F32),
            pltpu.VMEM((KVH, tok_all, HD), F32),
            pltpu.VMEM((KVH, tok_all, HD), F32),
            pltpu.VMEM((w.shape[0], LANES + tok_all, LANES), F32),
            pltpu.VMEM((seq_len, HD), F32),
            pltpu.VMEM((seq_len, HD), F32),
            pltpu.VMEM((n_dest, rp, HD), F32),
            pltpu.SemaphoreType.DMA,
            pltpu.SemaphoreType.DMA,
        ],
        compiler_params=pltpu.CompilerParams(vmem_limit_bytes=46 << 20),
        name="attend",
    )(me, *lists, z, z_other, kx, w, vga, vgb, ca, sa, cb, sb, in_hbm(cache_keys))


def merge_kernel(me_ref, parts_ref, out_ref, top_ref, sum_ref, *, steps, per_device):
    n, rp, _ = parts_ref.shape
    used = steps * per_device
    parts = parts_ref[...].astype(F32)
    rows = pl.ds(pl.multiple_of(me_ref[0] % (LANES // rp) * rp, 8), rp)
    top_ref[...] = (parts[:, used, :] + parts[:, used + 1, :] + parts[:, used + 2, :]).T
    sum_ref[...] = parts[:, used + 3, :].T
    tops = top_ref[rows, :]
    w = jnp.exp(tops - jnp.max(tops, axis=1, keepdims=True))
    w = w / jnp.sum(w * sum_ref[rows, :], axis=1, keepdims=True)
    o = jnp.zeros((rp, HD), F32)
    for s in range(n):
        o = o + w[:, s:s + 1] * parts[s]
    for t in range(steps):
        for i in range(per_device):
            r = t * per_device + i
            out_ref[t:t + 1, i * HD:(i + 1) * HD] = o[r:r + 1, :].astype(BF)


def swap(x, moves):
    return lax.ppermute(x, "seq", moves)


def on_device(
    cache_keys,
    cache_values,
    sketch_matrix,
    queries,
    fresh_keys,
    fresh_values,
    chosen,
    shard_counts,
    outliers,
):
    seq_len, width = cache_keys.shape
    devices = lax.axis_size("seq")
    myself = lax.axis_index("seq")
    length = seq_len * devices
    steps = queries.shape[0]
    rank = sketch_matrix.shape[1]
    per_device = QH // devices
    n_lists = steps * KVH
    most = 3 * chosen.shape[2] // devices
    slots_all = round_up(max(steps * most, steps * STRAIGHT * PART), LANES // SPAN)
    tok_all = slots_all * SPAN
    main = min(MAIN, tok_all)
    used = steps * per_device
    rp = round_up(used + 4, 16)
    n_dest = devices
    me = jnp.full((1,), myself, jnp.int32)

    keep, send = sketch_share(me, sketch_matrix.T, cache_keys, length)

    half_width = HD // 2
    exponents = jnp.arange(half_width, dtype=F32) * (2.0 / HD)
    inverse_freq = jnp.exp(-jnp.log(F32(500000.0)) * exponents)
    inverse_freq = jnp.concatenate([inverse_freq, inverse_freq])
    blk = 64
    coarse = (myself * seq_len + blk * jnp.arange(seq_len // blk, dtype=jnp.int32)).astype(F32)[:, None] * inverse_freq
    fine = jnp.arange(blk, dtype=jnp.int32).astype(F32)[:, None] * inverse_freq
    late = (length + jnp.arange(steps, dtype=jnp.int32)).astype(F32)[:, None] * inverse_freq
    turns = (jnp.cos(coarse), jnp.sin(coarse), jnp.cos(fine), jnp.sin(fine))

    shard = jnp.arange(devices, dtype=jnp.int32)
    begin = jnp.sum(jnp.where(shard < myself, shard_counts, 0), axis=2)
    count = jnp.sum(jnp.where(shard == myself, shard_counts, 0), axis=2)
    lists = (chosen.reshape(n_lists, -1), begin, count)
    places = slots_all + 4 * PART
    tie_shape = jax.ShapeDtypeStruct((1, LANES), F32)

    def known(after):
        return pl.pallas_call(
            functools.partial(known_kernel, per_device=per_device, rp=rp, spans=seq_len // SPAN),
            in_specs=[smem()] * 2 + [vmem()] * 8 + [hbm(), anywhere()],
            out_specs=[vmem()] * 3,
            out_shape=[
                jax.ShapeDtypeStruct((KVH, LANES, 2 * HD), BF),
                jax.ShapeDtypeStruct((n_dest * rp // LANES, 4 * HD, LANES), BF),
                tie_shape,
            ],
            scratch_shapes=[
                pltpu.VMEM((OMOST, 16, width), BF),
                pltpu.VMEM((LANES, HD), F32),
                pltpu.VMEM((n_dest * rp, HD), F32),
                pltpu.SemaphoreType.DMA((OMOST,)),
            ],
            compiler_params=pltpu.CompilerParams(vmem_limit_bytes=8 << 20),
            name="known_keys",
        )(me, outliers, queries, fresh_keys, *turns, jnp.cos(late), jnp.sin(late), in_hbm(cache_keys), after)

    def slot_values(g0, n, after):
        return pl.pallas_call(
            functools.partial(values_kernel, main=main, g0=g0, most=most),
            in_specs=[smem()] * 5 + [vmem(), hbm(), anywhere()],
            out_specs=[smem(), vmem(), vmem()],
            out_shape=[
                jax.ShapeDtypeStruct((n, places), jnp.int32),
                jax.ShapeDtypeStruct((n, LANES + tok_all, HD), BF),
                tie_shape,
            ],
            scratch_shapes=[
                pltpu.VMEM((n, seq_len, HD), BF),
                pltpu.VMEM((LANES + tok_all, HD), F32),
                pltpu.SemaphoreType.DMA((n,)),
            ],
            compiler_params=pltpu.CompilerParams(vmem_limit_bytes=16 << 20),
            name="slot_values",
        )(me, *lists, outliers, fresh_values, in_hbm(cache_values), after)

    z = keep + swap(send, [(i, i ^ 1) for i in range(devices)])
    hops = [1 << k for k in range(1, devices.bit_length() - 1)]
    for k in range(len(hops)):
        other = k ^ 1 if k < 2 and len(hops) >= 2 else k
        moves = [(i, i ^ hops[k if i % 2 == 0 else other]) for i in range(devices)]
        going = z.astype(BF)
        came = swap(going, moves).astype(F32)
        if k == 0:
            kx, w, tie = known(going)
            came = came + tie[0, 0]
        if k == min(1, len(hops) - 1):
            slots_a, vga, tie = slot_values(0, EARLY, going)
            came = came + tie[0, 0]
        if k == len(hops) - 1:
            slots_b, vgb, tie = slot_values(EARLY, KVH - EARLY, going)
            came = came + tie[0, 0]
        z = z + came
    z = z.astype(BF)
    z_other = swap(z, [(i, i ^ 1) for i in range(devices)])

    kft, parts = attend_call(
        me, (count, outliers, slots_a, slots_b), z, z_other, kx, w, vga, vgb, *turns, cache_keys,
        steps=steps, per_device=per_device, main=main, most=most, rp=rp, n_dest=n_dest,
    )
    parts = lax.all_to_all(parts, "seq", 0, 0, tiled=True)
    attended = pl.pallas_call(
        functools.partial(merge_kernel, steps=steps, per_device=per_device),
        in_specs=[smem(), vmem()],
        out_specs=vmem(),
        out_shape=jax.ShapeDtypeStruct((steps, per_device * HD), BF),
        scratch_shapes=[pltpu.VMEM((LANES, devices), F32)] * 2,
        name="merge",
    )(me, parts)
    return (attended, kft.T)


def solution(mesh):
    in_specs = (
        P(("groups", "seq"), None),
        P(("groups", "seq"), None),
        P(),
        P("groups", None),
        P("groups", None),
        P("groups", None),
        P("groups", None, None),
        P("groups", None, None),
        P("groups"),
    )
    out_specs = (P("groups", "seq"), P(("groups", "seq"), None))
    return jax.shard_map(
        on_device, mesh=mesh, in_specs=in_specs, out_specs=out_specs, check_vma=False
    )
```
